128 devices in a mesh: gx: 8 (over z, core), gy: 4 (over y), gz: 4 (over x).
Axes of the slice: x: 4, y: 4, z: 4, core: 2. Of those that a mesh axis runs over, the one named last changes fastest.
Arguments:
- right_side: float32 [128, 128, 512], P('gx', 'gy', 'gz'), may hold values from -2.35 to 2.35
- initial: float32 [128, 128, 512], P('gx', 'gy', 'gz'), may hold values from -3 to 3
- alpha: float32 [128, 128, 512], P('gx', 'gy', 'gz'), may hold values from 0.0001 to 0.004
- beta_x: float32 [128, 128, 512], P('gx', 'gy', 'gz'), may hold values from 0.25 to 4
- beta_y: float32 [128, 128, 512], P('gx', 'gy', 'gz'), may hold values from 0.25 to 4
- beta_z: float32 [128, 128, 512], P('gx', 'gy', 'gz'), may hold values from 0.25 to 4
Outputs:
- solution_field: float32 [128, 128, 512], P('gx', 'gy', 'gz')
- residual: float32 [128, 128, 512], P('gx', 'gy', 'gz')
The draws below stay inside these ranges and needn't reach their ends.
All inputs are finite; a program needn't handle non-finite values.
Results may differ from the reference program's by a relative error of at most 0.0003.
Values sent between devices are 32-bit elements; how exact they have to be, the bound alone decides.
A program may use at most 192 MiB of HBM per device.

```python
import math
import jax
import jax.numpy as jnp
from jax import lax

LEVELS = 5
NU = 2
BOTTOM = 12
NX = 128
NY = 128
NZ = 512


def block_term(key):
    width = 2 ** (LEVELS - 1)
    values = jax.random.uniform(key, (NX // width, NY // width, NZ // width), jnp.float32, -0.05, 0.05)
    values = jnp.repeat(values, width, axis=0)
    values = jnp.repeat(values, width, axis=1)
    return jnp.repeat(values, width, axis=2)


def draw_right_side(key, part):
    key = jax.random.fold_in(key, 11)
    block_key = jax.random.fold_in(key, 5)
    blocks = block_term(block_key)
    values = jax.random.normal(key, (NX, NY, NZ), jnp.float32)
    return (jnp.clip(values, -2.3, 2.3) + blocks).astype(jnp.float32)


def level_of(key, dims, pieces, smallest, largest):
    loudness, own = 1.0, jax.random.fold_in(key, 6)
    for position, blocks in pieces:
        draws = jnp.exp(jax.random.uniform(jax.random.fold_in(own, position), (blocks,), jnp.float32, smallest / len(pieces), largest / len(pieces)))
        loudness = loudness * jnp.repeat(draws, dims[position] // blocks).reshape([-1 if axis == position else 1 for axis in range(len(dims))])
    return loudness


def gaussian(rng, shape, scale, bound, shards=(), kind=jnp.bfloat16):
    loudness = level_of(rng, shape, shards, -0.22, 0.18) if shards else 1.0
    entries = jax.random.normal(rng, shape, jnp.float32) * scale * loudness
    return jnp.minimum(jnp.maximum(entries, -bound), bound).astype(kind)


def setup_inputs(seed: int = 0) -> dict:
    splits = jax.random.split(jax.random.key(seed), 7)
    right_side = draw_right_side(jax.random.fold_in(splits[6], 71), 0)
    initial = gaussian(splits[1], (NX, NY, NZ), 0.5, 3.0, ((0, 8), (1, 4), (2, 4)), jnp.float32)
    alpha = jnp.clip(jnp.exp(math.log(0.004) - 3.6888795 * jax.random.uniform(splits[2], (NX, NY, NZ), jnp.float32) ** level_of(splits[2], (NX, NY, NZ), ((0, 8), (1, 4), (2, 4)), -0.2, 0.2)), 0.0001, 0.004)
    beta_x = jnp.clip(jnp.exp(math.log(4.0) - 2.7725887 * jax.random.uniform(splits[3], (NX, NY, NZ), jnp.float32) ** level_of(splits[3], (NX, NY, NZ), ((0, 8), (1, 4), (2, 4)), -0.2, 0.2)), 0.25, 4.0)
    beta_y = jnp.clip(jnp.exp(math.log(4.0) - 2.7725887 * jax.random.uniform(splits[4], (NX, NY, NZ), jnp.float32) ** level_of(splits[4], (NX, NY, NZ), ((0, 8), (1, 4), (2, 4)), -0.2, 0.2)), 0.25, 4.0)
    beta_z = jnp.clip(jnp.exp(math.log(4.0) - 2.7725887 * jax.random.uniform(splits[5], (NX, NY, NZ), jnp.float32) ** level_of(splits[5], (NX, NY, NZ), ((0, 8), (1, 4), (2, 4)), -0.2, 0.2)), 0.25, 4.0)
    return {"right_side": right_side, "initial": initial, "alpha": alpha, "beta_x": beta_x, "beta_y": beta_y, "beta_z": beta_z}


def apply_op(field, coefs, scale):
    alpha, low_x, low_y, low_z, high_x, high_y, high_z = coefs
    padded = jnp.pad(field, 1)
    flux = low_x * (field - padded[:-2, 1:-1, 1:-1]) + high_x * (field - padded[2:, 1:-1, 1:-1])
    flux = flux + low_y * (field - padded[1:-1, :-2, 1:-1]) + high_y * (field - padded[1:-1, 2:, 1:-1])
    flux = flux + low_z * (field - padded[1:-1, 1:-1, :-2]) + high_z * (field - padded[1:-1, 1:-1, 2:])
    return alpha * field + scale * flux


def parity_of(shape):
    first = lax.broadcasted_iota(jnp.int32, shape, 0)
    second = lax.broadcasted_iota(jnp.int32, shape, 1)
    third = lax.broadcasted_iota(jnp.int32, shape, 2)
    return (first + second + third) % 2


def smooth(field, source, coefs, scale, sweeps):
    alpha, low_x, low_y, low_z, high_x, high_y, high_z = coefs
    diag = alpha + scale * (low_x + high_x + low_y + high_y + low_z + high_z)
    parity = parity_of(field.shape)
    for sweep in range(sweeps):
        for colour in (0, 1):
            update = field + (source - apply_op(field, coefs, scale)) / diag
            field = jnp.where(parity == colour, update, field)
    return field


def mean_eight(arr):
    a, b, c = arr.shape
    return 0.125 * arr.reshape(a // 2, 2, b // 2, 2, c // 2, 2).sum(axis=(1, 3, 5))


def face_mean(arr, dim, side):
    a, b, c = arr.shape
    blocks = arr.reshape(a // 2, 2, b // 2, 2, c // 2, 2)
    if dim == 0:
        return 0.25 * blocks[:, side].sum(axis=(2, 4))
    if dim == 1:
        return 0.25 * blocks[:, :, :, side].sum(axis=(1, 4))
    return 0.25 * blocks[:, :, :, :, :, side].sum(axis=(1, 3))


def coarsen(coefs):
    alpha, low_x, low_y, low_z, high_x, high_y, high_z = coefs
    return (mean_eight(alpha), face_mean(low_x, 0, 0), face_mean(low_y, 1, 0), face_mean(low_z, 2, 0),
            face_mean(high_x, 0, 1), face_mean(high_y, 1, 1), face_mean(high_z, 2, 1))


def prolong(arr):
    a, b, c = arr.shape
    return jnp.broadcast_to(arr[:, None, :, None, :, None], (a, 2, b, 2, c, 2)).reshape(2 * a, 2 * b, 2 * c)


def cycle(level, source, field, levels_coefs):
    scale = 0.25 ** level
    coefs = levels_coefs[level]
    if level == LEVELS - 1:
        return smooth(field, source, coefs, scale, BOTTOM)
    field = smooth(field, source, coefs, scale, NU)
    remainder = source - apply_op(field, coefs, scale)
    coarse_source = mean_eight(remainder)
    correction = cycle(level + 1, coarse_source, jnp.zeros_like(coarse_source), levels_coefs)
    field = field + prolong(correction)
    return smooth(field, source, coefs, scale, NU)


def reference(right_side, initial, alpha, beta_x, beta_y, beta_z):
    high_x = jnp.concatenate([beta_x[1:], jnp.zeros_like(beta_x[:1])], axis=0)
    high_y = jnp.concatenate([beta_y[:, 1:], jnp.zeros_like(beta_y[:, :1])], axis=1)
    high_z = jnp.concatenate([beta_z[:, :, 1:], jnp.zeros_like(beta_z[:, :, :1])], axis=2)
    levels_coefs = [(alpha, beta_x, beta_y, beta_z, high_x, high_y, high_z)]
    for level in range(1, LEVELS):
        levels_coefs.append(coarsen(levels_coefs[-1]))
    solution_field = cycle(0, right_side, initial, levels_coefs)
    residual = right_side - apply_op(solution_field, levels_coefs[0], 1.0)
    return solution_field, residual
```

```python
import itertools

import jax
import jax.numpy as jnp
from jax import lax
from jax.experimental import pallas as pl
from jax.experimental.pallas import tpu as pltpu
from jax.sharding import PartitionSpec as P

MESH = pl.DeviceIdType.MESH
F32 = jnp.float32
GRID = (8, 4, 4)
OFFS = [o for o in itertools.product((-1, 0, 1), repeat=3) if o != (0, 0, 0)]
FLAT = [o for o in OFFS if o[2] == 0]
TALL = [o for o in OFFS if o[2] != 0]
RED, BLACK = 0, 1
SAME, OTHER_R, YL_R, YH_R, ZL_R, ZH_R, ID_R, D_R, OTHER_B, YL_B, YH_B, ZL_B, ZH_B, ID_B, D_B = range(15)


def dot(a, b):
    return jnp.dot(a, b, precision=lax.Precision.HIGHEST, preferred_element_type=F32)


def iota(shape, dim):
    return lax.broadcasted_iota(jnp.int32, shape, dim)


def checker(shape):
    return ((iota(shape, 0) + iota(shape, 1)) & 1) == 0


def roll(x, shift, axis):
    size = x.shape[axis]
    shift = shift % size
    return pltpu.roll(x, shift, axis) if shift else x


def couplings(even, odd, next_x, keep_x, keep_next, keep_y, keep_z, scale, q0):
    parts = []
    for alpha, low_x, low_y, low_z in (even, odd):
        low_y, low_z = scale * low_y, scale * low_z
        own_y, own_z = low_y * keep_y, low_z * keep_z
        high_y, high_z = roll(own_y, -1, 0), roll(own_z, -1, 1)
        parts.append((own_y, high_y, own_z, high_z, alpha + (low_y + high_y) + (low_z + high_z)))
    x_e, x_o = scale * even[1], scale * odd[1]
    x_n = scale * next_x * keep_next
    d_e = parts[0][4] + (x_e + x_o)
    d_o = parts[1][4] + (x_o + x_n)
    x_e = x_e * keep_x
    i_e, i_o = 1.0 / d_e, 1.0 / d_o
    red = [jnp.where(q0, x_e, x_n)] + [jnp.where(q0, parts[0][n], parts[1][n]) for n in range(4)]
    red += [jnp.where(q0, i_e, i_o), jnp.where(q0, d_e, d_o)]
    black = [jnp.where(q0, x_n, x_e)] + [jnp.where(q0, parts[1][n], parts[0][n]) for n in range(4)]
    black += [jnp.where(q0, i_o, i_e), jnp.where(q0, d_o, d_e)]
    return [x_o] + red + black


def gathered_sum(colour, here, below, above, source, coef, q0):
    if colour == RED:
        other, base = jnp.where(q0, below, above), OTHER_R
    else:
        other, base = jnp.where(q0, above, below), OTHER_B
    total = source + coef(SAME) * here + coef(base) * other
    total = total + (coef(base + 1) * roll(here, 1, 0) + coef(base + 2) * roll(here, -1, 0))
    return total + (coef(base + 3) * roll(here, 1, 1) + coef(base + 4) * roll(here, -1, 1))


def kernel(
    f_hbm, u_hbm, a_hbm, bx_hbm, by_hbm, bz_hbm, sol, res,
    e5, u_in, u0, s_hi, s_lo, l_lo, l_hi, k0, g0, r0, b0, u1, us, us_lo, us_hi,
    e1, e1s, e1s_lo, e1s_hi, k1, f1, f1s, f1s_lo, f1s_hi, g1, r1, b1, v1, v1s, v1s_lo, v1s_hi,
    ga, gb, w2, k2, g2, r2, b2, k3, k4, work, work2, mats, qz0,
    in_sem, a_send, a_recv, b_send, b_recv, c_send, c_recv, d_send, d_recv, e_send, e_recv,
    h_send, h_recv, p_send, p_recv, i_send, i_recv, j_send, j_recv,
):
    gx, gy, gz = lax.axis_index("gx"), lax.axis_index("gy"), lax.axis_index("gz")
    me = (gx, gy, gz)
    core = lax.rem(gx, 2)
    chip = ((gx // 2) * 4 + gy) * 4 + gz

    def nb(o):
        return tuple(lax.rem(me[d] + (o[d] + GRID[d]), GRID[d]) if o[d] else me[d] for d in range(3))

    def peer(step):
        other = lax.rem(chip + step, 64)
        return (other // 16) * 2 + core, lax.rem(other // 4, 4), lax.rem(other, 4)

    partner = (gx + 1 - 2 * core, gy, gz)

    loads = [pltpu.make_async_copy(u_hbm, u_in, in_sem.at[5])]
    for n, ref in enumerate((f_hbm, a_hbm, bx_hbm, by_hbm, bz_hbm)):
        loads.append(pltpu.make_async_copy(ref, e5.at[n, pl.ds(4, 16), pl.ds(8, 32)], in_sem.at[n]))
    for c in loads:
        c.start()
    barrier = pltpu.get_barrier_semaphore()

    def greet(step, carry):
        pl.semaphore_signal(barrier, inc=1, device_id=peer(step), device_id_type=MESH)
        return carry

    lax.fori_loop(1, 64, greet, 0)
    for o in OFFS:
        if o[0]:
            pl.semaphore_signal(barrier, inc=1, device_id=nb(o), device_id_type=MESH)

    row, col = iota((128, 128), 0), iota((128, 128), 1)
    one = lambda cond: jnp.where(cond, 1.0, 0.0).astype(F32)
    SUM, EVEN, SUM32, DOUBLE, TO1 = range(5)
    mats[SUM] = one((row >> 1) == (col & 63))
    mats[EVEN] = one(row == 2 * (col & 63))
    mats[SUM32] = one((row >> 1) == (col & 31))
    mats[DOUBLE] = one(row == (col >> 1))
    z1 = jnp.where(col < 96, col, col - 128)
    mats[TO1] = one(row == (((z1 + 64 * gz) >> 1) & 127))
    wide_col, wide_row = iota((128, 256), 1), iota((128, 256), 0)
    z0 = jnp.where(wide_col < 192, wide_col, wide_col - 256)
    qz0[...] = one(wide_row == ((z0 >> 1) & 127))
    qy0 = one(iota((48, 32), 1) == (iota((48, 32), 0) >> 1) + 4)
    qy1 = one(iota((32, 32), 1) == (((iota((32, 32), 0) - 8 + 16 * gy) >> 1) & 31))
    qy2 = one(iota((32, 16), 1) == (iota((32, 16), 0) >> 1))
    qy3 = one(iota((16, 8), 1) == (iota((16, 8), 0) >> 1))

    q_l0 = checker((48, 256))
    q_in = checker((32, 128))
    q16 = checker((16, 128))
    q8 = checker((8, 128))
    lane8 = iota((8, 128), 1)
    lane16 = iota((16, 128), 1)
    lane32 = iota((32, 128), 1)
    lane48 = iota((48, 128), 1)
    first16 = (lane32 & 15) < 8
    first48 = (lane48 & 15) < 8

    def zero(ref, at):
        ref[at] = jnp.zeros(ref.shape[1:], F32)

    for ref, at in ((r0, 0), (r0, 13), (b0, 0), (b0, 13), (r1, 0), (r1, 13), (b1, 0), (b1, 13)):
        zero(ref, at)
    for ref in (r2, b2):
        zero(ref, 0)
        zero(ref, 17)

    for c in loads:
        c.wait()

    def take_black(p, carry):
        u0[4 + p - 1, pl.ds(8, 32), pl.ds(0, 128)] = jnp.where(q_in, u_in[2 * p + 1], u_in[2 * p])
        return carry

    lax.fori_loop(0, 8, take_black, 0, unroll=2)

    for half in range(2):
        for t, (first, second) in enumerate(((0, 1), (2, 3), (4, 5))):
            acc_a = jnp.zeros((32, 128), F32)
            acc_b = jnp.zeros((32, 128), F32)
            for m in range(8):
                at = 8 * half + m
                rolled = roll(e5[first, 4 + at, pl.ds(8, 32), :], 16 * m + 8, 1)
                acc_a = jnp.where((lane32 >> 4) == m, rolled, acc_a)
                if second < 5:
                    rolled = roll(e5[second, 4 + at, pl.ds(8, 32), :], 16 * m + 16, 1)
                elif m < 4:
                    rolled = roll(u0[3 + 4 * half + m, pl.ds(8, 32), pl.ds(0, 128)], 16 * m + 16, 1)
                else:
                    continue
                acc_b = jnp.where((((lane32 + 120) & 127) >> 4) == m, rolled, acc_b)
            s_hi[t, half] = jnp.where(first16, acc_a, acc_b)
            s_lo[t, half] = jnp.where(first16, acc_b, acc_a)

    pl.semaphore_wait(barrier, 81)

    def remote(src, dst, send, recv, to):
        return pltpu.make_async_remote_copy(
            src_ref=src, dst_ref=dst, send_sem=send, recv_sem=recv, device_id=to, device_id_type=MESH
        )

    Y0 = {-1: (8, 40, 8), 0: (8, 8, 32), 1: (32, 0, 8)}
    X5 = {-1: (4, 20, 5), 0: (4, 4, 16), 1: (16, 0, 4)}
    XU = {-1: (3, 11, 3), 0: (3, 3, 8), 1: (8, 0, 3)}
    XS = {-1: (0, 3, 1), 0: (0, 1, 2), 1: (1, 0, 1)}
    YS = {-1: (0, 40, 8), 0: (0, 8, 32), 1: (24, 0, 8)}
    first = []
    for n, o in enumerate(TALL):
        (xs, xd, xn), (ys, yd, yn) = XS[o[0]], YS[o[1]]
        src, dst = (s_hi, l_lo) if o[2] == 1 else (s_lo, l_hi)
        first.append(remote(
            src.at[:, pl.ds(xs, xn), pl.ds(ys, yn)], dst.at[:, pl.ds(xd, xn), pl.ds(yd, yn)],
            a_send.at[n], a_recv.at[n], nb(o),
        ))
    for n, o in enumerate(FLAT):
        (xs, xd, xn), (ys, yd, yn) = X5[o[0]], Y0[o[1]]
        first.append(remote(
            e5.at[:, pl.ds(xs, xn), pl.ds(ys, yn)], e5.at[:, pl.ds(xd, xn), pl.ds(yd, yn)],
            a_send.at[18 + n], a_recv.at[18 + n], nb(o),
        ))
        (xs, xd, xn) = XU[o[0]]
        first.append(remote(
            u0.at[pl.ds(xs, xn), pl.ds(ys, yn), pl.ds(0, 128)], u0.at[pl.ds(xd, xn), pl.ds(yd, yn), pl.ds(0, 128)],
            a_send.at[26 + n], a_recv.at[26 + n], nb(o),
        ))
    for c in first:
        c.start()

    def coarsen(count, rows, read):
        size = count * rows
        for p in range(count):
            for n in range(4):
                even = read(n, 2 * p)
                work[pl.ds(n * size + p * rows, rows), :] = even if n == 1 else even + read(n, 2 * p + 1)
        work2[pl.ds(0, 3 * size), :] = dot(work[pl.ds(0, 3 * size), :], mats[SUM])
        work2[pl.ds(3 * size, size), :] = dot(work[pl.ds(3 * size, size), :], mats[EVEN])

        def result(n, p):
            at = n * size + p * rows
            low = work2[pl.ds(at, rows // 2, stride=2), :]
            if n == 2:
                return 0.25 * low
            return (0.125 if n == 0 else 0.25) * (low + work2[pl.ds(at + 1, rows // 2, stride=2), :])

        return result

    got = coarsen(8, 32, lambda n, x: e5[n + 1, 4 + x, pl.ds(8, 32), :])
    for n in range(4):
        acc = jnp.zeros((16, 128), F32)
        for m in range(8):
            value = got(n, m)
            e1[n, 8 + m, pl.ds(8, 16), :] = value
            acc = jnp.where((lane16 >> 4) == m, roll(value, 16 * m + 8, 1), acc)
        e1s[n] = acc

    Y1 = {-1: (8, 24, 8), 0: (8, 8, 16), 1: (16, 0, 8)}
    YT = {-1: (0, 24, 8), 0: (0, 8, 16), 1: (8, 0, 8)}
    X1 = {-1: (8, 16, 8), 0: (8, 8, 8), 1: (8, 0, 8)}
    XT = {-1: 2, 0: 1, 1: 0}

    def spread1(main, strip, low, high, send, recv, lead):
        out = []
        for n, o in enumerate(TALL):
            ys, yd, yn = YT[o[1]]
            dst = low if o[2] == 1 else high
            src = strip.at[:, pl.ds(ys, yn)] if lead else strip.at[pl.ds(ys, yn)]
            dst = dst.at[:, XT[o[0]], pl.ds(yd, yn)] if lead else dst.at[XT[o[0]], pl.ds(yd, yn)]
            out.append(remote(src, dst, send.at[n], recv.at[n], nb(o)))
        for n, o in enumerate(FLAT):
            (xs, xd, xn), (ys, yd, yn) = X1[o[0]], Y1[o[1]]
            src = (pl.ds(xs, xn), pl.ds(ys, yn))
            dst = (pl.ds(xd, xn), pl.ds(yd, yn))
            if lead:
                src, dst = (slice(None),) + src, (slice(None),) + dst
            out.append(remote(main.at[src], main.at[dst], send.at[18 + n], recv.at[18 + n], nb(o)))
        return out

    coefs1 = spread1(e1, e1s, e1s_lo, e1s_hi, b_send, b_recv, True)
    for c in coefs1:
        c.start()

    got = coarsen(4, 16, lambda n, x: e1[n, 8 + x, pl.ds(8, 16), :])
    for n in range(4):
        acc = got(n, 0)
        for m in range(1, 4):
            acc = jnp.where((lane8 >> 5) == m, got(n, m), acc)
        ga[core, chip, n] = acc

    def scatter(buf, send, recv):
        def one_step(step, carry):
            remote(buf.at[core, chip], buf.at[core, chip], send.at[step], recv.at[chip], peer(step)).start()
            return carry

        lax.fori_loop(1, 64, one_step, 0)

    def collect(buf, send, recv):
        def one_step(step, carry):
            source = lax.rem(chip + step, 64)
            remote(buf.at[core, source], buf.at[core, source], send.at[step], recv.at[source], peer(step)).wait()
            return carry

        lax.fori_loop(1, 64, one_step, 0)

    scatter(ga, h_send, h_recv)

    for c in first:
        c.wait()
    keep_y0 = one(((iota((48, 256), 0) - 8 + 32 * gy) & 127) != 0)
    lane256 = iota((48, 256), 1)
    keep_z0 = one(((jnp.where(lane256 < 192, lane256, lane256 - 256) + 128 * gz) & 511) != 0)

    def side(n, group, m):
        t, low, high = n // 2, l_lo, l_hi
        if n % 2:
            return pltpu.roll(jnp.where(first48, high[t, group], low[t, group]), lax.rem(112 - 16 * m + 128, 128), 1)
        return pltpu.roll(jnp.where(first48, low[t, group], high[t, group]), lax.rem(120 - 16 * m + 128, 128), 1)

    def fine_row(n, x):
        at = x + 4
        return jnp.concatenate([e5[n, x], side(n, at // 8, lax.rem(at, 8))], axis=1)

    def build0(p, carry):
        e, o = 2 * p, 2 * p + 1
        even = tuple(fine_row(n, e) for n in range(1, 5))
        odd = tuple(fine_row(n, o) for n in range(1, 5))
        keep_e = jnp.where(((e - 4 + 16 * gx) & 127) == 0, 0.0, 1.0).astype(F32)
        keep_n = jnp.where(((e - 2 + 16 * gx) & 127) == 0, 0.0, 1.0).astype(F32)
        for n, value in enumerate(couplings(even, odd, fine_row(2, e + 2), keep_e, keep_n, keep_y0, keep_z0, 1.0, q_l0)):
            k0[n, p] = value
        f_e, f_o = fine_row(0, e), fine_row(0, o)
        g0[RED, p] = jnp.where(q_l0, f_e, f_o)
        g0[BLACK, p] = jnp.where(q_l0, f_o, f_e)
        return carry

    lax.fori_loop(0, 12, build0, 0)

    def side_u(p, carry):
        at = p + 1
        u0[p, :, pl.ds(128, 128)] = side(5, at // 4, lax.rem(at, 4))
        return carry

    lax.fori_loop(0, 14, side_u, 0)

    def half0(colour, src, dst, start, stop):
        def one_pair(p, carry):
            coef = lambda n: k0[n, p]
            total = gathered_sum(colour, src[p + 1], src[p], src[p + 2], g0[colour, p], coef, q_l0)
            dst[p + 1] = total * k0[ID_R if colour == RED else ID_B, p]
            return carry

        lax.fori_loop(start, stop, one_pair, 0)

    half0(RED, u0, r0, 0, 12)
    half0(BLACK, r0, b0, 0, 12)
    half0(RED, b0, r0, 1, 11)
    half0(BLACK, r0, b0, 1, 11)

    def resid0(p):
        coef = lambda n: k0[n, p]
        out = []
        for colour, own, far in ((RED, r0, b0), (BLACK, b0, r0)):
            total = gathered_sum(colour, far[p + 1], far[p], far[p + 2], g0[colour, p], coef, q_l0)
            out.append(total - k0[D_R if colour == RED else D_B, p] * own[p + 1])
        return out

    def restrict0(p, carry):
        red, black = resid0(p + 2)
        work[pl.ds(32 * p, 32), :] = (red + black)[8:40, :128]
        return carry

    lax.fori_loop(0, 8, restrict0, 0)
    work2[pl.ds(0, 256), :] = dot(work[pl.ds(0, 256), :], mats[SUM])
    acc = jnp.zeros((16, 128), F32)
    for m in range(8):
        value = 0.125 * (work2[pl.ds(32 * m, 16, stride=2), :] + work2[pl.ds(32 * m + 1, 16, stride=2), :])
        f1[8 + m, pl.ds(8, 16), :] = value
        acc = jnp.where((lane16 >> 4) == m, roll(value, 16 * m + 8, 1), acc)
    f1s[...] = acc

    right1 = spread1(f1, f1s, f1s_lo, f1s_hi, c_send, c_recv, False)
    for c in right1:
        c.start()

    acc = jnp.zeros((32, 128), F32)
    for m in range(8):
        acc = jnp.where((lane32 >> 4) == m, roll(b0[3 + m, pl.ds(8, 32), pl.ds(0, 128)], 16 * m + 8, 1), acc)
    us[...] = acc
    YU = {-1: (0, 40, 8), 0: (0, 8, 32), 1: (24, 0, 8)}
    fine = []
    for n, o in enumerate(TALL):
        ys, yd, yn = YU[o[1]]
        dst = us_lo if o[2] == 1 else us_hi
        fine.append(remote(us.at[pl.ds(ys, yn)], dst.at[XT[o[0]], pl.ds(yd, yn)], d_send.at[n], d_recv.at[n], nb(o)))
    for n, o in enumerate(FLAT):
        (xs, xd, xn), (ys, yd, yn) = XU[o[0]], Y0[o[1]]
        fine.append(remote(
            b0.at[pl.ds(xs, xn), pl.ds(ys, yn), pl.ds(0, 128)], u1.at[pl.ds(xd, xn), pl.ds(yd, yn), pl.ds(0, 128)],
            d_send.at[18 + n], d_recv.at[18 + n], nb(o),
        ))
    for c in fine:
        c.start()

    for c in coefs1:
        c.wait()
    keep_y1 = one(((iota((32, 128), 0) - 8 + 16 * gy) & 63) != 0)
    keep_z1 = one(((jnp.where(lane32 < 96, lane32, lane32 - 128) + 64 * gz) & 255) != 0)

    def joined(main, low, high, m):
        above = pltpu.roll(high, lax.rem(56 - 16 * m + 256, 128), 1)
        below = pltpu.roll(low, lax.rem(120 - 16 * m + 256, 128), 1)
        return jnp.where(lane32 < 64, main, jnp.where(lane32 < 96, above, below))

    def coarse_row(n, x):
        return joined(e1[n, x], e1s_lo[n, x // 8], e1s_hi[n, x // 8], lax.rem(x, 8))

    def build1(p, carry):
        e, o = 2 * p, 2 * p + 1
        even = tuple(coarse_row(n, e) for n in range(4))
        odd = tuple(coarse_row(n, o) for n in range(4))
        after = coarse_row(1, lax.rem(e + 2, 24))
        keep_e = jnp.where(((e - 8 + 8 * gx) & 63) == 0, 0.0, 1.0).astype(F32)
        keep_n = jnp.where(((e - 6 + 8 * gx) & 63) == 0, 0.0, 1.0).astype(F32)
        for n, value in enumerate(couplings(even, odd, after, keep_e, keep_n, keep_y1, keep_z1, 0.25, q_in)):
            k1[n, p] = value
        return carry

    lax.fori_loop(0, 12, build1, 0)

    collect(ga, h_send, h_recv)
    pair_a = remote(ga.at[core], ga.at[core], p_send.at[0], p_recv.at[0], partner)
    pair_a.start()

    for c in right1:
        c.wait()

    def source1(p, carry):
        e, o = 2 * p, 2 * p + 1
        f_e = joined(f1[e], f1s_lo[e // 8], f1s_hi[e // 8], lax.rem(e, 8))
        f_o = joined(f1[o], f1s_lo[o // 8], f1s_hi[o // 8], lax.rem(o, 8))
        red = jnp.where(q_in, f_e, f_o)
        g1[RED, p] = red
        g1[BLACK, p] = jnp.where(q_in, f_o, f_e)
        r1[p + 1] = red * k1[ID_R, p]
        return carry

    lax.fori_loop(0, 12, source1, 0)

    def half1(colour, src, dst):
        def one_pair(p, carry):
            coef = lambda n: k1[n, p]
            total = gathered_sum(colour, src[p + 1], src[p], src[p + 2], g1[colour, p], coef, q_in)
            dst[p + 1] = total * k1[ID_R if colour == RED else ID_B, p]
            return carry

        lax.fori_loop(0, 12, one_pair, 0, unroll=2)

    half1(BLACK, r1, b1)
    half1(RED, b1, r1)
    half1(BLACK, r1, b1)
    for p in range(4):
        coef = lambda n: k1[n, p + 4]
        total = gathered_sum(RED, b1[p + 5], b1[p + 4], b1[p + 6], g1[RED, p + 4], coef, q_in) - k1[D_R, p + 4] * r1[p + 5]
        other = gathered_sum(BLACK, r1[p + 5], r1[p + 4], r1[p + 6], g1[BLACK, p + 4], coef, q_in)
        total = total + (other - k1[D_B, p + 4] * b1[p + 5])
        work[pl.ds(16 * p, 16), :] = jnp.where(lane16 < 64, total[8:24], 0.0)
    work2[pl.ds(0, 64), :] = dot(work[pl.ds(0, 64), :], mats[SUM32])
    acc = jnp.zeros((8, 128), F32)
    for m in range(4):
        value = 0.125 * (work2[pl.ds(16 * m, 8, stride=2), :] + work2[pl.ds(16 * m + 1, 8, stride=2), :])
        acc = jnp.where((lane8 >> 5) == m, value, acc)
    gb[core, chip] = acc

    scatter(gb, i_send, i_recv)

    acc = jnp.zeros((16, 128), F32)
    for m in range(4):
        value = b1[5 + m, pl.ds(8, 16), :]
        value = jnp.where(lane16 < 64, value, roll(value, 64, 1))
        acc = jnp.where((lane16 >> 4) == m, roll(value, 16 * m + 8, 1), acc)
        v1[4 + m, pl.ds(8, 16), :] = value
    v1s[...] = acc
    black1 = []
    for n, o in enumerate(TALL):
        ys, yd, yn = YT[o[1]]
        dst = v1s_lo if o[2] == 1 else v1s_hi
        black1.append(remote(v1s.at[pl.ds(ys, yn)], dst.at[XT[o[0]], pl.ds(yd, yn)], e_send.at[n], e_recv.at[n], nb(o)))
    for n, o in enumerate(FLAT):
        (xs, xd, xn), (ys, yd, yn) = {-1: (4, 8, 4), 0: (4, 4, 4), 1: (4, 0, 4)}[o[0]], Y1[o[1]]
        black1.append(remote(
            v1.at[pl.ds(xs, xn), pl.ds(ys, yn)], v1.at[pl.ds(xd, xn), pl.ds(yd, yn)],
            e_send.at[18 + n], e_recv.at[18 + n], nb(o),
        ))
    for c in black1:
        c.start()

    pair_a.wait()

    def untile(tiles):
        out = []
        for m in range(4):
            total = tiles[0] if m == 0 else roll(tiles[0], -32 * m, 1)
            for k in range(1, 4):
                total = jnp.where((lane8 >> 5) == k, roll(tiles[k], 32 * (k - m), 1), total)
            out.append(total)
        return out

    def place(buf, lead, write):
        def one_block(t, carry):
            bx, by = t // 4, lax.rem(t, 4)
            at = (bx // 2) * 16 + by * 4
            tiles = [buf[(lax.rem(bx, 2), at + k) + lead] for k in range(4)]
            for m, value in enumerate(untile(tiles)):
                write(4 * bx + m, pl.ds(pl.multiple_of(8 * by, 8), 8), value)
            return carry

        lax.fori_loop(0, 32, one_block, 0)

    for n in range(4):
        def write(x, rows, value, n=n):
            w2[n, x, rows, :] = value

        place(ga, (n,), write)

    keep_y2 = one(iota((32, 128), 0) != 0)
    keep_z2 = one(lane32 != 0)

    def build2(p, carry):
        e, o = 2 * p, 2 * p + 1
        even = tuple(w2[n, e] for n in range(4))
        odd = tuple(w2[n, o] for n in range(4))
        keep_e = jnp.where(p == 0, 0.0, 1.0).astype(F32)
        keep_n = jnp.where(p == 15, 0.0, 1.0).astype(F32)
        after = w2[1, lax.rem(e + 2, 32)]
        for n, value in enumerate(couplings(even, odd, after, keep_e, keep_n, keep_y2, keep_z2, 0.25**2, q_in)):
            k2[n, p] = value
        return carry

    lax.fori_loop(0, 16, build2, 0)

    def small(level_coefs, count, rows, period, scale, q, dest):
        keep_y = one(iota((rows, 128), 0) != 0)
        keep_z = one((iota((rows, 128), 1) & (period - 1)) != 0)
        for p in range(count):
            even = tuple(level_coefs(n, 2 * p) for n in range(4))
            odd = tuple(level_coefs(n, 2 * p + 1) for n in range(4))
            after = level_coefs(1, (2 * p + 2) % (2 * count))
            for n, value in enumerate(couplings(
                even, odd, after, 0.0 if p == 0 else 1.0, 0.0 if p == count - 1 else 1.0, keep_y, keep_z, scale, q
            )):
                dest[n, p] = value

    got3 = coarsen(16, 32, lambda n, x: w2[n, x])
    rows3 = [[got3(n, x) for x in range(16)] for n in range(4)]
    for n in range(4):
        for x in range(16):
            w2[n, x, pl.ds(0, 16), :] = rows3[n][x]
    small(lambda n, x: w2[n, x, pl.ds(0, 16), :], 8, 16, 64, 0.25**3, q16, k3)
    got4 = coarsen(8, 16, lambda n, x: w2[n, x, pl.ds(0, 16), :])
    small(got4, 4, 8, 32, 0.25**4, q8, k4)

    collect(gb, i_send, i_recv)
    pair_b = remote(gb.at[core], gb.at[core], p_send.at[1], p_recv.at[1], partner)
    pair_b.start()
    pair_b.wait()

    def write_right(x, rows, value):
        w2[0, x, rows, :] = value

    place(gb, (), write_right)

    def source2(p, carry):
        f_e, f_o = w2[0, 2 * p], w2[0, 2 * p + 1]
        red = jnp.where(q_in, f_e, f_o)
        g2[RED, p] = red
        g2[BLACK, p] = jnp.where(q_in, f_o, f_e)
        r2[p + 1] = red * k2[ID_R, p]
        return carry

    lax.fori_loop(0, 16, source2, 0, unroll=2)

    def half2(colour, src, dst):
        def one_pair(p, carry):
            coef = lambda n: k2[n, p]
            total = gathered_sum(colour, src[p + 1], src[p], src[p + 2], g2[colour, p], coef, q_in)
            dst[p + 1] = total * k2[ID_R if colour == RED else ID_B, p]
            return carry

        lax.fori_loop(0, 16, one_pair, 0, unroll=2)

    half2(BLACK, r2, b2)
    half2(RED, b2, r2)
    half2(BLACK, r2, b2)

    def restrict2(p, carry):
        coef = lambda n: k2[n, p]
        total = gathered_sum(RED, b2[p + 1], b2[p], b2[p + 2], g2[RED, p], coef, q_in) - k2[D_R, p] * r2[p + 1]
        other = gathered_sum(BLACK, r2[p + 1], r2[p], r2[p + 2], g2[BLACK, p], coef, q_in)
        work[pl.ds(pl.multiple_of(32 * p, 32), 32), :] = total + (other - k2[D_B, p] * b2[p + 1])
        return carry

    lax.fori_loop(0, 16, restrict2, 0)
    work2[pl.ds(0, 512), :] = dot(work[pl.ds(0, 512), :], mats[SUM])

    def pack(rows, q):
        count = len(rows) // 2
        red = [jnp.where(q, rows[2 * p], rows[2 * p + 1]) for p in range(count)]
        black = [jnp.where(q, rows[2 * p + 1], rows[2 * p]) for p in range(count)]
        return red, black

    def half_small(colour, src, source, k, q, own=None):
        count = len(src)
        out = []
        for p in range(count):
            coef = lambda n: k[n, p]
            total = gathered_sum(colour, src[p], src[p - 1], src[(p + 1) % count], source[p], coef, q)
            if own is None:
                out.append(total * k[ID_R if colour == RED else ID_B, p])
            else:
                out.append(total - k[D_R if colour == RED else D_B, p] * own[p])
        return out

    def paired(count, rows):
        return [
            0.125 * (work2[pl.ds(2 * rows * m, rows, stride=2), :] + work2[pl.ds(2 * rows * m + 1, rows, stride=2), :])
            for m in range(count)
        ]

    def unpacked(red, black, q):
        out = []
        for r, b in zip(red, black):
            out += [jnp.where(q, r, b), jnp.where(q, b, r)]
        return out

    fr3, fb3 = pack(paired(16, 16), q16)
    r3 = [fr3[p] * k3[ID_R, p] for p in range(8)]
    b3 = half_small(BLACK, r3, fb3, k3, q16)
    r3 = half_small(RED, b3, fr3, k3, q16)
    b3 = half_small(BLACK, r3, fb3, k3, q16)
    left_r = half_small(RED, b3, fr3, k3, q16, r3)
    left_b = half_small(BLACK, r3, fb3, k3, q16, b3)
    for p in range(8):
        work[pl.ds(16 * p, 16), :] = left_r[p] + left_b[p]
    work2[pl.ds(0, 128), :] = dot(work[pl.ds(0, 128), :], mats[SUM])

    fr4, fb4 = pack(paired(8, 8), q8)
    r4 = [fr4[p] * k4[ID_R, p] for p in range(4)]
    b4 = half_small(BLACK, r4, fb4, k4, q8)

    def bottom(step, carry):
        black = list(carry[4:])
        red = half_small(RED, black, fr4, k4, q8)
        black = half_small(BLACK, red, fb4, k4, q8)
        return tuple(red + black)

    done = lax.fori_loop(0, 11, bottom, tuple(r4 + b4))
    e4 = unpacked(done[:4], done[4:], q8)

    def doubled(rows, qy, size):
        for m, value in enumerate(rows):
            work[pl.ds(size * m, size), :] = value
        work2[pl.ds(0, size * len(rows)), :] = dot(work[pl.ds(0, size * len(rows)), :], mats[DOUBLE])
        return [dot(qy, work2[pl.ds(size * m, size), :]) for m in range(len(rows))]

    up3 = doubled(e4, qy3, 8)
    b3 = [b3[p] + up3[p] for p in range(8)]
    r3 = half_small(RED, b3, fr3, k3, q16)
    b3 = half_small(BLACK, r3, fb3, k3, q16)
    r3 = half_small(RED, b3, fr3, k3, q16)
    b3 = half_small(BLACK, r3, fb3, k3, q16)
    up2 = doubled(unpacked(r3, b3, q16), qy2, 16)
    for p in range(16):
        b2[p + 1] = b2[p + 1] + up2[p]

    half2(RED, b2, r2)
    half2(BLACK, r2, b2)
    half2(RED, b2, r2)
    half2(BLACK, r2, b2)

    for c in black1:
        c.wait()

    def spread2(p, carry):
        x = (p - 4 + 4 * gx) & 31
        red, black = r2[x // 2 + 1], b2[x // 2 + 1]
        work[pl.ds(pl.multiple_of(32 * p, 32), 32), :] = jnp.where(
            q_in, jnp.where((x & 1) == 0, red, black), jnp.where((x & 1) == 0, black, red)
        )
        return carry

    lax.fori_loop(0, 12, spread2, 0)
    work2[pl.ds(0, 384), :] = dot(work[pl.ds(0, 384), :], mats[TO1])

    def lift1(p, carry):
        m = lax.rem(p, 4)
        value = joined(v1[p], v1s_lo[p // 4], v1s_hi[p // 4], m)
        b1[p + 1] = value + dot(qy1, work2[pl.ds(pl.multiple_of(32 * p, 32), 32), :])
        return carry

    lax.fori_loop(0, 12, lift1, 0)
    half1(RED, b1, r1)
    half1(BLACK, r1, b1)
    half1(RED, b1, r1)
    half1(BLACK, r1, b1)

    for c in fine:
        c.wait()
    used = (lane32 < 72) | (lane32 >= 120)

    def spread1_up(p, carry):
        x = p + 5
        red, black = r1[x // 2 + 1], b1[x // 2 + 1]
        value = jnp.where(q_in, jnp.where((x & 1) == 0, red, black), jnp.where((x & 1) == 0, black, red))
        work[pl.ds(pl.multiple_of(32 * p, 32), 32), :] = jnp.where(used, value, 0.0)
        return carry

    lax.fori_loop(0, 14, spread1_up, 0)

    def lift0(p, carry):
        wide = dot(work[pl.ds(pl.multiple_of(32 * p, 32), 32), :], qz0[...])
        at = p + 1
        strip = jnp.where(first48, us_lo[at // 4], us_hi[at // 4])
        return dot(qy0, wide), strip, at

    def lift_halo(p, carry):
        wide = dot(work[pl.ds(pl.multiple_of(32 * p, 32), 32), :], qz0[...])
        at = p + 5
        group, m = at // 8, lax.rem(at, 8)
        merged = jnp.where(first48, us_lo[group], us_hi[group])
        beyond = pltpu.roll(merged, lax.rem(120 - 16 * m + 128, 128), 1)
        u1[p] = jnp.concatenate([u1[p, :, pl.ds(0, 128)], beyond], axis=1) + dot(qy0, wide)
        return carry

    def own_black(p, carry):
        u1[p, pl.ds(8, 32), pl.ds(0, 128)] = b0[p, pl.ds(8, 32), pl.ds(0, 128)]
        return carry

    lax.fori_loop(3, 11, own_black, 0)
    lax.fori_loop(0, 14, lift_halo, 0)
    half0(RED, u1, r0, 0, 12)
    half0(BLACK, r0, b0, 0, 12)
    half0(RED, b0, r0, 1, 11)
    half0(BLACK, r0, b0, 1, 11)

    def finish(p, carry):
        red, black = resid0(p + 2)
        red, black = red[8:40, :128], black[8:40, :128]
        res[2 * p] = jnp.where(q_in, red, black)
        res[2 * p + 1] = jnp.where(q_in, black, red)
        red, black = r0[p + 3, pl.ds(8, 32), pl.ds(0, 128)], b0[p + 3, pl.ds(8, 32), pl.ds(0, 128)]
        sol[2 * p] = jnp.where(q_in, red, black)
        sol[2 * p + 1] = jnp.where(q_in, black, red)
        return carry

    lax.fori_loop(0, 8, finish, 0)


def on_device(right_side, initial, alpha, beta_x, beta_y, beta_z):
    block = jax.ShapeDtypeStruct(right_side.shape, F32)
    V = lambda *shape: pltpu.VMEM(shape, F32)
    D = lambda n: pltpu.SemaphoreType.DMA((n,))
    scratch = [
        V(5, 26, 48, 128), V(16, 32, 128), V(14, 48, 256),
        V(3, 2, 32, 128), V(3, 2, 32, 128), V(3, 4, 48, 128), V(3, 4, 48, 128),
        V(15, 12, 48, 256), V(2, 12, 48, 256), V(14, 48, 256), V(14, 48, 256), V(14, 48, 256),
        V(32, 128), V(3, 48, 128), V(3, 48, 128),
        V(4, 24, 32, 128), V(4, 16, 128), V(4, 3, 32, 128), V(4, 3, 32, 128), V(15, 12, 32, 128),
        V(24, 32, 128), V(16, 128), V(3, 32, 128), V(3, 32, 128),
        V(2, 12, 32, 128), V(14, 32, 128), V(14, 32, 128),
        V(12, 32, 128), V(16, 128), V(3, 32, 128), V(3, 32, 128),
        V(2, 64, 4, 8, 128), V(2, 64, 8, 128), V(4, 32, 32, 128), V(15, 16, 32, 128), V(2, 16, 32, 128),
        V(18, 32, 128), V(18, 32, 128), V(15, 8, 16, 128), V(15, 4, 8, 128),
        V(2048, 128), V(2048, 128), V(5, 128, 128), V(128, 256),
        D(6), D(34), D(34), D(26), D(26), D(26), D(26), D(26), D(26), D(26), D(26),
        D(64), D(64), D(2), D(2), D(64), D(64), D(1), D(1),
    ]
    return pl.pallas_call(
        kernel,
        out_shape=(block, block),
        in_specs=[pl.BlockSpec(memory_space=pl.ANY)] * 6,
        out_specs=[pl.BlockSpec(memory_space=pltpu.VMEM)] * 2,
        scratch_shapes=scratch,
        compiler_params=pltpu.CompilerParams(collective_id=0, has_side_effects=True, vmem_limit_bytes=60 << 20),
    )(right_side, initial, alpha, beta_x, beta_y, beta_z)


def solution(mesh):
    spec = P("gx", "gy", "gz")
    return jax.shard_map(on_device, mesh=mesh, in_specs=(spec,) * 6, out_specs=(spec, spec), check_vma=False)
```

```python
import itertools

import jax
import jax.numpy as jnp
from jax import lax
from jax.experimental import pallas as pl
from jax.experimental.pallas import tpu as pltpu
from jax.sharding import PartitionSpec as P

MESH = pl.DeviceIdType.MESH
F32 = jnp.float32
GRID = (8, 4, 4)
OFFS = [o for o in itertools.product((-1, 0, 1), repeat=3) if o != (0, 0, 0)]
FLAT = [o for o in OFFS if o[2] == 0]
TALL = [o for o in OFFS if o[2] != 0]
RED, BLACK = 0, 1
SAME, OTHER_R, YL_R, YH_R, ZL_R, ZH_R, ID_R, D_R, OTHER_B, YL_B, YH_B, ZL_B, ZH_B, ID_B, D_B = range(15)


def dot(a, pick):
    total = None
    for _ in range(3):
        term = a.astype(jnp.bfloat16)
        part = jnp.dot(term, pick, preferred_element_type=F32)
        total = part if total is None else total + part
        a = a - term.astype(F32)
    return total


def iota(shape, dim):
    return lax.broadcasted_iota(jnp.int32, shape, dim)


def checker(shape):
    return ((iota(shape, 0) + iota(shape, 1)) & 1) == 0


def roll(x, shift, axis):
    size = x.shape[axis]
    shift = shift % size
    return pltpu.roll(x, shift, axis) if shift else x


def couplings(even, odd, next_x, keep_x, keep_next, keep_y, keep_z, scale, q0):
    parts = []
    for alpha, low_x, low_y, low_z in (even, odd):
        low_y, low_z = scale * low_y, scale * low_z
        own_y, own_z = low_y * keep_y, low_z * keep_z
        high_y, high_z = roll(own_y, -1, 0), roll(own_z, -1, 1)
        parts.append((own_y, high_y, own_z, high_z, alpha + (low_y + high_y) + (low_z + high_z)))
    x_e, x_o = scale * even[1], scale * odd[1]
    x_n = scale * next_x * keep_next
    d_e = parts[0][4] + (x_e + x_o)
    d_o = parts[1][4] + (x_o + x_n)
    x_e = x_e * keep_x
    i_e, i_o = 1.0 / d_e, 1.0 / d_o
    red = [jnp.where(q0, x_e, x_n)] + [jnp.where(q0, parts[0][n], parts[1][n]) for n in range(4)]
    red += [jnp.where(q0, i_e, i_o), jnp.where(q0, d_e, d_o)]
    black = [jnp.where(q0, x_n, x_e)] + [jnp.where(q0, parts[1][n], parts[0][n]) for n in range(4)]
    black += [jnp.where(q0, i_o, i_e), jnp.where(q0, d_o, d_e)]
    return [x_o] + red + black


def gathered_sum(colour, here, below, above, source, coef, q0):
    if colour == RED:
        other, base = jnp.where(q0, below, above), OTHER_R
    else:
        other, base = jnp.where(q0, above, below), OTHER_B
    total = source + coef(SAME) * here + coef(base) * other
    total = total + (coef(base + 1) * roll(here, 1, 0) + coef(base + 2) * roll(here, -1, 0))
    return total + (coef(base + 3) * roll(here, 1, 1) + coef(base + 4) * roll(here, -1, 1))


def kernel(
    f_hbm, u_hbm, a_hbm, bx_hbm, by_hbm, bz_hbm, sol, res,
    e5, y_top, y_bot, y_lo, y_hi, u_in, u0, s_hi, s_lo, l_lo, l_hi, k0, g0, r0, b0, u1, us, us_lo, us_hi,
    e1, e1s, e1s_lo, e1s_hi, k1, f1, f1s, f1s_lo, f1s_hi, g1, r1, b1, v1, v1s, v1s_lo, v1s_hi,
    ga, gb, w2, k2, g2, r2, b2, k3, k4, work, work2, work3, mats, qz0,
    in_sem, a_send, a_recv, b_send, b_recv, c_send, c_recv, d_send, d_recv, e_send, e_recv,
    h_send, h_recv, p_send, p_recv, i_send, i_recv, j_send, j_recv,
):
    gx, gy, gz = lax.axis_index("gx"), lax.axis_index("gy"), lax.axis_index("gz")
    me = (gx, gy, gz)
    core = lax.rem(gx, 2)
    chip = ((gx // 2) * 4 + gy) * 4 + gz

    def nb(o):
        return tuple(lax.rem(me[d] + (o[d] + GRID[d]), GRID[d]) if o[d] else me[d] for d in range(3))

    def peer(step):
        other = lax.rem(chip + step, 64)
        return (other // 16) * 2 + core, lax.rem(other // 4, 4), lax.rem(other, 4)

    partner = (gx + 1 - 2 * core, gy, gz)

    loads = [pltpu.make_async_copy(u_hbm, u_in, in_sem.at[5])]
    for n, ref in enumerate((f_hbm, a_hbm, bx_hbm, by_hbm, bz_hbm)):
        loads.append(pltpu.make_async_copy(ref, e5.at[n, pl.ds(4, 16)], in_sem.at[n]))
    for c in loads:
        c.start()

    def zero(ref, at):
        ref[at] = jnp.zeros(ref.shape[1:], F32)

    for ref in (u0, u1):
        zero(ref, 0)
        zero(ref, 13)
    barrier = pltpu.get_barrier_semaphore()

    def greet(step, carry):
        pl.semaphore_signal(barrier, inc=1, device_id=peer(step), device_id_type=MESH)
        return carry

    lax.fori_loop(1, 64, greet, 0)
    for o in OFFS:
        if o[0]:
            pl.semaphore_signal(barrier, inc=1, device_id=nb(o), device_id_type=MESH)

    row, col = iota((128, 128), 0), iota((128, 128), 1)
    one = lambda cond: jnp.where(cond, 1.0, 0.0).astype(F32)
    SUM, EVEN, SUM32, DOUBLE, TO1 = range(5)
    mats[SUM] = one((row >> 1) == (col & 63)).astype(jnp.bfloat16)
    mats[EVEN] = one(row == 2 * (col & 63)).astype(jnp.bfloat16)
    mats[SUM32] = one((row >> 1) == (col & 31)).astype(jnp.bfloat16)
    mats[DOUBLE] = one(row == (col >> 1)).astype(jnp.bfloat16)
    z1 = jnp.where(col < 96, col, col - 128)
    mats[TO1] = one(row == (((z1 + 64 * gz) >> 1) & 127)).astype(jnp.bfloat16)
    wide_col, wide_row = iota((128, 256), 1), iota((128, 256), 0)
    z0 = jnp.where(wide_col < 192, wide_col, wide_col - 256)
    qz0[...] = one(wide_row == ((z0 >> 1) & 127)).astype(jnp.bfloat16)

    q_l0 = checker((48, 256))
    q_in = checker((32, 128))
    q16 = checker((16, 128))
    q8 = checker((8, 128))
    lane8 = iota((8, 128), 1)
    lane16 = iota((16, 128), 1)
    lane32 = iota((32, 128), 1)
    lane48 = iota((48, 128), 1)
    first16 = (lane32 & 15) < 8
    first48 = (lane48 & 15) < 8

    for ref, at in ((r0, 0), (r0, 13), (b0, 0), (b0, 13), (r1, 0), (r1, 13), (b1, 0), (b1, 13)):
        zero(ref, at)
    for ref in (r2, b2):
        zero(ref, 0)
        zero(ref, 17)

    for c in loads:
        c.wait()

    def take_black(p, carry):
        u0[4 + p - 1, pl.ds(8, 32), pl.ds(0, 128)] = jnp.where(q_in, u_in[2 * p + 1], u_in[2 * p])
        return carry

    lax.fori_loop(0, 8, take_black, 0, unroll=2)

    sub8 = iota((8, 128), 0) < 4
    y_lo[:, 24] = jnp.zeros((3, 8, 128), F32)
    y_hi[:, 24] = jnp.zeros((3, 8, 128), F32)

    def take_ends(x, carry):
        for t, (n, k) in enumerate(((0, 1), (2, 4))):
            y_top[t, x] = jnp.where(sub8, roll(e5[n, 4 + x, pl.ds(24, 8), :], 4, 0), e5[k, 4 + x, pl.ds(24, 8), :])
            y_bot[t, x] = jnp.where(sub8, e5[n, 4 + x, pl.ds(0, 8), :], roll(e5[k, 4 + x, pl.ds(0, 8), :], 4, 0))
        y_top[2, x] = e5[3, 4 + x, pl.ds(24, 8), :]
        y_bot[2, x] = e5[3, 4 + x, pl.ds(0, 8), :]
        return carry

    lax.fori_loop(0, 16, take_ends, 0, unroll=4)

    for half in range(2):
        for t, (first, second) in enumerate(((0, 1), (2, 3), (4, 5))):
            acc_a = jnp.zeros((32, 128), F32)
            acc_b = jnp.zeros((32, 128), F32)
            for m in range(8):
                at = 8 * half + m
                rolled = roll(e5[first, 4 + at], 16 * m + 8, 1)
                acc_a = jnp.where((lane32 >> 4) == m, rolled, acc_a)
                if second < 5:
                    rolled = roll(e5[second, 4 + at], 16 * m + 16, 1)
                elif m < 4:
                    rolled = roll(u0[3 + 4 * half + m, pl.ds(8, 32), pl.ds(0, 128)], 16 * m + 16, 1)
                else:
                    continue
                acc_b = jnp.where((((lane32 + 120) & 127) >> 4) == m, rolled, acc_b)
            s_hi[t, half] = jnp.where(first16, acc_a, acc_b)
            s_lo[t, half] = jnp.where(first16, acc_b, acc_a)

    pl.semaphore_wait(barrier, 81)

    def remote(src, dst, send, recv, to):
        return pltpu.make_async_remote_copy(
            src_ref=src, dst_ref=dst, send_sem=send, recv_sem=recv, device_id=to, device_id_type=MESH
        )

    Y0 = {-1: (8, 40, 8), 0: (8, 8, 32), 1: (32, 0, 8)}
    X5 = {-1: (0, 20, 5), 1: (12, 0, 4)}
    XY = {-1: (0, 20, 4), 0: (0, 4, 16), 1: (12, 0, 4)}
    XE = {-1: (3, 11, 2), 1: (9, 1, 2)}
    XU = {-1: (3, 11, 3), 0: (3, 3, 8), 1: (8, 0, 3)}
    XS = {-1: (0, 3, 1), 0: (0, 1, 2), 1: (1, 0, 1)}
    YS = {-1: (0, 40, 8), 0: (0, 8, 32), 1: (24, 0, 8)}
    first = []
    for n, o in enumerate(TALL):
        (xs, xd, xn), (ys, yd, yn) = XS[o[0]], YS[o[1]]
        src, dst = (s_hi, l_lo) if o[2] == 1 else (s_lo, l_hi)
        first.append(remote(
            src.at[:, pl.ds(xs, xn), pl.ds(ys, yn)], dst.at[:, pl.ds(xd, xn), pl.ds(yd, yn)],
            a_send.at[n], a_recv.at[n], nb(o),
        ))
    for n, o in enumerate(FLAT):
        if o[1]:
            (xs, xd, xn), (src, dst) = XY[o[0]], (y_top, y_lo) if o[1] == 1 else (y_bot, y_hi)
        else:
            (xs, xd, xn), (src, dst) = X5[o[0]], (e5, e5)
            xs += 4
        first.append(remote(
            src.at[:, pl.ds(xs, xn)], dst.at[:, pl.ds(xd, xn)], a_send.at[18 + n], a_recv.at[18 + n], nb(o)
        ))
        (xs, xd, xn), (ys, yd, yn) = (XE if o[0] and o[1] else XU)[o[0]], Y0[o[1]]
        first.append(remote(
            u0.at[pl.ds(xs, xn), pl.ds(ys, yn), pl.ds(0, 128)], u0.at[pl.ds(xd, xn), pl.ds(yd, yn), pl.ds(0, 128)],
            a_send.at[26 + n], a_recv.at[26 + n], nb(o),
        ))
    for c in first:
        c.start()

    def coarsen(count, rows, read):
        size = count * rows
        for p in range(count):
            for n in range(4):
                even = read(n, 2 * p)
                work[pl.ds(n * size + p * rows, rows), :] = even if n == 1 else even + read(n, 2 * p + 1)
        work2[pl.ds(0, 3 * size), :] = dot(work[pl.ds(0, 3 * size), :], mats[SUM])
        work2[pl.ds(3 * size, size), :] = dot(work[pl.ds(3 * size, size), :], mats[EVEN])

        def result(n, p):
            at = n * size + p * rows
            low = work2[pl.ds(at, rows // 2, stride=2), :]
            if n == 2:
                return 0.25 * low
            return (0.125 if n == 0 else 0.25) * (low + work2[pl.ds(at + 1, rows // 2, stride=2), :])

        return result

    before = [None] * 8
    got = coarsen(8, 32, lambda n, x: e5[n + 1, 4 + x])
    for n in range(4):
        acc = jnp.zeros((16, 128), F32)
        for m in range(8):
            value = got(n, m)
            if n % 2:
                value_pair = jnp.where(lane16 < 64, before[m], value)
                e1[n // 2, 8 + m, pl.ds(8, 16), :] = value_pair
            before[m] = value
            acc = jnp.where((lane16 >> 4) == m, roll(value, 16 * m + 8, 1), acc)
        e1s[n] = acc

    Y1 = {-1: (8, 24, 8), 0: (8, 8, 16), 1: (16, 0, 8)}
    YT = {-1: (0, 24, 8), 0: (0, 8, 16), 1: (8, 0, 8)}
    X1 = {-1: (8, 16, 8), 0: (8, 8, 8), 1: (8, 0, 8)}
    XT = {-1: 2, 0: 1, 1: 0}

    def spread1(main, strip, low, high, send, recv, lead):
        out = []
        for n, o in enumerate(TALL):
            ys, yd, yn = YT[o[1]]
            dst = low if o[2] == 1 else high
            src = strip.at[:, pl.ds(ys, yn)] if lead else strip.at[pl.ds(ys, yn)]
            dst = dst.at[:, XT[o[0]], pl.ds(yd, yn)] if lead else dst.at[XT[o[0]], pl.ds(yd, yn)]
            out.append(remote(src, dst, send.at[n], recv.at[n], nb(o)))
        for n, o in enumerate(FLAT):
            (xs, xd, xn), (ys, yd, yn) = X1[o[0]], Y1[o[1]]
            src = (pl.ds(xs, xn), pl.ds(ys, yn))
            dst = (pl.ds(xd, xn), pl.ds(yd, yn))
            if lead:
                src, dst = (slice(None),) + src, (slice(None),) + dst
            out.append(remote(main.at[src], main.at[dst], send.at[18 + n], recv.at[18 + n], nb(o)))
        return out

    coefs1 = spread1(e1, e1s, e1s_lo, e1s_hi, b_send, b_recv, True)
    for c in coefs1:
        c.start()

    def twice(n, value):
        other = roll(value, 64, 1)
        return jnp.where(lane16 < 64, other, value) if n % 2 else jnp.where(lane16 < 64, value, other)

    got = coarsen(4, 16, lambda n, x: twice(n, e1[n // 2, 8 + x, pl.ds(8, 16), :]))
    for n in range(4):
        acc = got(n, 0)
        for m in range(1, 4):
            acc = jnp.where((lane8 >> 5) == m, got(n, m), acc)
        ga[core, chip, n] = acc

    def scatter(buf, send, recv):
        def one_step(step, carry):
            remote(buf.at[core, chip], buf.at[core, chip], send.at[step], recv.at[chip], peer(step)).start()
            return carry

        lax.fori_loop(1, 64, one_step, 0)

    def collect(buf, send, recv):
        def one_step(step, carry):
            source = lax.rem(chip + step, 64)
            remote(buf.at[core, source], buf.at[core, source], send.at[step], recv.at[source], peer(step)).wait()
            return carry

        lax.fori_loop(1, 64, one_step, 0)

    scatter(ga, h_send, h_recv)

    for c in first:
        c.wait()
    keep_y0 = one(((iota((48, 256), 0) - 8 + 32 * gy) & 127) != 0)
    lane256 = iota((48, 256), 1)
    keep_z0 = one(((jnp.where(lane256 < 192, lane256, lane256 - 256) + 128 * gz) & 511) != 0)

    def side(n, group, m):
        t, low, high = n // 2, l_lo, l_hi
        if n % 2:
            return pltpu.roll(jnp.where(first48, high[t, group], low[t, group]), lax.rem(112 - 16 * m + 128, 128), 1)
        return pltpu.roll(jnp.where(first48, low[t, group], high[t, group]), lax.rem(120 - 16 * m + 128, 128), 1)

    def fine_row(n, x):
        at = x + 4
        t, swap = ((0, 0), (0, 4), (1, 0), (2, 0), (1, 4))[n]
        low = y_lo[t, x] if swap or n == 3 else roll(y_lo[t, x], 4, 0)
        high = roll(y_hi[t, x], 4, 0) if swap else y_hi[t, x]
        main = jnp.concatenate([low, e5[n, x], high], axis=0)
        return jnp.concatenate([main, side(n, at // 8, lax.rem(at, 8))], axis=1)

    def build0(p, carry):
        e, o = 2 * p, 2 * p + 1
        even = tuple(fine_row(n, e) for n in range(1, 5))
        odd = tuple(fine_row(n, o) for n in range(1, 5))
        keep_e = jnp.where(((e - 4 + 16 * gx) & 127) == 0, 0.0, 1.0).astype(F32)
        keep_n = jnp.where(((e - 2 + 16 * gx) & 127) == 0, 0.0, 1.0).astype(F32)
        for n, value in enumerate(couplings(even, odd, fine_row(2, e + 2), keep_e, keep_n, keep_y0, keep_z0, 1.0, q_l0)):
            k0[n, p] = value
        f_e, f_o = fine_row(0, e), fine_row(0, o)
        g0[RED, p] = jnp.where(q_l0, f_e, f_o)
        g0[BLACK, p] = jnp.where(q_l0, f_o, f_e)
        return carry

    lax.fori_loop(0, 12, build0, 0)

    def side_u(p, carry):
        at = p + 1
        u0[p, :, pl.ds(128, 128)] = side(5, at // 4, lax.rem(at, 4))
        return carry

    lax.fori_loop(0, 14, side_u, 0, unroll=7)

    def half0(colour, src, dst, start, stop):
        def one_pair(p, carry):
            coef = lambda n: k0[n, p]
            total = gathered_sum(colour, src[p + 1], src[p], src[p + 2], g0[colour, p], coef, q_l0)
            dst[p + 1] = total * k0[ID_R if colour == RED else ID_B, p]
            return carry

        lax.fori_loop(start, stop, one_pair, 0, unroll=2)

    half0(RED, u0, r0, 0, 12)
    half0(BLACK, r0, b0, 0, 12)
    half0(RED, b0, r0, 1, 11)
    half0(BLACK, r0, b0, 1, 11)

    def resid0(p):
        coef = lambda n: k0[n, p]
        out = []
        for colour, own, far in ((RED, r0, b0), (BLACK, b0, r0)):
            total = gathered_sum(colour, far[p + 1], far[p], far[p + 2], g0[colour, p], coef, q_l0)
            out.append(total - k0[D_R if colour == RED else D_B, p] * own[p + 1])
        return out

    def restrict0(p, carry):
        red, black = resid0(p + 2)
        work[pl.ds(32 * p, 32), :] = (red + black)[8:40, :128]
        return carry

    lax.fori_loop(0, 8, restrict0, 0, unroll=2)
    work2[pl.ds(0, 256), :] = dot(work[pl.ds(0, 256), :], mats[SUM])
    acc = jnp.zeros((16, 128), F32)
    for m in range(8):
        value = 0.125 * (work2[pl.ds(32 * m, 16, stride=2), :] + work2[pl.ds(32 * m + 1, 16, stride=2), :])
        f1[8 + m, pl.ds(8, 16), :] = value
        acc = jnp.where((lane16 >> 4) == m, roll(value, 16 * m + 8, 1), acc)
    f1s[...] = acc

    right1 = spread1(f1, f1s, f1s_lo, f1s_hi, c_send, c_recv, False)
    for c in right1:
        c.start()

    acc = jnp.zeros((32, 128), F32)
    for m in range(8):
        acc = jnp.where((lane32 >> 4) == m, roll(b0[3 + m, pl.ds(8, 32), pl.ds(0, 128)], 16 * m + 8, 1), acc)
    us[...] = acc
    YU = {-1: (0, 40, 8), 0: (0, 8, 32), 1: (24, 0, 8)}
    fine = []
    for n, o in enumerate(TALL):
        ys, yd, yn = YU[o[1]]
        dst = us_lo if o[2] == 1 else us_hi
        fine.append(remote(us.at[pl.ds(ys, yn)], dst.at[XT[o[0]], pl.ds(yd, yn)], d_send.at[n], d_recv.at[n], nb(o)))
    for n, o in enumerate(FLAT):
        (xs, xd, xn), (ys, yd, yn) = (XE if o[0] and o[1] else XU)[o[0]], Y0[o[1]]
        fine.append(remote(
            b0.at[pl.ds(xs, xn), pl.ds(ys, yn), pl.ds(0, 128)], u1.at[pl.ds(xd, xn), pl.ds(yd, yn), pl.ds(0, 128)],
            d_send.at[18 + n], d_recv.at[18 + n], nb(o),
        ))
    for c in fine:
        c.start()

    for c in coefs1:
        c.wait()
    keep_y1 = one(((iota((32, 128), 0) - 8 + 16 * gy) & 63) != 0)
    keep_z1 = one(((jnp.where(lane32 < 96, lane32, lane32 - 128) + 64 * gz) & 255) != 0)

    def joined(main, low, high, m):
        above = pltpu.roll(high, lax.rem(56 - 16 * m + 256, 128), 1)
        below = pltpu.roll(low, lax.rem(120 - 16 * m + 256, 128), 1)
        return jnp.where(lane32 < 64, main, jnp.where(lane32 < 96, above, below))

    def coarse_row(n, x):
        main = e1[n // 2, x]
        if n % 2:
            main = roll(main, 64, 1)
        return joined(main, e1s_lo[n, x // 8], e1s_hi[n, x // 8], lax.rem(x, 8))

    def build1(p, carry):
        e, o = 2 * p, 2 * p + 1
        even = tuple(coarse_row(n, e) for n in range(4))
        odd = tuple(coarse_row(n, o) for n in range(4))
        after = coarse_row(1, lax.rem(e + 2, 24))
        keep_e = jnp.where(((e - 8 + 8 * gx) & 63) == 0, 0.0, 1.0).astype(F32)
        keep_n = jnp.where(((e - 6 + 8 * gx) & 63) == 0, 0.0, 1.0).astype(F32)
        for n, value in enumerate(couplings(even, odd, after, keep_e, keep_n, keep_y1, keep_z1, 0.25, q_in)):
            k1[n, p] = value
        return carry

    lax.fori_loop(0, 12, build1, 0, unroll=2)

    collect(ga, h_send, h_recv)
    pair_a = remote(ga.at[core], ga.at[core], p_send.at[0], p_recv.at[0], partner)
    pair_a.start()

    for c in right1:
        c.wait()

    def source1(p, carry):
        e, o = 2 * p, 2 * p + 1
        f_e = joined(f1[e], f1s_lo[e // 8], f1s_hi[e // 8], lax.rem(e, 8))
        f_o = joined(f1[o], f1s_lo[o // 8], f1s_hi[o // 8], lax.rem(o, 8))
        red = jnp.where(q_in, f_e, f_o)
        g1[RED, p] = red
        g1[BLACK, p] = jnp.where(q_in, f_o, f_e)
        r1[p + 1] = red * k1[ID_R, p]
        return carry

    lax.fori_loop(0, 12, source1, 0, unroll=4)

    def half1(colour, src, dst):
        def one_pair(p, carry):
            coef = lambda n: k1[n, p]
            total = gathered_sum(colour, src[p + 1], src[p], src[p + 2], g1[colour, p], coef, q_in)
            dst[p + 1] = total * k1[ID_R if colour == RED else ID_B, p]
            return carry

        lax.fori_loop(0, 12, one_pair, 0, unroll=6)

    half1(BLACK, r1, b1)
    half1(RED, b1, r1)
    half1(BLACK, r1, b1)
    for p in range(4):
        coef = lambda n: k1[n, p + 4]
        total = gathered_sum(RED, b1[p + 5], b1[p + 4], b1[p + 6], g1[RED, p + 4], coef, q_in) - k1[D_R, p + 4] * r1[p + 5]
        other = gathered_sum(BLACK, r1[p + 5], r1[p + 4], r1[p + 6], g1[BLACK, p + 4], coef, q_in)
        total = total + (other - k1[D_B, p + 4] * b1[p + 5])
        work[pl.ds(16 * p, 16), :] = jnp.where(lane16 < 64, total[8:24], 0.0)
    work2[pl.ds(0, 64), :] = dot(work[pl.ds(0, 64), :], mats[SUM32])
    acc = jnp.zeros((8, 128), F32)
    for m in range(4):
        value = 0.125 * (work2[pl.ds(16 * m, 8, stride=2), :] + work2[pl.ds(16 * m + 1, 8, stride=2), :])
        acc = jnp.where((lane8 >> 5) == m, value, acc)
    gb[core, chip] = acc

    scatter(gb, i_send, i_recv)

    acc = jnp.zeros((16, 128), F32)
    for m in range(4):
        value = b1[5 + m, pl.ds(8, 16), :]
        value = jnp.where(lane16 < 64, value, roll(value, 64, 1))
        acc = jnp.where((lane16 >> 4) == m, roll(value, 16 * m + 8, 1), acc)
        v1[4 + m, pl.ds(8, 16), :] = value
    v1s[...] = acc
    black1 = []
    for n, o in enumerate(TALL):
        ys, yd, yn = YT[o[1]]
        dst = v1s_lo if o[2] == 1 else v1s_hi
        black1.append(remote(v1s.at[pl.ds(ys, yn)], dst.at[XT[o[0]], pl.ds(yd, yn)], e_send.at[n], e_recv.at[n], nb(o)))
    for n, o in enumerate(FLAT):
        (xs, xd, xn), (ys, yd, yn) = {-1: (4, 8, 4), 0: (4, 4, 4), 1: (4, 0, 4)}[o[0]], Y1[o[1]]
        black1.append(remote(
            v1.at[pl.ds(xs, xn), pl.ds(ys, yn)], v1.at[pl.ds(xd, xn), pl.ds(yd, yn)],
            e_send.at[18 + n], e_recv.at[18 + n], nb(o),
        ))
    for c in black1:
        c.start()

    pair_a.wait()

    def untile(tiles):
        out = []
        for m in range(4):
            total = tiles[0] if m == 0 else roll(tiles[0], -32 * m, 1)
            for k in range(1, 4):
                total = jnp.where((lane8 >> 5) == k, roll(tiles[k], 32 * (k - m), 1), total)
            out.append(total)
        return out

    def place(tiles_of, count):
        def one_block(t, carry):
            bx, by = t // 4, lax.rem(t, 4)
            at = (bx // 2) * 16 + by * 4
            rows = pl.ds(pl.multiple_of(8 * by, 8), 8)
            for n in range(count):
                for m, value in enumerate(untile([tiles_of(lax.rem(bx, 2), at + k, n) for k in range(4)])):
                    w2[n, 4 * bx + m, rows, :] = value
            return carry

        lax.fori_loop(0, 32, one_block, 0, unroll=4)

    place(lambda side_core, at, n: ga[side_core, at, n], 4)

    keep_y2 = one(iota((32, 128), 0) != 0)
    keep_z2 = one(lane32 != 0)

    def build2(p, carry):
        e, o = 2 * p, 2 * p + 1
        even = tuple(w2[n, e] for n in range(4))
        odd = tuple(w2[n, o] for n in range(4))
        keep_e = jnp.where(p == 0, 0.0, 1.0).astype(F32)
        keep_n = jnp.where(p == 15, 0.0, 1.0).astype(F32)
        after = w2[1, lax.rem(e + 2, 32)]
        for n, value in enumerate(couplings(even, odd, after, keep_e, keep_n, keep_y2, keep_z2, 0.25**2, q_in)):
            k2[n, p] = value
        return carry

    lax.fori_loop(0, 16, build2, 0, unroll=2)

    def small(level_coefs, count, rows, period, scale, q, dest):
        keep_y = one(iota((rows, 128), 0) != 0)
        keep_z = one((iota((rows, 128), 1) & (period - 1)) != 0)
        for p in range(count):
            even = tuple(level_coefs(n, 2 * p) for n in range(4))
            odd = tuple(level_coefs(n, 2 * p + 1) for n in range(4))
            after = level_coefs(1, (2 * p + 2) % (2 * count))
            for n, value in enumerate(couplings(
                even, odd, after, 0.0 if p == 0 else 1.0, 0.0 if p == count - 1 else 1.0, keep_y, keep_z, scale, q
            )):
                dest[n, p] = value

    got3 = coarsen(16, 32, lambda n, x: w2[n, x])
    rows3 = [[got3(n, x) for x in range(16)] for n in range(4)]
    for n in range(4):
        for x in range(16):
            w2[n, x, pl.ds(0, 16), :] = rows3[n][x]
    small(lambda n, x: w2[n, x, pl.ds(0, 16), :], 8, 16, 64, 0.25**3, q16, k3)
    got4 = coarsen(8, 16, lambda n, x: w2[n, x, pl.ds(0, 16), :])
    small(got4, 4, 8, 32, 0.25**4, q8, k4)

    collect(gb, i_send, i_recv)
    pair_b = remote(gb.at[core], gb.at[core], p_send.at[1], p_recv.at[1], partner)
    pair_b.start()
    pair_b.wait()

    place(lambda side_core, at, n: gb[side_core, at], 1)

    def source2(p, carry):
        f_e, f_o = w2[0, 2 * p], w2[0, 2 * p + 1]
        red = jnp.where(q_in, f_e, f_o)
        g2[RED, p] = red
        g2[BLACK, p] = jnp.where(q_in, f_o, f_e)
        r2[p + 1] = red * k2[ID_R, p]
        return carry

    lax.fori_loop(0, 16, source2, 0, unroll=2)

    def half2(colour, src, dst):
        def one_pair(p, carry):
            coef = lambda n: k2[n, p]
            total = gathered_sum(colour, src[p + 1], src[p], src[p + 2], g2[colour, p], coef, q_in)
            dst[p + 1] = total * k2[ID_R if colour == RED else ID_B, p]
            return carry

        lax.fori_loop(0, 16, one_pair, 0, unroll=8)

    half2(BLACK, r2, b2)
    half2(RED, b2, r2)
    half2(BLACK, r2, b2)

    def restrict2(p, carry):
        coef = lambda n: k2[n, p]
        total = gathered_sum(RED, b2[p + 1], b2[p], b2[p + 2], g2[RED, p], coef, q_in) - k2[D_R, p] * r2[p + 1]
        other = gathered_sum(BLACK, r2[p + 1], r2[p], r2[p + 2], g2[BLACK, p], coef, q_in)
        work[pl.ds(pl.multiple_of(32 * p, 32), 32), :] = total + (other - k2[D_B, p] * b2[p + 1])
        return carry

    lax.fori_loop(0, 16, restrict2, 0, unroll=4)
    work2[pl.ds(0, 512), :] = dot(work[pl.ds(0, 512), :], mats[SUM])

    def pack(rows, q):
        count = len(rows) // 2
        red = [jnp.where(q, rows[2 * p], rows[2 * p + 1]) for p in range(count)]
        black = [jnp.where(q, rows[2 * p + 1], rows[2 * p]) for p in range(count)]
        return red, black

    def half_small(colour, src, source, k, q, own=None):
        count = len(src)
        out = []
        for p in range(count):
            coef = lambda n: k[n, p]
            total = gathered_sum(colour, src[p], src[p - 1], src[(p + 1) % count], source[p], coef, q)
            if own is None:
                out.append(total * k[ID_R if colour == RED else ID_B, p])
            else:
                out.append(total - k[D_R if colour == RED else D_B, p] * own[p])
        return out

    def paired(count, rows):
        return [
            0.125 * (work2[pl.ds(2 * rows * m, rows, stride=2), :] + work2[pl.ds(2 * rows * m + 1, rows, stride=2), :])
            for m in range(count)
        ]

    def unpacked(red, black, q):
        out = []
        for r, b in zip(red, black):
            out += [jnp.where(q, r, b), jnp.where(q, b, r)]
        return out

    fr3, fb3 = pack(paired(16, 16), q16)
    r3 = [fr3[p] * k3[ID_R, p] for p in range(8)]
    b3 = half_small(BLACK, r3, fb3, k3, q16)
    r3 = half_small(RED, b3, fr3, k3, q16)
    b3 = half_small(BLACK, r3, fb3, k3, q16)
    left_r = half_small(RED, b3, fr3, k3, q16, r3)
    left_b = half_small(BLACK, r3, fb3, k3, q16, b3)
    for p in range(8):
        work[pl.ds(16 * p, 16), :] = left_r[p] + left_b[p]
    work2[pl.ds(0, 128), :] = dot(work[pl.ds(0, 128), :], mats[SUM])

    fr4, fb4 = pack(paired(8, 8), q8)
    r4 = [fr4[p] * k4[ID_R, p] for p in range(4)]
    b4 = half_small(BLACK, r4, fb4, k4, q8)

    def bottom(step, carry):
        black = list(carry[4:])
        red = half_small(RED, black, fr4, k4, q8)
        black = half_small(BLACK, red, fb4, k4, q8)
        return tuple(red + black)

    done = lax.fori_loop(0, 11, bottom, tuple(r4 + b4))
    e4 = unpacked(done[:4], done[4:], q8)

    def doubled(rows, size):
        total = 2 * size * len(rows)
        for m, value in enumerate(rows):
            work[pl.ds(2 * size * m, size, stride=2), :] = value
            work[pl.ds(2 * size * m + 1, size, stride=2), :] = value
        work2[pl.ds(0, total), :] = dot(work[pl.ds(0, total), :], mats[DOUBLE])
        return [work2[pl.ds(2 * size * m, 2 * size), :] for m in range(len(rows))]

    up3 = doubled(e4, 8)
    b3 = [b3[p] + up3[p] for p in range(8)]
    r3 = half_small(RED, b3, fr3, k3, q16)
    b3 = half_small(BLACK, r3, fb3, k3, q16)
    r3 = half_small(RED, b3, fr3, k3, q16)
    b3 = half_small(BLACK, r3, fb3, k3, q16)
    up2 = doubled(unpacked(r3, b3, q16), 16)
    for p in range(16):
        b2[p + 1] = b2[p + 1] + up2[p]

    half2(RED, b2, r2)
    half2(BLACK, r2, b2)
    half2(RED, b2, r2)
    half2(BLACK, r2, b2)

    for c in black1:
        c.wait()

    turn = (4 - 8 * gy) & 31
    for p in range(12):
        x = (p - 4 + 4 * gx) & 31
        red, black = r2[x // 2 + 1], b2[x // 2 + 1]
        lower = jnp.where((x & 1) == 0, 1, 0) == jnp.where(q_in, 1, 0)
        value = pltpu.roll(jnp.where(lower, red, black), turn, 0)[:16]
        work[pl.ds(32 * p, 16, stride=2), :] = value
        work[pl.ds(32 * p + 1, 16, stride=2), :] = value
    work2[pl.ds(0, 384), :] = dot(work[pl.ds(0, 384), :], mats[TO1])

    def lift1(p, carry):
        value = joined(v1[p], v1s_lo[p // 4], v1s_hi[p // 4], lax.rem(p, 4))
        b1[p + 1] = value + work2[pl.ds(pl.multiple_of(32 * p, 32), 32), :]
        return carry

    lax.fori_loop(0, 12, lift1, 0, unroll=4)
    half1(RED, b1, r1)
    half1(BLACK, r1, b1)
    half1(RED, b1, r1)
    half1(BLACK, r1, b1)

    for c in fine:
        c.wait()
    used = (lane32 < 72) | (lane32 >= 120)

    for p in range(14):
        x = p + 5
        red, black = r1[x // 2 + 1], b1[x // 2 + 1]
        value = jnp.where(q_in, red, black) if x % 2 == 0 else jnp.where(q_in, black, red)
        value = jnp.where(used, value, 0.0)[4:28]
        work[pl.ds(48 * p, 24, stride=2), :] = value
        work[pl.ds(48 * p + 1, 24, stride=2), :] = value
    work3[...] = dot(work[pl.ds(0, 672), :], qz0[...])

    def lift_halo(p, carry):
        at = p + 5
        group, m = at // 8, lax.rem(at, 8)
        merged = jnp.where(first48, us_lo[group], us_hi[group])
        beyond = pltpu.roll(merged, lax.rem(120 - 16 * m + 128, 128), 1)
        u1[p] = jnp.concatenate([u1[p, :, pl.ds(0, 128)], beyond], axis=1) + work3[pl.ds(pl.multiple_of(48 * p, 16), 48), :]
        return carry

    def own_black(p, carry):
        u1[p, pl.ds(8, 32), pl.ds(0, 128)] = b0[p, pl.ds(8, 32), pl.ds(0, 128)]
        return carry

    lax.fori_loop(3, 11, own_black, 0)
    lax.fori_loop(0, 14, lift_halo, 0, unroll=2)
    half0(RED, u1, r0, 0, 12)
    half0(BLACK, r0, b0, 0, 12)
    half0(RED, b0, r0, 1, 11)
    half0(BLACK, r0, b0, 1, 11)

    def finish(p, carry):
        red, black = resid0(p + 2)
        red, black = red[8:40, :128], black[8:40, :128]
        res[2 * p] = jnp.where(q_in, red, black)
        res[2 * p + 1] = jnp.where(q_in, black, red)
        red, black = r0[p + 3, pl.ds(8, 32), pl.ds(0, 128)], b0[p + 3, pl.ds(8, 32), pl.ds(0, 128)]
        sol[2 * p] = jnp.where(q_in, red, black)
        sol[2 * p + 1] = jnp.where(q_in, black, red)
        return carry

    lax.fori_loop(0, 8, finish, 0, unroll=2)


def on_device(right_side, initial, alpha, beta_x, beta_y, beta_z):
    block = jax.ShapeDtypeStruct(right_side.shape, F32)
    V = lambda *shape: pltpu.VMEM(shape, F32)
    D = lambda n: pltpu.SemaphoreType.DMA((n,))
    scratch = [
        V(5, 26, 32, 128), V(3, 16, 8, 128), V(3, 16, 8, 128), V(3, 25, 8, 128), V(3, 25, 8, 128),
        V(16, 32, 128), V(14, 48, 256),
        V(3, 2, 32, 128), V(3, 2, 32, 128), V(3, 4, 48, 128), V(3, 4, 48, 128),
        V(15, 12, 48, 256), V(2, 12, 48, 256), V(14, 48, 256), V(14, 48, 256), V(14, 48, 256),
        V(32, 128), V(3, 48, 128), V(3, 48, 128),
        V(2, 24, 32, 128), V(4, 16, 128), V(4, 3, 32, 128), V(4, 3, 32, 128), V(15, 12, 32, 128),
        V(24, 32, 128), V(16, 128), V(3, 32, 128), V(3, 32, 128),
        V(2, 12, 32, 128), V(14, 32, 128), V(14, 32, 128),
        V(12, 32, 128), V(16, 128), V(3, 32, 128), V(3, 32, 128),
        V(2, 64, 4, 8, 128), V(2, 64, 8, 128), V(4, 32, 32, 128), V(15, 16, 32, 128), V(2, 16, 32, 128),
        V(18, 32, 128), V(18, 32, 128), V(15, 8, 16, 128), V(15, 4, 8, 128),
        V(2048, 128), V(2048, 128), V(672, 256), pltpu.VMEM((5, 128, 128), jnp.bfloat16), pltpu.VMEM((128, 256), jnp.bfloat16),
        D(6), D(34), D(34), D(26), D(26), D(26), D(26), D(26), D(26), D(26), D(26),
        D(64), D(64), D(2), D(2), D(64), D(64), D(1), D(1),
    ]
    return pl.pallas_call(
        kernel,
        out_shape=(block, block),
        in_specs=[pl.BlockSpec(memory_space=pl.ANY)] * 6,
        out_specs=[pl.BlockSpec(memory_space=pltpu.VMEM)] * 2,
        scratch_shapes=scratch,
        compiler_params=pltpu.CompilerParams(collective_id=0, has_side_effects=True, vmem_limit_bytes=60 << 20),
    )(right_side, initial, alpha, beta_x, beta_y, beta_z)


def solution(mesh):
    spec = P("gx", "gy", "gz")
    return jax.shard_map(on_device, mesh=mesh, in_specs=(spec,) * 6, out_specs=(spec, spec), check_vma=False)
```

```python
import itertools

import jax
import jax.numpy as jnp
from jax import lax
from jax.experimental import pallas as pl
from jax.experimental.pallas import tpu as pltpu
from jax.sharding import PartitionSpec as P

MESH = pl.DeviceIdType.MESH
F32 = jnp.float32
GRID = (8, 4, 4)
OFFS = [o for o in itertools.product((-1, 0, 1), repeat=3) if o != (0, 0, 0)]
FLAT = sorted([o for o in OFFS if o[2] == 0], key=lambda o: (o[0] != 0, o[1] == 0))
TALL = [o for o in OFFS if o[2] != 0]
RED, BLACK = 0, 1
SAME, OTHER_R, YL_R, YH_R, ZL_R, ZH_R, ID_R, D_R, OTHER_B, YL_B, YH_B, ZL_B, ZH_B, ID_B, D_B = range(15)


def dot(a, pick):
    total = None
    for _ in range(3):
        term = a.astype(jnp.bfloat16)
        part = jnp.dot(term, pick, preferred_element_type=F32)
        total = part if total is None else total + part
        a = a - term.astype(F32)
    return total


def iota(shape, dim):
    return lax.broadcasted_iota(jnp.int32, shape, dim)


def checker(shape):
    return ((iota(shape, 0) + iota(shape, 1)) & 1) == 0


def roll(x, shift, axis):
    size = x.shape[axis]
    shift = shift % size
    return pltpu.roll(x, shift, axis) if shift else x


def couplings(even, odd, next_x, keep_x, keep_next, keep_y, keep_z, scale, q0):
    parts = []
    for alpha, low_x, low_y, low_z in (even, odd):
        low_y, low_z = scale * low_y, scale * low_z
        own_y, own_z = low_y * keep_y, low_z * keep_z
        high_y, high_z = roll(own_y, -1, 0), roll(own_z, -1, 1)
        parts.append((own_y, high_y, own_z, high_z, alpha + (low_y + high_y) + (low_z + high_z)))
    x_e, x_o = scale * even[1], scale * odd[1]
    x_n = scale * next_x * keep_next
    d_e = parts[0][4] + (x_e + x_o)
    d_o = parts[1][4] + (x_o + x_n)
    x_e = x_e * keep_x
    i_e, i_o = 1.0 / d_e, 1.0 / d_o
    red = [jnp.where(q0, x_e, x_n)] + [jnp.where(q0, parts[0][n], parts[1][n]) for n in range(4)]
    red += [jnp.where(q0, i_e, i_o), jnp.where(q0, d_e, d_o)]
    black = [jnp.where(q0, x_n, x_e)] + [jnp.where(q0, parts[1][n], parts[0][n]) for n in range(4)]
    black += [jnp.where(q0, i_o, i_e), jnp.where(q0, d_o, d_e)]
    return [x_o] + red + black


def gathered_sum(colour, here, below, above, source, coef, q0):
    if colour == RED:
        other, base = jnp.where(q0, below, above), OTHER_R
    else:
        other, base = jnp.where(q0, above, below), OTHER_B
    total = source + coef(SAME) * here + coef(base) * other
    total = total + (coef(base + 1) * roll(here, 1, 0) + coef(base + 2) * roll(here, -1, 0))
    return total + (coef(base + 3) * roll(here, 1, 1) + coef(base + 4) * roll(here, -1, 1))


def kernel(
    f_hbm, u_hbm, a_hbm, bx_hbm, by_hbm, bz_hbm, sol, res,
    e5, y_top, y_bot, y_lo, y_hi, u_in, u0, s_hi, s_lo, l_lo, l_hi, k0, g0, r0, b0, u1, us, us_lo, us_hi,
    e1, e1s, e1s_lo, e1s_hi, k1, f1, f1s, f1s_lo, f1s_hi, g1, r1, b1, v1, v1s, v1s_lo, v1s_hi,
    ga, gb, w2, k2, g2, r2, b2, k3, k4, work, work2, work3, mats, qz0,
    in_sem, a_send, a_recv, b_send, b_recv, c_send, c_recv, d_send, d_recv, e_send, e_recv,
    h_send, h_recv, p_send, p_recv, i_send, i_recv,
):
    gx, gy, gz = lax.axis_index("gx"), lax.axis_index("gy"), lax.axis_index("gz")
    me = (gx, gy, gz)
    core = lax.rem(gx, 2)
    chip = ((gx // 2) * 4 + gy) * 4 + gz

    def nb(o):
        return tuple(lax.rem(me[d] + (o[d] + GRID[d]), GRID[d]) if o[d] else me[d] for d in range(3))

    def peer(step):
        other = lax.rem(chip + step, 64)
        return (other // 16) * 2 + core, lax.rem(other // 4, 4), lax.rem(other, 4)

    partner = (gx + 1 - 2 * core, gy, gz)

    loads = [pltpu.make_async_copy(u_hbm, u_in, in_sem.at[5])]
    for n, ref in enumerate((f_hbm, a_hbm, bx_hbm, by_hbm, bz_hbm)):
        loads.append(pltpu.make_async_copy(ref, e5.at[n, pl.ds(4, 16)], in_sem.at[n]))
    for c in loads:
        c.start()

    def zero(ref, at):
        ref[at] = jnp.zeros(ref.shape[1:], F32)

    for ref in (u0, u1):
        zero(ref, 0)
        zero(ref, 13)
    barrier = pltpu.get_barrier_semaphore()

    def greet(step, carry):
        pl.semaphore_signal(barrier, inc=1, device_id=peer(step), device_id_type=MESH)
        return carry

    lax.fori_loop(1, 64, greet, 0)
    for o in OFFS:
        if o[0]:
            pl.semaphore_signal(barrier, inc=1, device_id=nb(o), device_id_type=MESH)

    row, col = iota((128, 128), 0), iota((128, 128), 1)
    one = lambda cond: jnp.where(cond, 1.0, 0.0).astype(F32)
    SUM, EVEN, SUM32, DOUBLE, TO1 = range(5)
    mats[SUM] = one((row >> 1) == (col & 63)).astype(jnp.bfloat16)
    mats[EVEN] = one(row == 2 * (col & 63)).astype(jnp.bfloat16)
    mats[SUM32] = one((row >> 1) == (col & 31)).astype(jnp.bfloat16)
    mats[DOUBLE] = one(row == (col >> 1)).astype(jnp.bfloat16)
    z1 = jnp.where(col < 96, col, col - 128)
    mats[TO1] = one(row == (((z1 + 64 * gz) >> 1) & 127)).astype(jnp.bfloat16)
    wide_col, wide_row = iota((128, 256), 1), iota((128, 256), 0)
    z0 = jnp.where(wide_col < 192, wide_col, wide_col - 256)
    qz0[...] = one(wide_row == ((z0 >> 1) & 127)).astype(jnp.bfloat16)

    q_l0 = checker((48, 256))
    q_in = checker((32, 128))
    q16 = checker((16, 128))
    q8 = checker((8, 128))
    lane8 = iota((8, 128), 1)
    lane16 = iota((16, 128), 1)
    lane32 = iota((32, 128), 1)
    lane48 = iota((48, 128), 1)
    first16 = (lane32 & 15) < 8
    first48 = (lane48 & 15) < 8

    for ref, at in ((r0, 0), (r0, 13), (b0, 0), (b0, 13), (r1, 0), (r1, 13), (b1, 0), (b1, 13)):
        zero(ref, at)
    for ref in (r2, b2):
        zero(ref, 0)
        zero(ref, 17)

    for c in loads:
        c.wait()

    def take_black(p, carry):
        u0[4 + p - 1, pl.ds(8, 32), pl.ds(0, 128)] = jnp.where(q_in, u_in[2 * p + 1], u_in[2 * p])
        return carry

    lax.fori_loop(0, 8, take_black, 0, unroll=2)

    sub8 = iota((8, 128), 0) < 4
    y_lo[:, 24] = jnp.zeros((3, 8, 128), F32)
    y_hi[:, 24] = jnp.zeros((3, 8, 128), F32)

    def take_ends(x, carry):
        for t, (n, k) in enumerate(((0, 1), (2, 4))):
            y_top[t, x] = jnp.where(sub8, roll(e5[n, 4 + x, pl.ds(24, 8), :], 4, 0), e5[k, 4 + x, pl.ds(24, 8), :])
            y_bot[t, x] = jnp.where(sub8, e5[n, 4 + x, pl.ds(0, 8), :], roll(e5[k, 4 + x, pl.ds(0, 8), :], 4, 0))
        y_top[2, x] = e5[3, 4 + x, pl.ds(24, 8), :]
        y_bot[2, x] = e5[3, 4 + x, pl.ds(0, 8), :]
        return carry

    lax.fori_loop(0, 16, take_ends, 0, unroll=4)

    pl.semaphore_wait(barrier, 81)

    def remote(src, dst, send, recv, to):
        return pltpu.make_async_remote_copy(
            src_ref=src, dst_ref=dst, send_sem=send, recv_sem=recv, device_id=to, device_id_type=MESH
        )

    Y0 = {-1: (8, 40, 8), 0: (8, 8, 32), 1: (32, 0, 8)}
    X5 = {-1: (0, 20, 5), 1: (12, 0, 4)}
    XY = {-1: (0, 20, 4), 0: (0, 4, 16), 1: (12, 0, 4)}
    XE = {-1: (3, 11, 2), 1: (9, 1, 2)}
    XU = {-1: (3, 11, 3), 0: (3, 3, 8), 1: (8, 0, 3)}
    XS = {-1: (0, 3, 1), 0: (0, 1, 2), 1: (1, 0, 1)}
    YS = {-1: (0, 40, 8), 0: (0, 8, 32), 1: (24, 0, 8)}
    first = []
    for n, o in enumerate(FLAT):
        if o[1]:
            (xs, xd, xn), (src, dst) = XY[o[0]], (y_top, y_lo) if o[1] == 1 else (y_bot, y_hi)
        else:
            (xs, xd, xn), (src, dst) = X5[o[0]], (e5, e5)
            xs += 4
        first.append(remote(
            src.at[:, pl.ds(xs, xn)], dst.at[:, pl.ds(xd, xn)], a_send.at[18 + n], a_recv.at[18 + n], nb(o)
        ))
        (xs, xd, xn), (ys, yd, yn) = (XE if o[0] and o[1] else XU)[o[0]], Y0[o[1]]
        first.append(remote(
            u0.at[pl.ds(xs, xn), pl.ds(ys, yn), pl.ds(0, 128)], u0.at[pl.ds(xd, xn), pl.ds(yd, yn), pl.ds(0, 128)],
            a_send.at[26 + n], a_recv.at[26 + n], nb(o),
        ))
    for c in first:
        c.start()

    for half in range(2):
        for t, (one_n, two_n) in enumerate(((0, 1), (2, 3), (4, 5))):
            acc_a = jnp.zeros((32, 128), F32)
            acc_b = jnp.zeros((32, 128), F32)
            for m in range(8):
                at = 8 * half + m
                rolled = roll(e5[one_n, 4 + at], 16 * m + 8, 1)
                acc_a = jnp.where((lane32 >> 4) == m, rolled, acc_a)
                if two_n < 5:
                    rolled = roll(e5[two_n, 4 + at], 16 * m + 16, 1)
                elif m < 4:
                    rolled = roll(u0[3 + 4 * half + m, pl.ds(8, 32), pl.ds(0, 128)], 16 * m + 16, 1)
                else:
                    continue
                acc_b = jnp.where((((lane32 + 120) & 127) >> 4) == m, rolled, acc_b)
            s_hi[t, half] = jnp.where(first16, acc_a, acc_b)
            s_lo[t, half] = jnp.where(first16, acc_b, acc_a)

    beyond = []
    for n, o in enumerate(TALL):
        (xs, xd, xn), (ys, yd, yn) = XS[o[0]], YS[o[1]]
        src, dst = (s_hi, l_lo) if o[2] == 1 else (s_lo, l_hi)
        beyond.append(remote(
            src.at[:, pl.ds(xs, xn), pl.ds(ys, yn)], dst.at[:, pl.ds(xd, xn), pl.ds(yd, yn)],
            a_send.at[n], a_recv.at[n], nb(o),
        ))
    for c in beyond:
        c.start()
    first += beyond

    def coarsen(count, rows, read):
        size = count * rows
        for p in range(count):
            for n in range(4):
                even = read(n, 2 * p)
                work[pl.ds(n * size + p * rows, rows), :] = even if n == 1 else even + read(n, 2 * p + 1)
        work2[pl.ds(0, 3 * size), :] = dot(work[pl.ds(0, 3 * size), :], mats[SUM])
        work2[pl.ds(3 * size, size), :] = dot(work[pl.ds(3 * size, size), :], mats[EVEN])

        def result(n, p):
            at = n * size + p * rows
            low = work2[pl.ds(at, rows // 2, stride=2), :]
            if n == 2:
                return 0.25 * low
            return (0.125 if n == 0 else 0.25) * (low + work2[pl.ds(at + 1, rows // 2, stride=2), :])

        return result

    before = [None] * 8
    got = coarsen(8, 32, lambda n, x: e5[n + 1, 4 + x])
    for n in range(4):
        acc = jnp.zeros((16, 128), F32)
        for m in range(8):
            value = got(n, m)
            if n % 2:
                value_pair = jnp.where(lane16 < 64, before[m], value)
                e1[n // 2, 8 + m, pl.ds(8, 16), :] = value_pair
            before[m] = value
            acc = jnp.where((lane16 >> 4) == m, roll(value, 16 * m + 8, 1), acc)
        e1s[n] = acc

    Y1 = {-1: (8, 24, 8), 0: (8, 8, 16), 1: (16, 0, 8)}
    YT = {-1: (0, 24, 8), 0: (0, 8, 16), 1: (8, 0, 8)}
    X1 = {-1: (8, 16, 8), 0: (8, 8, 8), 1: (8, 0, 8)}
    XT = {-1: 2, 0: 1, 1: 0}

    def spread1(main, strip, low, high, send, recv, lead):
        out = []
        for n, o in enumerate(TALL):
            ys, yd, yn = YT[o[1]]
            dst = low if o[2] == 1 else high
            src = strip.at[:, pl.ds(ys, yn)] if lead else strip.at[pl.ds(ys, yn)]
            dst = dst.at[:, XT[o[0]], pl.ds(yd, yn)] if lead else dst.at[XT[o[0]], pl.ds(yd, yn)]
            out.append(remote(src, dst, send.at[n], recv.at[n], nb(o)))
        for n, o in enumerate(FLAT):
            (xs, xd, xn), (ys, yd, yn) = X1[o[0]], Y1[o[1]]
            src = (pl.ds(xs, xn), pl.ds(ys, yn))
            dst = (pl.ds(xd, xn), pl.ds(yd, yn))
            if lead:
                src, dst = (slice(None),) + src, (slice(None),) + dst
            out.append(remote(main.at[src], main.at[dst], send.at[18 + n], recv.at[18 + n], nb(o)))
        return out

    coefs1 = spread1(e1, e1s, e1s_lo, e1s_hi, b_send, b_recv, True)
    for c in coefs1:
        c.start()

    def twice(n, value):
        other = roll(value, 64, 1)
        return jnp.where(lane16 < 64, other, value) if n % 2 else jnp.where(lane16 < 64, value, other)

    got = coarsen(4, 16, lambda n, x: twice(n, e1[n // 2, 8 + x, pl.ds(8, 16), :]))
    for n in range(4):
        acc = got(n, 0)
        for m in range(1, 4):
            acc = jnp.where((lane8 >> 5) == m, got(n, m), acc)
        ga[core, gx // 2, gy, gz, n] = acc

    def along(axis, k):
        if axis == "z":
            return lax.rem(gx + 2 * k, 8), gy, gz
        return (gx, lax.rem(gy + k, 4), gz) if axis == "y" else (gx, gy, lax.rem(gz + k, 4))

    def part(order, axis, back):
        z, y, x = gx // 2, gy, gz
        if axis == "z":
            z = lax.rem(z + 4 - back, 4)
        elif axis == "y":
            y = lax.rem(y + 4 - back, 4)
        else:
            x = lax.rem(x + 4 - back, 4)
        if order == "xyz":
            y, x = slice(None) if axis == "z" else y, x if axis == "x" else slice(None)
            return ga.at[core, z, y, x, pl.ds(0, 2)]
        z, y = slice(None) if axis == "x" else z, y if axis == "y" else slice(None)
        return ga.at[core, z, y, x, pl.ds(2, 2)]

    def legs(stage):
        for n, order in enumerate(("xyz", "yzx")):
            for k in range(1, 4):
                yield order, order[stage], k, 6 * stage + 3 * n + k - 1

    def pass_on(stage):
        for order, axis, k, at in legs(stage):
            own = part(order, axis, 0)
            remote(own, own, h_send.at[at], h_recv.at[at], along(axis, k)).start()

    def passed_on(stage):
        for order, axis, k, at in legs(stage):
            own, theirs = part(order, axis, 0), part(order, axis, k)
            remote(own, own, h_send.at[at], h_recv.at[at], along(axis, k)).wait_send()
            remote(theirs, theirs, h_send.at[at], h_recv.at[at], along(axis, k)).wait_recv()

    pass_on(0)
    passed_on(0)
    pass_on(1)

    for c in first:
        c.wait_recv()
    keep_y0 = one(((iota((48, 256), 0) - 8 + 32 * gy) & 127) != 0)
    lane256 = iota((48, 256), 1)
    keep_z0 = one(((jnp.where(lane256 < 192, lane256, lane256 - 256) + 128 * gz) & 511) != 0)

    def side(n, group, m):
        t, low, high = n // 2, l_lo, l_hi
        if n % 2:
            return pltpu.roll(jnp.where(first48, high[t, group], low[t, group]), lax.rem(112 - 16 * m + 128, 128), 1)
        return pltpu.roll(jnp.where(first48, low[t, group], high[t, group]), lax.rem(120 - 16 * m + 128, 128), 1)

    def fine_row(n, x):
        at = x + 4
        t, swap = ((0, 0), (0, 4), (1, 0), (2, 0), (1, 4))[n]
        low = y_lo[t, x] if swap or n == 3 else roll(y_lo[t, x], 4, 0)
        high = roll(y_hi[t, x], 4, 0) if swap else y_hi[t, x]
        main = jnp.concatenate([low, e5[n, x], high], axis=0)
        return jnp.concatenate([main, side(n, at // 8, lax.rem(at, 8))], axis=1)

    def build0(p, carry):
        e, o = 2 * p, 2 * p + 1
        even = tuple(fine_row(n, e) for n in range(1, 5))
        odd = tuple(fine_row(n, o) for n in range(1, 5))
        keep_e = jnp.where(((e - 4 + 16 * gx) & 127) == 0, 0.0, 1.0).astype(F32)
        keep_n = jnp.where(((e - 2 + 16 * gx) & 127) == 0, 0.0, 1.0).astype(F32)
        for n, value in enumerate(couplings(even, odd, fine_row(2, e + 2), keep_e, keep_n, keep_y0, keep_z0, 1.0, q_l0)):
            k0[n, p] = value
        f_e, f_o = fine_row(0, e), fine_row(0, o)
        g0[RED, p] = jnp.where(q_l0, f_e, f_o)
        g0[BLACK, p] = jnp.where(q_l0, f_o, f_e)
        return carry

    lax.fori_loop(0, 12, build0, 0)

    passed_on(1)
    pass_on(2)

    def side_u(p, carry):
        at = p + 1
        u0[p, :, pl.ds(128, 128)] = side(5, at // 4, lax.rem(at, 4))
        return carry

    lax.fori_loop(0, 14, side_u, 0, unroll=7)

    def half0(colour, src, dst, start, stop):
        def one_pair(p, carry):
            coef = lambda n: k0[n, p]
            total = gathered_sum(colour, src[p + 1], src[p], src[p + 2], g0[colour, p], coef, q_l0)
            dst[p + 1] = total * k0[ID_R if colour == RED else ID_B, p]
            return carry

        lax.fori_loop(start, stop, one_pair, 0, unroll=2)

    half0(RED, u0, r0, 0, 12)
    half0(BLACK, r0, b0, 0, 12)
    half0(RED, b0, r0, 1, 11)
    half0(BLACK, r0, b0, 1, 11)

    def resid0(p):
        coef = lambda n: k0[n, p]
        out = []
        for colour, own, far in ((RED, r0, b0), (BLACK, b0, r0)):
            total = gathered_sum(colour, far[p + 1], far[p], far[p + 2], g0[colour, p], coef, q_l0)
            out.append(total - k0[D_R if colour == RED else D_B, p] * own[p + 1])
        return out

    def restrict0(p, carry):
        red, black = resid0(p + 2)
        work[pl.ds(32 * p, 32), :] = (red + black)[8:40, :128]
        return carry

    lax.fori_loop(0, 8, restrict0, 0, unroll=2)
    work2[pl.ds(0, 256), :] = dot(work[pl.ds(0, 256), :], mats[SUM])
    acc = jnp.zeros((16, 128), F32)
    for m in range(8):
        value = 0.125 * (work2[pl.ds(32 * m, 16, stride=2), :] + work2[pl.ds(32 * m + 1, 16, stride=2), :])
        f1[8 + m, pl.ds(8, 16), :] = value
        acc = jnp.where((lane16 >> 4) == m, roll(value, 16 * m + 8, 1), acc)
    f1s[...] = acc

    right1 = spread1(f1, f1s, f1s_lo, f1s_hi, c_send, c_recv, False)
    for c in right1:
        c.start()

    acc = jnp.zeros((32, 128), F32)
    for m in range(8):
        acc = jnp.where((lane32 >> 4) == m, roll(b0[3 + m, pl.ds(8, 32), pl.ds(0, 128)], 16 * m + 8, 1), acc)
    us[...] = acc
    YU = {-1: (0, 40, 8), 0: (0, 8, 32), 1: (24, 0, 8)}
    fine = []
    for n, o in enumerate(TALL):
        ys, yd, yn = YU[o[1]]
        dst = us_lo if o[2] == 1 else us_hi
        fine.append(remote(us.at[pl.ds(ys, yn)], dst.at[XT[o[0]], pl.ds(yd, yn)], d_send.at[n], d_recv.at[n], nb(o)))
    for n, o in enumerate(FLAT):
        (xs, xd, xn), (ys, yd, yn) = (XE if o[0] and o[1] else XU)[o[0]], Y0[o[1]]
        fine.append(remote(
            b0.at[pl.ds(xs, xn), pl.ds(ys, yn), pl.ds(0, 128)], u1.at[pl.ds(xd, xn), pl.ds(yd, yn), pl.ds(0, 128)],
            d_send.at[18 + n], d_recv.at[18 + n], nb(o),
        ))
    for c in fine:
        c.start()

    for c in first:
        c.wait_send()
    for c in coefs1:
        c.wait()
    keep_y1 = one(((iota((32, 128), 0) - 8 + 16 * gy) & 63) != 0)
    keep_z1 = one(((jnp.where(lane32 < 96, lane32, lane32 - 128) + 64 * gz) & 255) != 0)

    def joined(main, low, high, m):
        above = pltpu.roll(high, lax.rem(56 - 16 * m + 256, 128), 1)
        below = pltpu.roll(low, lax.rem(120 - 16 * m + 256, 128), 1)
        return jnp.where(lane32 < 64, main, jnp.where(lane32 < 96, above, below))

    def coarse_row(n, x):
        main = e1[n // 2, x]
        if n % 2:
            main = roll(main, 64, 1)
        return joined(main, e1s_lo[n, x // 8], e1s_hi[n, x // 8], lax.rem(x, 8))

    def build1(p, carry):
        e, o = 2 * p, 2 * p + 1
        even = tuple(coarse_row(n, e) for n in range(4))
        odd = tuple(coarse_row(n, o) for n in range(4))
        after = coarse_row(1, lax.rem(e + 2, 24))
        keep_e = jnp.where(((e - 8 + 8 * gx) & 63) == 0, 0.0, 1.0).astype(F32)
        keep_n = jnp.where(((e - 6 + 8 * gx) & 63) == 0, 0.0, 1.0).astype(F32)
        for n, value in enumerate(couplings(even, odd, after, keep_e, keep_n, keep_y1, keep_z1, 0.25, q_in)):
            k1[n, p] = value
        return carry

    lax.fori_loop(0, 12, build1, 0, unroll=2)

    passed_on(2)
    pair_a = remote(ga.at[core], ga.at[core], p_send.at[0], p_recv.at[0], partner)
    pair_a.start()

    for c in right1:
        c.wait_recv()

    def source1(p, carry):
        e, o = 2 * p, 2 * p + 1
        f_e = joined(f1[e], f1s_lo[e // 8], f1s_hi[e // 8], lax.rem(e, 8))
        f_o = joined(f1[o], f1s_lo[o // 8], f1s_hi[o // 8], lax.rem(o, 8))
        red = jnp.where(q_in, f_e, f_o)
        g1[RED, p] = red
        g1[BLACK, p] = jnp.where(q_in, f_o, f_e)
        r1[p + 1] = red * k1[ID_R, p]
        return carry

    lax.fori_loop(0, 12, source1, 0, unroll=4)

    def half1(colour, src, dst):
        def one_pair(p, carry):
            coef = lambda n: k1[n, p]
            total = gathered_sum(colour, src[p + 1], src[p], src[p + 2], g1[colour, p], coef, q_in)
            dst[p + 1] = total * k1[ID_R if colour == RED else ID_B, p]
            return carry

        lax.fori_loop(0, 12, one_pair, 0, unroll=6)

    half1(BLACK, r1, b1)
    half1(RED, b1, r1)
    half1(BLACK, r1, b1)
    for p in range(4):
        coef = lambda n: k1[n, p + 4]
        total = gathered_sum(RED, b1[p + 5], b1[p + 4], b1[p + 6], g1[RED, p + 4], coef, q_in) - k1[D_R, p + 4] * r1[p + 5]
        other = gathered_sum(BLACK, r1[p + 5], r1[p + 4], r1[p + 6], g1[BLACK, p + 4], coef, q_in)
        total = total + (other - k1[D_B, p + 4] * b1[p + 5])
        work[pl.ds(16 * p, 16), :] = jnp.where(lane16 < 64, total[8:24], 0.0)
    work2[pl.ds(0, 64), :] = dot(work[pl.ds(0, 64), :], mats[SUM32])
    acc = jnp.zeros((8, 128), F32)
    for m in range(4):
        value = 0.125 * (work2[pl.ds(16 * m, 8, stride=2), :] + work2[pl.ds(16 * m + 1, 8, stride=2), :])
        acc = jnp.where((lane8 >> 5) == m, value, acc)
    gb[core, chip] = acc

    turns = [[lax.rem(at + k, 4) for k in range(4)] for at in (gx // 2, gy, gz)]
    for k in sorted(itertools.product(range(4), repeat=3), key=lambda k: -sum(min(n, 4 - n) for n in k))[:-1]:
        to = (turns[0][k[0]] * 2 + core, turns[1][k[1]], turns[2][k[2]])
        remote(gb.at[core, chip], gb.at[core, chip], i_send.at[0], i_recv.at[0], to).start()

    acc = jnp.zeros((16, 128), F32)
    for m in range(4):
        value = b1[5 + m, pl.ds(8, 16), :]
        value = jnp.where(lane16 < 64, value, roll(value, 64, 1))
        acc = jnp.where((lane16 >> 4) == m, roll(value, 16 * m + 8, 1), acc)
        v1[4 + m, pl.ds(8, 16), :] = value
    v1s[...] = acc
    black1 = []
    for n, o in enumerate(TALL):
        ys, yd, yn = YT[o[1]]
        dst = v1s_lo if o[2] == 1 else v1s_hi
        black1.append(remote(v1s.at[pl.ds(ys, yn)], dst.at[XT[o[0]], pl.ds(yd, yn)], e_send.at[n], e_recv.at[n], nb(o)))
    for n, o in enumerate(FLAT):
        (xs, xd, xn), (ys, yd, yn) = {-1: (4, 8, 4), 0: (4, 4, 4), 1: (4, 0, 4)}[o[0]], Y1[o[1]]
        black1.append(remote(
            v1.at[pl.ds(xs, xn), pl.ds(ys, yn)], v1.at[pl.ds(xd, xn), pl.ds(yd, yn)],
            e_send.at[18 + n], e_recv.at[18 + n], nb(o),
        ))
    for c in black1:
        c.start()

    for c in right1:
        c.wait_send()

    pair_a.wait()

    def untile(tiles):
        out = []
        for m in range(4):
            total = tiles[0] if m == 0 else roll(tiles[0], -32 * m, 1)
            for k in range(1, 4):
                total = jnp.where((lane8 >> 5) == k, roll(tiles[k], 32 * (k - m), 1), total)
            out.append(total)
        return out

    def place(tiles_of, count):
        def one_block(t, carry):
            bx, by = t // 4, lax.rem(t, 4)
            rows = pl.ds(pl.multiple_of(8 * by, 8), 8)
            for n in range(count):
                for m, value in enumerate(untile([tiles_of(lax.rem(bx, 2), bx // 2, by, k, n) for k in range(4)])):
                    w2[n, 4 * bx + m, rows, :] = value
            return carry

        lax.fori_loop(0, 32, one_block, 0, unroll=4)

    place(lambda side_core, bz, by, k, n: ga[side_core, bz, by, k, n], 4)

    keep_y2 = one(iota((32, 128), 0) != 0)
    keep_z2 = one(lane32 != 0)

    def build2(p, carry):
        e, o = 2 * p, 2 * p + 1
        even = tuple(w2[n, e] for n in range(4))
        odd = tuple(w2[n, o] for n in range(4))
        keep_e = jnp.where(p == 0, 0.0, 1.0).astype(F32)
        keep_n = jnp.where(p == 15, 0.0, 1.0).astype(F32)
        after = w2[1, lax.rem(e + 2, 32)]
        for n, value in enumerate(couplings(even, odd, after, keep_e, keep_n, keep_y2, keep_z2, 0.25**2, q_in)):
            k2[n, p] = value
        return carry

    lax.fori_loop(0, 16, build2, 0, unroll=2)

    def small(level_coefs, count, rows, period, scale, q, dest):
        keep_y = one(iota((rows, 128), 0) != 0)
        keep_z = one((iota((rows, 128), 1) & (period - 1)) != 0)
        for p in range(count):
            even = tuple(level_coefs(n, 2 * p) for n in range(4))
            odd = tuple(level_coefs(n, 2 * p + 1) for n in range(4))
            after = level_coefs(1, (2 * p + 2) % (2 * count))
            for n, value in enumerate(couplings(
                even, odd, after, 0.0 if p == 0 else 1.0, 0.0 if p == count - 1 else 1.0, keep_y, keep_z, scale, q
            )):
                dest[n, p] = value

    got3 = coarsen(16, 32, lambda n, x: w2[n, x])
    rows3 = [[got3(n, x) for x in range(16)] for n in range(4)]
    for n in range(4):
        for x in range(16):
            w2[n, x, pl.ds(0, 16), :] = rows3[n][x]
    small(lambda n, x: w2[n, x, pl.ds(0, 16), :], 8, 16, 64, 0.25**3, q16, k3)
    got4 = coarsen(8, 16, lambda n, x: w2[n, x, pl.ds(0, 16), :])
    small(got4, 4, 8, 32, 0.25**4, q8, k4)

    others = gb.at[core, pl.ds(0, 63)]
    remote(others, others, i_send.at[0], i_recv.at[0], partner).wait()
    pair_b = remote(gb.at[core], gb.at[core], p_send.at[1], p_recv.at[1], partner)
    pair_b.start()
    pair_b.wait()

    place(lambda side_core, bz, by, k, n: gb[side_core, bz * 16 + by * 4 + k], 1)

    def source2(p, carry):
        f_e, f_o = w2[0, 2 * p], w2[0, 2 * p + 1]
        red = jnp.where(q_in, f_e, f_o)
        g2[RED, p] = red
        g2[BLACK, p] = jnp.where(q_in, f_o, f_e)
        r2[p + 1] = red * k2[ID_R, p]
        return carry

    lax.fori_loop(0, 16, source2, 0, unroll=2)

    def half2(colour, src, dst):
        def one_pair(p, carry):
            coef = lambda n: k2[n, p]
            total = gathered_sum(colour, src[p + 1], src[p], src[p + 2], g2[colour, p], coef, q_in)
            dst[p + 1] = total * k2[ID_R if colour == RED else ID_B, p]
            return carry

        lax.fori_loop(0, 16, one_pair, 0, unroll=8)

    half2(BLACK, r2, b2)
    half2(RED, b2, r2)
    half2(BLACK, r2, b2)

    def restrict2(p, carry):
        coef = lambda n: k2[n, p]
        total = gathered_sum(RED, b2[p + 1], b2[p], b2[p + 2], g2[RED, p], coef, q_in) - k2[D_R, p] * r2[p + 1]
        other = gathered_sum(BLACK, r2[p + 1], r2[p], r2[p + 2], g2[BLACK, p], coef, q_in)
        work[pl.ds(pl.multiple_of(32 * p, 32), 32), :] = total + (other - k2[D_B, p] * b2[p + 1])
        return carry

    lax.fori_loop(0, 16, restrict2, 0, unroll=4)
    work2[pl.ds(0, 512), :] = dot(work[pl.ds(0, 512), :], mats[SUM])

    def pack(rows, q):
        count = len(rows) // 2
        red = [jnp.where(q, rows[2 * p], rows[2 * p + 1]) for p in range(count)]
        black = [jnp.where(q, rows[2 * p + 1], rows[2 * p]) for p in range(count)]
        return red, black

    def half_small(colour, src, source, k, q, own=None):
        count = len(src)
        out = []
        for p in range(count):
            coef = lambda n: k[n, p]
            total = gathered_sum(colour, src[p], src[p - 1], src[(p + 1) % count], source[p], coef, q)
            if own is None:
                out.append(total * k[ID_R if colour == RED else ID_B, p])
            else:
                out.append(total - k[D_R if colour == RED else D_B, p] * own[p])
        return out

    def paired(count, rows):
        return [
            0.125 * (work2[pl.ds(2 * rows * m, rows, stride=2), :] + work2[pl.ds(2 * rows * m + 1, rows, stride=2), :])
            for m in range(count)
        ]

    def unpacked(red, black, q):
        out = []
        for r, b in zip(red, black):
            out += [jnp.where(q, r, b), jnp.where(q, b, r)]
        return out

    fr3, fb3 = pack(paired(16, 16), q16)
    r3 = [fr3[p] * k3[ID_R, p] for p in range(8)]
    b3 = half_small(BLACK, r3, fb3, k3, q16)
    r3 = half_small(RED, b3, fr3, k3, q16)
    b3 = half_small(BLACK, r3, fb3, k3, q16)
    left_r = half_small(RED, b3, fr3, k3, q16, r3)
    left_b = half_small(BLACK, r3, fb3, k3, q16, b3)
    for p in range(8):
        work[pl.ds(16 * p, 16), :] = left_r[p] + left_b[p]
    work2[pl.ds(0, 128), :] = dot(work[pl.ds(0, 128), :], mats[SUM])

    fr4, fb4 = pack(paired(8, 8), q8)
    r4 = [fr4[p] * k4[ID_R, p] for p in range(4)]
    b4 = half_small(BLACK, r4, fb4, k4, q8)

    def bottom(step, carry):
        black = list(carry[4:])
        red = half_small(RED, black, fr4, k4, q8)
        black = half_small(BLACK, red, fb4, k4, q8)
        return tuple(red + black)

    done = lax.fori_loop(0, 11, bottom, tuple(r4 + b4))
    e4 = unpacked(done[:4], done[4:], q8)

    def doubled(rows, size):
        total = 2 * size * len(rows)
        for m, value in enumerate(rows):
            work[pl.ds(2 * size * m, size, stride=2), :] = value
            work[pl.ds(2 * size * m + 1, size, stride=2), :] = value
        work2[pl.ds(0, total), :] = dot(work[pl.ds(0, total), :], mats[DOUBLE])
        return [work2[pl.ds(2 * size * m, 2 * size), :] for m in range(len(rows))]

    up3 = doubled(e4, 8)
    b3 = [b3[p] + up3[p] for p in range(8)]
    r3 = half_small(RED, b3, fr3, k3, q16)
    b3 = half_small(BLACK, r3, fb3, k3, q16)
    r3 = half_small(RED, b3, fr3, k3, q16)
    b3 = half_small(BLACK, r3, fb3, k3, q16)
    up2 = doubled(unpacked(r3, b3, q16), 16)
    for p in range(16):
        b2[p + 1] = b2[p + 1] + up2[p]

    half2(RED, b2, r2)
    half2(BLACK, r2, b2)
    half2(RED, b2, r2)
    half2(BLACK, r2, b2)

    for c in black1:
        c.wait()

    turn = (4 - 8 * gy) & 31
    for p in range(12):
        x = (p - 4 + 4 * gx) & 31
        red, black = r2[x // 2 + 1], b2[x // 2 + 1]
        lower = jnp.where((x & 1) == 0, 1, 0) == jnp.where(q_in, 1, 0)
        value = pltpu.roll(jnp.where(lower, red, black), turn, 0)[:16]
        work[pl.ds(32 * p, 16, stride=2), :] = value
        work[pl.ds(32 * p + 1, 16, stride=2), :] = value
    work2[pl.ds(0, 384), :] = dot(work[pl.ds(0, 384), :], mats[TO1])

    def lift1(p, carry):
        value = joined(v1[p], v1s_lo[p // 4], v1s_hi[p // 4], lax.rem(p, 4))
        b1[p + 1] = value + work2[pl.ds(pl.multiple_of(32 * p, 32), 32), :]
        return carry

    lax.fori_loop(0, 12, lift1, 0, unroll=4)
    half1(RED, b1, r1)
    half1(BLACK, r1, b1)
    half1(RED, b1, r1)
    half1(BLACK, r1, b1)

    for c in fine:
        c.wait()
    used = (lane32 < 72) | (lane32 >= 120)

    for p in range(14):
        x = p + 5
        red, black = r1[x // 2 + 1], b1[x // 2 + 1]
        value = jnp.where(q_in, red, black) if x % 2 == 0 else jnp.where(q_in, black, red)
        value = jnp.where(used, value, 0.0)[4:28]
        work[pl.ds(48 * p, 24, stride=2), :] = value
        work[pl.ds(48 * p + 1, 24, stride=2), :] = value
    work3[...] = dot(work[pl.ds(0, 672), :], qz0[...])

    def lift_halo(p, carry):
        at = p + 5
        group, m = at // 8, lax.rem(at, 8)
        merged = jnp.where(first48, us_lo[group], us_hi[group])
        beyond = pltpu.roll(merged, lax.rem(120 - 16 * m + 128, 128), 1)
        u1[p] = jnp.concatenate([u1[p, :, pl.ds(0, 128)], beyond], axis=1) + work3[pl.ds(pl.multiple_of(48 * p, 16), 48), :]
        return carry

    def own_black(p, carry):
        u1[p, pl.ds(8, 32), pl.ds(0, 128)] = b0[p, pl.ds(8, 32), pl.ds(0, 128)]
        return carry

    lax.fori_loop(3, 11, own_black, 0)
    lax.fori_loop(0, 14, lift_halo, 0, unroll=2)
    half0(RED, u1, r0, 0, 12)
    half0(BLACK, r0, b0, 0, 12)
    half0(RED, b0, r0, 1, 11)
    half0(BLACK, r0, b0, 1, 11)

    def finish(p, carry):
        red, black = resid0(p + 2)
        red, black = red[8:40, :128], black[8:40, :128]
        res[2 * p] = jnp.where(q_in, red, black)
        res[2 * p + 1] = jnp.where(q_in, black, red)
        red, black = r0[p + 3, pl.ds(8, 32), pl.ds(0, 128)], b0[p + 3, pl.ds(8, 32), pl.ds(0, 128)]
        sol[2 * p] = jnp.where(q_in, red, black)
        sol[2 * p + 1] = jnp.where(q_in, black, red)
        return carry

    lax.fori_loop(0, 8, finish, 0, unroll=2)


def on_device(right_side, initial, alpha, beta_x, beta_y, beta_z):
    block = jax.ShapeDtypeStruct(right_side.shape, F32)
    V = lambda *shape: pltpu.VMEM(shape, F32)
    D = lambda n: pltpu.SemaphoreType.DMA((n,))
    scratch = [
        V(5, 26, 32, 128), V(3, 16, 8, 128), V(3, 16, 8, 128), V(3, 25, 8, 128), V(3, 25, 8, 128),
        V(16, 32, 128), V(14, 48, 256),
        V(3, 2, 32, 128), V(3, 2, 32, 128), V(3, 4, 48, 128), V(3, 4, 48, 128),
        V(15, 12, 48, 256), V(2, 12, 48, 256), V(14, 48, 256), V(14, 48, 256), V(14, 48, 256),
        V(32, 128), V(3, 48, 128), V(3, 48, 128),
        V(2, 24, 32, 128), V(4, 16, 128), V(4, 3, 32, 128), V(4, 3, 32, 128), V(15, 12, 32, 128),
        V(24, 32, 128), V(16, 128), V(3, 32, 128), V(3, 32, 128),
        V(2, 12, 32, 128), V(14, 32, 128), V(14, 32, 128),
        V(12, 32, 128), V(16, 128), V(3, 32, 128), V(3, 32, 128),
        V(2, 4, 4, 4, 4, 8, 128), V(2, 64, 8, 128), V(4, 32, 32, 128), V(15, 16, 32, 128), V(2, 16, 32, 128),
        V(18, 32, 128), V(18, 32, 128), V(15, 8, 16, 128), V(15, 4, 8, 128),
        V(2048, 128), V(2048, 128), V(672, 256), pltpu.VMEM((5, 128, 128), jnp.bfloat16), pltpu.VMEM((128, 256), jnp.bfloat16),
        D(6), D(34), D(34), D(26), D(26), D(26), D(26), D(26), D(26), D(26), D(26),
        D(18), D(18), D(2), D(2), D(1), D(1),
    ]
    return pl.pallas_call(
        kernel,
        out_shape=(block, block),
        in_specs=[pl.BlockSpec(memory_space=pl.ANY)] * 6,
        out_specs=[pl.BlockSpec(memory_space=pltpu.VMEM)] * 2,
        scratch_shapes=scratch,
        compiler_params=pltpu.CompilerParams(collective_id=0, has_side_effects=True, vmem_limit_bytes=60 << 20),
    )(right_side, initial, alpha, beta_x, beta_y, beta_z)


def solution(mesh):
    spec = P("gx", "gy", "gz")
    return jax.shard_map(on_device, mesh=mesh, in_specs=(spec,) * 6, out_specs=(spec, spec), check_vma=False)
```

```python
import itertools

import jax
import jax.numpy as jnp
from jax import lax
from jax.experimental import pallas as pl
from jax.experimental.pallas import tpu as pltpu
from jax.sharding import PartitionSpec as P

MESH = pl.DeviceIdType.MESH
F32 = jnp.float32
GRID = (8, 4, 4)
OFFS = [o for o in itertools.product((-1, 0, 1), repeat=3) if o != (0, 0, 0)]
FLAT = sorted([o for o in OFFS if o[2] == 0], key=lambda o: (o[0] != 0, o[1] == 0))
TALL = [o for o in OFFS if o[2] != 0]
RED, BLACK = 0, 1
SAME, OTHER_R, YL_R, YH_R, ZL_R, ZH_R, ID_R, D_R, OTHER_B, YL_B, YH_B, ZL_B, ZH_B, ID_B, D_B = range(15)


def dot(a, pick):
    total = None
    for _ in range(3):
        term = a.astype(jnp.bfloat16)
        part = jnp.dot(term, pick, preferred_element_type=F32)
        total = part if total is None else total + part
        a = a - term.astype(F32)
    return total


def iota(shape, dim):
    return lax.broadcasted_iota(jnp.int32, shape, dim)


def checker(shape):
    return ((iota(shape, 0) + iota(shape, 1)) & 1) == 0


def roll(x, shift, axis):
    size = x.shape[axis]
    shift = shift % size
    return pltpu.roll(x, shift, axis) if shift else x


def couplings(even, odd, next_x, keep_x, keep_next, keep_y, keep_z, scale, q0):
    parts = []
    for alpha, low_x, low_y, low_z in (even, odd):
        low_y, low_z = scale * low_y, scale * low_z
        own_y, own_z = low_y * keep_y, low_z * keep_z
        high_y, high_z = roll(own_y, -1, 0), roll(own_z, -1, 1)
        parts.append((own_y, high_y, own_z, high_z, alpha + (low_y + high_y) + (low_z + high_z)))
    x_e, x_o = scale * even[1], scale * odd[1]
    x_n = scale * next_x * keep_next
    d_e = parts[0][4] + (x_e + x_o)
    d_o = parts[1][4] + (x_o + x_n)
    x_e = x_e * keep_x
    i_e, i_o = 1.0 / d_e, 1.0 / d_o
    red = [jnp.where(q0, x_e, x_n)] + [jnp.where(q0, parts[0][n], parts[1][n]) for n in range(4)]
    red += [jnp.where(q0, i_e, i_o), jnp.where(q0, d_e, d_o)]
    black = [jnp.where(q0, x_n, x_e)] + [jnp.where(q0, parts[1][n], parts[0][n]) for n in range(4)]
    black += [jnp.where(q0, i_o, i_e), jnp.where(q0, d_o, d_e)]
    return [x_o] + red + black


def gathered_sum(colour, here, below, above, source, coef, q0):
    if colour == RED:
        other, base = jnp.where(q0, below, above), OTHER_R
    else:
        other, base = jnp.where(q0, above, below), OTHER_B
    total = source + coef(SAME) * here + coef(base) * other
    total = total + (coef(base + 1) * roll(here, 1, 0) + coef(base + 2) * roll(here, -1, 0))
    return total + (coef(base + 3) * roll(here, 1, 1) + coef(base + 4) * roll(here, -1, 1))


def kernel(
    f_hbm, u_hbm, a_hbm, bx_hbm, by_hbm, bz_hbm, sol, res,
    e5, y_top, y_bot, y_lo, y_hi, u_in, u0, s_hi, s_lo, l_lo, l_hi, k0, g0, r0, b0, u1, us, us_lo, us_hi,
    e1, e1s_up, e1s_dn, e1s_lo, e1s_hi, k1, f1, f1s, f1s_lo, f1s_hi, g1, r1, b1, v1, v1s, v1s_lo, v1s_hi,
    ga, gb, w2, k2, g2, r2, b2, k3, k4, work, work2, work3, mats, qz0,
    in_sem, a_send, a_recv, b_send, b_recv, c_send, c_recv, d_send, d_recv, e_send, e_recv,
    h_send, h_recv, p_send, p_recv, i_send, i_recv,
):
    gx, gy, gz = lax.axis_index("gx"), lax.axis_index("gy"), lax.axis_index("gz")
    me = (gx, gy, gz)
    core = lax.rem(gx, 2)
    chip = ((gx // 2) * 4 + gy) * 4 + gz

    def nb(o):
        return tuple(lax.rem(me[d] + (o[d] + GRID[d]), GRID[d]) if o[d] else me[d] for d in range(3))

    partner = (gx + 1 - 2 * core, gy, gz)

    loads = [pltpu.make_async_copy(u_hbm, u_in, in_sem.at[5])]
    for n, ref in enumerate((f_hbm, a_hbm, bx_hbm, by_hbm, bz_hbm)):
        loads.append(pltpu.make_async_copy(ref, e5.at[n, pl.ds(4, 16)], in_sem.at[n]))
    for c in loads:
        c.start()

    def zero(ref, at):
        ref[at] = jnp.zeros(ref.shape[1:], F32)

    for ref in (u0, u1):
        zero(ref, 0)
        zero(ref, 13)
    barrier = pltpu.get_barrier_semaphore()

    turns = [[lax.rem(at + k, 4) for k in range(4)] for at in (gx // 2, gy, gz)]
    peers = sorted(itertools.product(range(4), repeat=3), key=lambda k: -sum(min(n, 4 - n) for n in k))[:-1]
    peers = [(turns[0][k[0]] * 2 + core, turns[1][k[1]], turns[2][k[2]]) for k in peers]
    for to in peers:
        pl.semaphore_signal(barrier, inc=1, device_id=to, device_id_type=MESH)
    for o in OFFS:
        if o[0]:
            pl.semaphore_signal(barrier, inc=1, device_id=nb(o), device_id_type=MESH)

    row, col = iota((128, 128), 0), iota((128, 128), 1)
    one = lambda cond: jnp.where(cond, 1.0, 0.0).astype(F32)
    SUM, EVEN, SUM32, DOUBLE, TO1 = range(5)
    mats[SUM] = one((row >> 1) == (col & 63)).astype(jnp.bfloat16)
    mats[EVEN] = one(row == 2 * (col & 63)).astype(jnp.bfloat16)
    mats[SUM32] = one((row >> 1) == (col & 31)).astype(jnp.bfloat16)
    mats[DOUBLE] = one(row == (col >> 1)).astype(jnp.bfloat16)
    z1 = jnp.where(col < 96, col, col - 128)
    mats[TO1] = one(row == (((z1 + 64 * gz) >> 1) & 127)).astype(jnp.bfloat16)
    wide_col, wide_row = iota((128, 256), 1), iota((128, 256), 0)
    z0 = jnp.where(wide_col < 192, wide_col, wide_col - 256)
    qz0[...] = one(wide_row == ((z0 >> 1) & 127)).astype(jnp.bfloat16)

    q_l0 = checker((48, 256))
    q_in = checker((32, 128))
    q16 = checker((16, 128))
    q8 = checker((8, 128))
    lane8 = iota((8, 128), 1)
    lane16 = iota((16, 128), 1)
    lane32 = iota((32, 128), 1)
    lane48 = iota((48, 128), 1)
    first16 = (lane32 & 15) < 8
    first48 = (lane48 & 15) < 8

    for ref, at in ((r0, 0), (r0, 13), (b0, 0), (b0, 13), (r1, 0), (r1, 13), (b1, 0), (b1, 13)):
        zero(ref, at)
    for ref in (r2, b2):
        zero(ref, 0)
        zero(ref, 17)

    for c in loads:
        c.wait()

    def take_black(p, carry):
        u0[4 + p - 1, pl.ds(8, 32), pl.ds(0, 128)] = jnp.where(q_in, u_in[2 * p + 1], u_in[2 * p])
        return carry

    lax.fori_loop(0, 8, take_black, 0, unroll=2)

    sub8 = iota((8, 128), 0) < 4
    y_lo[:, 24] = jnp.zeros((3, 8, 128), F32)
    y_hi[:, 24] = jnp.zeros((3, 8, 128), F32)

    def take_ends(x, carry):
        for t, (n, k) in enumerate(((0, 1), (2, 4))):
            y_top[t, x] = jnp.where(sub8, roll(e5[n, 4 + x, pl.ds(24, 8), :], 4, 0), e5[k, 4 + x, pl.ds(24, 8), :])
            y_bot[t, x] = jnp.where(sub8, e5[n, 4 + x, pl.ds(0, 8), :], roll(e5[k, 4 + x, pl.ds(0, 8), :], 4, 0))
        y_top[2, x] = e5[3, 4 + x, pl.ds(24, 8), :]
        y_bot[2, x] = e5[3, 4 + x, pl.ds(0, 8), :]
        return carry

    lax.fori_loop(0, 16, take_ends, 0, unroll=4)

    pl.semaphore_wait(barrier, 81)

    def remote(src, dst, send, recv, to):
        return pltpu.make_async_remote_copy(
            src_ref=src, dst_ref=dst, send_sem=send, recv_sem=recv, device_id=to, device_id_type=MESH
        )

    Y0 = {-1: (8, 40, 8), 0: (8, 8, 32), 1: (32, 0, 8)}
    X5 = {-1: (0, 20, 5), 1: (12, 0, 4)}
    XY = {-1: (0, 20, 4), 0: (0, 4, 16), 1: (12, 0, 4)}
    XE = {-1: (3, 11, 2), 1: (9, 1, 2)}
    XU = {-1: (3, 11, 3), 0: (3, 3, 8), 1: (8, 0, 3)}
    XS = {-1: (0, 3, 1), 0: (0, 1, 2), 1: (1, 0, 1)}
    YS = {-1: (0, 40, 8), 0: (0, 8, 32), 1: (24, 0, 8)}
    first = []
    for n, o in enumerate(FLAT):
        if o[1]:
            (xs, xd, xn), (src, dst) = XY[o[0]], (y_top, y_lo) if o[1] == 1 else (y_bot, y_hi)
        else:
            (xs, xd, xn), (src, dst) = X5[o[0]], (e5, e5)
            xs += 4
        first.append(remote(
            src.at[:, pl.ds(xs, xn)], dst.at[:, pl.ds(xd, xn)], a_send.at[18 + n], a_recv.at[18 + n], nb(o)
        ))
        (xs, xd, xn), (ys, yd, yn) = (XE if o[0] and o[1] else XU)[o[0]], Y0[o[1]]
        first.append(remote(
            u0.at[pl.ds(xs, xn), pl.ds(ys, yn), pl.ds(0, 128)], u0.at[pl.ds(xd, xn), pl.ds(yd, yn), pl.ds(0, 128)],
            a_send.at[26 + n], a_recv.at[26 + n], nb(o),
        ))
    for c in first:
        c.start()

    for half in range(2):
        for t, (one_n, two_n) in enumerate(((0, 1), (2, 3), (4, 5))):
            acc_a = jnp.zeros((32, 128), F32)
            acc_b = jnp.zeros((32, 128), F32)
            for m in range(8):
                at = 8 * half + m
                rolled = roll(e5[one_n, 4 + at], 16 * m + 8, 1)
                acc_a = jnp.where((lane32 >> 4) == m, rolled, acc_a)
                if two_n < 5:
                    rolled = roll(e5[two_n, 4 + at], 16 * m + 16, 1)
                elif m < 4:
                    rolled = roll(u0[3 + 4 * half + m, pl.ds(8, 32), pl.ds(0, 128)], 16 * m + 16, 1)
                else:
                    continue
                acc_b = jnp.where((((lane32 + 120) & 127) >> 4) == m, rolled, acc_b)
            s_hi[t, half] = jnp.where(first16, acc_a, acc_b)
            s_lo[t, half] = jnp.where(first16, acc_b, acc_a)

    beyond = []
    for n, o in enumerate(TALL):
        (xs, xd, xn), (ys, yd, yn) = XS[o[0]], YS[o[1]]
        src, dst = (s_hi, l_lo) if o[2] == 1 else (s_lo, l_hi)
        beyond.append(remote(
            src.at[:, pl.ds(xs, xn), pl.ds(ys, yn)], dst.at[:, pl.ds(xd, xn), pl.ds(yd, yn)],
            a_send.at[n], a_recv.at[n], nb(o),
        ))
    for c in beyond:
        c.start()
    first += beyond

    def coarsen(count, rows, read):
        size = count * rows
        for p in range(count):
            for n in range(4):
                even = read(n, 2 * p)
                work[pl.ds(n * size + p * rows, rows), :] = even if n == 1 else even + read(n, 2 * p + 1)
        work2[pl.ds(0, 3 * size), :] = dot(work[pl.ds(0, 3 * size), :], mats[SUM])
        work2[pl.ds(3 * size, size), :] = dot(work[pl.ds(3 * size, size), :], mats[EVEN])

        def result(n, p):
            at = n * size + p * rows
            low = work2[pl.ds(at, rows // 2, stride=2), :]
            if n == 2:
                return 0.25 * low
            return (0.125 if n == 0 else 0.25) * (low + work2[pl.ds(at + 1, rows // 2, stride=2), :])

        return result

    got = coarsen(8, 32, lambda n, x: e5[n + 1, 4 + x])
    first16b = (lane16 & 15) < 8
    for n in range(0, 4, 2):
        acc_a = jnp.zeros((16, 128), F32)
        acc_b = jnp.zeros((16, 128), F32)
        for m in range(8):
            one_v, two_v = got(n, m), got(n + 1, m)
            e1[n // 2, 8 + m, pl.ds(8, 16), :] = jnp.where(lane16 < 64, one_v, two_v)
            acc_a = jnp.where((lane16 >> 4) == m, roll(one_v, 16 * m + 8, 1), acc_a)
            acc_b = jnp.where((((lane16 + 120) & 127) >> 4) == m, roll(two_v, 16 * m + 16, 1), acc_b)
        e1s_up[n // 2] = jnp.where(first16b, acc_a, acc_b)
        e1s_dn[n // 2] = jnp.where(first16b, acc_b, acc_a)

    Y1 = {-1: (8, 24, 8), 0: (8, 8, 16), 1: (16, 0, 8)}
    YT = {-1: (0, 24, 8), 0: (0, 8, 16), 1: (8, 0, 8)}
    XT = {-1: 2, 0: 1, 1: 0}

    def spread1(main, to_high, to_low, low, high, send, recv, lead):
        out = []
        for n, o in enumerate(TALL):
            ys, yd, yn = YT[o[1]]
            dst, strip = (low, to_high) if o[2] == 1 else (high, to_low)
            src = strip.at[:, pl.ds(ys, yn)] if lead else strip.at[pl.ds(ys, yn)]
            dst = dst.at[:, XT[o[0]], pl.ds(yd, yn)] if lead else dst.at[XT[o[0]], pl.ds(yd, yn)]
            out.append(remote(src, dst, send.at[n], recv.at[n], nb(o)))
        for n, o in enumerate(FLAT):
            size = main.shape[1 if lead else 0] // 3
            (xs, xd, xn), (ys, yd, yn) = (size, size * (1 - o[0]), size), Y1[o[1]]
            src = (pl.ds(xs, xn), pl.ds(ys, yn))
            dst = (pl.ds(xd, xn), pl.ds(yd, yn))
            if lead:
                src, dst = (slice(None),) + src, (slice(None),) + dst
            out.append(remote(main.at[src], main.at[dst], send.at[18 + n], recv.at[18 + n], nb(o)))
        return out

    coefs1 = spread1(e1, e1s_up, e1s_dn, e1s_lo, e1s_hi, b_send, b_recv, True)
    for c in coefs1:
        c.start()

    def twice(n, value):
        other = roll(value, 64, 1)
        return jnp.where(lane16 < 64, other, value) if n % 2 else jnp.where(lane16 < 64, value, other)

    got = coarsen(4, 16, lambda n, x: twice(n, e1[n // 2, 8 + x, pl.ds(8, 16), :]))
    for n in range(4):
        acc = got(n, 0)
        for m in range(1, 4):
            acc = jnp.where((lane8 >> 5) == m, got(n, m), acc)
        ga[core, gx // 2, gy, gz, n] = acc

    def along(axis, k):
        if axis == "z":
            return lax.rem(gx + 2 * k, 8), gy, gz
        return (gx, lax.rem(gy + k, 4), gz) if axis == "y" else (gx, gy, lax.rem(gz + k, 4))

    def part(order, axis, back):
        z, y, x = gx // 2, gy, gz
        if axis == "z":
            z = lax.rem(z + 4 - back, 4)
        elif axis == "y":
            y = lax.rem(y + 4 - back, 4)
        else:
            x = lax.rem(x + 4 - back, 4)
        if order == "xyz":
            y, x = slice(None) if axis == "z" else y, x if axis == "x" else slice(None)
            return ga.at[core, z, y, x, pl.ds(0, 2)]
        z, y = slice(None) if axis == "x" else z, y if axis == "y" else slice(None)
        return ga.at[core, z, y, x, pl.ds(2, 2)]

    def legs(stage):
        for n, order in enumerate(("xyz", "yzx")):
            for k in range(1, 4):
                yield order, order[stage], k, 6 * stage + 3 * n + k - 1

    def pass_on(stage):
        for order, axis, k, at in legs(stage):
            own = part(order, axis, 0)
            remote(own, own, h_send.at[at], h_recv.at[at], along(axis, k)).start()

    def passed_on(stage):
        for order, axis, k, at in legs(stage):
            own, theirs = part(order, axis, 0), part(order, axis, k)
            remote(own, own, h_send.at[at], h_recv.at[at], along(axis, k)).wait_send()
            remote(theirs, theirs, h_send.at[at], h_recv.at[at], along(axis, k)).wait_recv()

    pass_on(0)
    passed_on(0)
    pass_on(1)

    for c in first:
        c.wait_recv()
    keep_y0 = one(((iota((48, 256), 0) - 8 + 32 * gy) & 127) != 0)
    lane256 = iota((48, 256), 1)
    keep_z0 = one(((jnp.where(lane256 < 192, lane256, lane256 - 256) + 128 * gz) & 511) != 0)

    def side(n, group, m):
        t, low, high = n // 2, l_lo, l_hi
        if n % 2:
            return pltpu.roll(jnp.where(first48, high[t, group], low[t, group]), lax.rem(112 - 16 * m + 128, 128), 1)
        return pltpu.roll(jnp.where(first48, low[t, group], high[t, group]), lax.rem(120 - 16 * m + 128, 128), 1)

    def fine_row(n, x):
        at = x + 4
        t, swap = ((0, 0), (0, 4), (1, 0), (2, 0), (1, 4))[n]
        low = y_lo[t, x] if swap or n == 3 else roll(y_lo[t, x], 4, 0)
        high = roll(y_hi[t, x], 4, 0) if swap else y_hi[t, x]
        main = jnp.concatenate([low, e5[n, x], high], axis=0)
        return jnp.concatenate([main, side(n, at // 8, lax.rem(at, 8))], axis=1)

    def build0(p, carry):
        e, o = 2 * p, 2 * p + 1
        even = tuple(fine_row(n, e) for n in range(1, 5))
        odd = tuple(fine_row(n, o) for n in range(1, 5))
        keep_e = jnp.where(((e - 4 + 16 * gx) & 127) == 0, 0.0, 1.0).astype(F32)
        keep_n = jnp.where(((e - 2 + 16 * gx) & 127) == 0, 0.0, 1.0).astype(F32)
        for n, value in enumerate(couplings(even, odd, fine_row(2, e + 2), keep_e, keep_n, keep_y0, keep_z0, 1.0, q_l0)):
            k0[n, p] = value
        f_e, f_o = fine_row(0, e), fine_row(0, o)
        g0[RED, p] = jnp.where(q_l0, f_e, f_o)
        g0[BLACK, p] = jnp.where(q_l0, f_o, f_e)
        return carry

    lax.fori_loop(0, 12, build0, 0, unroll=2)

    passed_on(1)
    pass_on(2)

    def side_u(p, carry):
        at = p + 1
        u0[p, :, pl.ds(128, 128)] = side(5, at // 4, lax.rem(at, 4))
        return carry

    lax.fori_loop(0, 14, side_u, 0, unroll=7)

    def half0(colour, src, dst, start, stop):
        def one_pair(p, carry):
            coef = lambda n: k0[n, p]
            total = gathered_sum(colour, src[p + 1], src[p], src[p + 2], g0[colour, p], coef, q_l0)
            dst[p + 1] = total * k0[ID_R if colour == RED else ID_B, p]
            return carry

        lax.fori_loop(start, stop, one_pair, 0, unroll=2)

    half0(RED, u0, r0, 0, 12)
    half0(BLACK, r0, b0, 0, 12)
    half0(RED, b0, r0, 1, 11)
    half0(BLACK, r0, b0, 1, 11)

    def resid0(p):
        coef = lambda n: k0[n, p]
        out = []
        for colour, own, far in ((RED, r0, b0), (BLACK, b0, r0)):
            total = gathered_sum(colour, far[p + 1], far[p], far[p + 2], g0[colour, p], coef, q_l0)
            out.append(total - k0[D_R if colour == RED else D_B, p] * own[p + 1])
        return out

    def restrict0(p, carry):
        red, black = resid0(p + 2)
        work[pl.ds(32 * p, 32), :] = (red + black)[8:40, :128]
        return carry

    lax.fori_loop(0, 8, restrict0, 0, unroll=2)
    work2[pl.ds(0, 256), :] = dot(work[pl.ds(0, 256), :], mats[SUM])
    acc = jnp.zeros((16, 128), F32)
    values = []
    for m in range(8):
        value = 0.125 * (work2[pl.ds(32 * m, 16, stride=2), :] + work2[pl.ds(32 * m + 1, 16, stride=2), :])
        values.append(value)
        if m >= 4:
            f1[m, pl.ds(8, 16), :] = jnp.where(lane16 < 64, values[m - 4], value)
        acc = jnp.where((lane16 >> 4) == m, roll(value, 16 * m + 8, 1), acc)
    f1s[...] = acc

    right1 = spread1(f1, f1s, f1s, f1s_lo, f1s_hi, c_send, c_recv, False)
    for c in right1:
        c.start()

    acc = jnp.zeros((32, 128), F32)
    for m in range(8):
        acc = jnp.where((lane32 >> 4) == m, roll(b0[3 + m, pl.ds(8, 32), pl.ds(0, 128)], 16 * m + 8, 1), acc)
    us[...] = acc
    YU = {-1: (0, 40, 8), 0: (0, 8, 32), 1: (24, 0, 8)}
    fine = []
    for n, o in enumerate(TALL):
        ys, yd, yn = YU[o[1]]
        dst = us_lo if o[2] == 1 else us_hi
        fine.append(remote(us.at[pl.ds(ys, yn)], dst.at[XT[o[0]], pl.ds(yd, yn)], d_send.at[n], d_recv.at[n], nb(o)))
    for n, o in enumerate(FLAT):
        (xs, xd, xn), (ys, yd, yn) = (XE if o[0] and o[1] else XU)[o[0]], Y0[o[1]]
        fine.append(remote(
            b0.at[pl.ds(xs, xn), pl.ds(ys, yn), pl.ds(0, 128)], u1.at[pl.ds(xd, xn), pl.ds(yd, yn), pl.ds(0, 128)],
            d_send.at[18 + n], d_recv.at[18 + n], nb(o),
        ))
    for c in fine:
        c.start()

    for c in first:
        c.wait_send()
    for c in coefs1:
        c.wait()
    keep_y1 = one(((iota((32, 128), 0) - 8 + 16 * gy) & 63) != 0)
    keep_z1 = one(((jnp.where(lane32 < 96, lane32, lane32 - 128) + 64 * gz) & 255) != 0)

    def joined(main, low, high, m, back=0):
        above = pltpu.roll(high, lax.rem(56 - back - 16 * m + 256, 128), 1)
        below = pltpu.roll(low, lax.rem(120 - back - 16 * m + 256, 128), 1)
        return jnp.where(lane32 < 64, main, jnp.where(lane32 < 96, above, below))

    def coarse_row(n, x):
        main = e1[n // 2, x]
        if n % 2:
            main = roll(main, 64, 1)
        return joined(main, e1s_lo[n // 2, x // 8], e1s_hi[n // 2, x // 8], lax.rem(x, 8), 8 * (n % 2))

    def build1(p, carry):
        e, o = 2 * p, 2 * p + 1
        even = tuple(coarse_row(n, e) for n in range(4))
        odd = tuple(coarse_row(n, o) for n in range(4))
        after = coarse_row(1, lax.rem(e + 2, 24))
        keep_e = jnp.where(((e - 8 + 8 * gx) & 63) == 0, 0.0, 1.0).astype(F32)
        keep_n = jnp.where(((e - 6 + 8 * gx) & 63) == 0, 0.0, 1.0).astype(F32)
        for n, value in enumerate(couplings(even, odd, after, keep_e, keep_n, keep_y1, keep_z1, 0.25, q_in)):
            k1[n, p] = value
        return carry

    lax.fori_loop(0, 12, build1, 0, unroll=2)

    passed_on(2)
    pair_a = remote(ga.at[core], ga.at[core], p_send.at[0], p_recv.at[0], partner)
    pair_a.start()

    for c in right1:
        c.wait_recv()

    def source1(p, carry):
        e, o = 2 * p, 2 * p + 1
        f_e, f_o = (
            joined(pltpu.roll(f1[(x // 8) * 4 + lax.rem(x, 4)], 64 * (lax.rem(x, 8) // 4), 1),
                   f1s_lo[x // 8], f1s_hi[x // 8], lax.rem(x, 8))
            for x in (e, o)
        )
        red = jnp.where(q_in, f_e, f_o)
        g1[RED, p] = red
        g1[BLACK, p] = jnp.where(q_in, f_o, f_e)
        r1[p + 1] = red * k1[ID_R, p]
        return carry

    lax.fori_loop(0, 12, source1, 0, unroll=4)

    def half1(colour, src, dst):
        def one_pair(p, carry):
            coef = lambda n: k1[n, p]
            total = gathered_sum(colour, src[p + 1], src[p], src[p + 2], g1[colour, p], coef, q_in)
            dst[p + 1] = total * k1[ID_R if colour == RED else ID_B, p]
            return carry

        lax.fori_loop(0, 12, one_pair, 0, unroll=6)

    half1(BLACK, r1, b1)
    half1(RED, b1, r1)
    half1(BLACK, r1, b1)
    for p in range(4):
        coef = lambda n: k1[n, p + 4]
        total = gathered_sum(RED, b1[p + 5], b1[p + 4], b1[p + 6], g1[RED, p + 4], coef, q_in) - k1[D_R, p + 4] * r1[p + 5]
        other = gathered_sum(BLACK, r1[p + 5], r1[p + 4], r1[p + 6], g1[BLACK, p + 4], coef, q_in)
        total = total + (other - k1[D_B, p + 4] * b1[p + 5])
        work[pl.ds(16 * p, 16), :] = jnp.where(lane16 < 64, total[8:24], 0.0)
    work2[pl.ds(0, 64), :] = dot(work[pl.ds(0, 64), :], mats[SUM32])
    acc = jnp.zeros((8, 128), F32)
    for m in range(4):
        value = 0.125 * (work2[pl.ds(16 * m, 8, stride=2), :] + work2[pl.ds(16 * m + 1, 8, stride=2), :])
        acc = jnp.where((lane8 >> 5) == m, value, acc)
    gb[core, chip] = acc

    for to in peers:
        remote(gb.at[core, chip], gb.at[core, chip], i_send.at[0], i_recv.at[0], to).start()

    acc = jnp.zeros((16, 128), F32)
    for m in range(4):
        value = b1[5 + m, pl.ds(8, 16), :]
        value = jnp.where(lane16 < 64, value, roll(value, 64, 1))
        acc = jnp.where((lane16 >> 4) == m, roll(value, 16 * m + 8, 1), acc)
        v1[4 + m, pl.ds(8, 16), :] = value
    v1s[...] = acc
    black1 = []
    for n, o in enumerate(TALL):
        ys, yd, yn = YT[o[1]]
        dst = v1s_lo if o[2] == 1 else v1s_hi
        black1.append(remote(v1s.at[pl.ds(ys, yn)], dst.at[XT[o[0]], pl.ds(yd, yn)], e_send.at[n], e_recv.at[n], nb(o)))
    for n, o in enumerate(FLAT):
        (xs, xd, xn), (ys, yd, yn) = {-1: (4, 8, 4), 0: (4, 4, 4), 1: (4, 0, 4)}[o[0]], Y1[o[1]]
        black1.append(remote(
            v1.at[pl.ds(xs, xn), pl.ds(ys, yn)], v1.at[pl.ds(xd, xn), pl.ds(yd, yn)],
            e_send.at[18 + n], e_recv.at[18 + n], nb(o),
        ))
    for c in black1:
        c.start()

    for c in right1:
        c.wait_send()

    pair_a.wait()

    def untile(tiles):
        out = []
        for m in range(4):
            total = tiles[0] if m == 0 else roll(tiles[0], -32 * m, 1)
            for k in range(1, 4):
                total = jnp.where((lane8 >> 5) == k, roll(tiles[k], 32 * (k - m), 1), total)
            out.append(total)
        return out

    def place(tiles_of, count):
        def one_block(t, carry):
            bx, by = t // 4, lax.rem(t, 4)
            rows = pl.ds(pl.multiple_of(8 * by, 8), 8)
            for n in range(count):
                for m, value in enumerate(untile([tiles_of(lax.rem(bx, 2), bx // 2, by, k, n) for k in range(4)])):
                    w2[n, 4 * bx + m, rows, :] = value
            return carry

        lax.fori_loop(0, 32, one_block, 0, unroll=4)

    place(lambda side_core, bz, by, k, n: ga[side_core, bz, by, k, n], 4)

    keep_y2 = one(iota((32, 128), 0) != 0)
    keep_z2 = one(lane32 != 0)

    def build2(p, carry):
        e, o = 2 * p, 2 * p + 1
        even = tuple(w2[n, e] for n in range(4))
        odd = tuple(w2[n, o] for n in range(4))
        keep_e = jnp.where(p == 0, 0.0, 1.0).astype(F32)
        keep_n = jnp.where(p == 15, 0.0, 1.0).astype(F32)
        after = w2[1, lax.rem(e + 2, 32)]
        for n, value in enumerate(couplings(even, odd, after, keep_e, keep_n, keep_y2, keep_z2, 0.25**2, q_in)):
            k2[n, p] = value
        return carry

    lax.fori_loop(0, 16, build2, 0, unroll=2)

    def small(level_coefs, count, rows, period, scale, q, dest):
        keep_y = one(iota((rows, 128), 0) != 0)
        keep_z = one((iota((rows, 128), 1) & (period - 1)) != 0)
        for p in range(count):
            even = tuple(level_coefs(n, 2 * p) for n in range(4))
            odd = tuple(level_coefs(n, 2 * p + 1) for n in range(4))
            after = level_coefs(1, (2 * p + 2) % (2 * count))
            for n, value in enumerate(couplings(
                even, odd, after, 0.0 if p == 0 else 1.0, 0.0 if p == count - 1 else 1.0, keep_y, keep_z, scale, q
            )):
                dest[n, p] = value

    got3 = coarsen(16, 32, lambda n, x: w2[n, x])
    rows3 = [[got3(n, x) for x in range(16)] for n in range(4)]
    for n in range(4):
        for x in range(16):
            w2[n, x, pl.ds(0, 16), :] = rows3[n][x]
    small(lambda n, x: w2[n, x, pl.ds(0, 16), :], 8, 16, 64, 0.25**3, q16, k3)
    got4 = coarsen(8, 16, lambda n, x: w2[n, x, pl.ds(0, 16), :])
    small(got4, 4, 8, 32, 0.25**4, q8, k4)

    others = gb.at[core, pl.ds(0, 63)]
    remote(others, others, i_send.at[0], i_recv.at[0], partner).wait()
    pair_b = remote(gb.at[core], gb.at[core], p_send.at[1], p_recv.at[1], partner)
    pair_b.start()
    pair_b.wait()

    place(lambda side_core, bz, by, k, n: gb[side_core, bz * 16 + by * 4 + k], 1)

    def source2(p, carry):
        f_e, f_o = w2[0, 2 * p], w2[0, 2 * p + 1]
        red = jnp.where(q_in, f_e, f_o)
        g2[RED, p] = red
        g2[BLACK, p] = jnp.where(q_in, f_o, f_e)
        r2[p + 1] = red * k2[ID_R, p]
        return carry

    lax.fori_loop(0, 16, source2, 0, unroll=2)

    def half2(colour, src, dst):
        def one_pair(p, carry):
            coef = lambda n: k2[n, p]
            total = gathered_sum(colour, src[p + 1], src[p], src[p + 2], g2[colour, p], coef, q_in)
            dst[p + 1] = total * k2[ID_R if colour == RED else ID_B, p]
            return carry

        lax.fori_loop(0, 16, one_pair, 0, unroll=8)

    half2(BLACK, r2, b2)
    half2(RED, b2, r2)
    half2(BLACK, r2, b2)

    def restrict2(p, carry):
        coef = lambda n: k2[n, p]
        total = gathered_sum(RED, b2[p + 1], b2[p], b2[p + 2], g2[RED, p], coef, q_in) - k2[D_R, p] * r2[p + 1]
        other = gathered_sum(BLACK, r2[p + 1], r2[p], r2[p + 2], g2[BLACK, p], coef, q_in)
        work[pl.ds(pl.multiple_of(32 * p, 32), 32), :] = total + (other - k2[D_B, p] * b2[p + 1])
        return carry

    lax.fori_loop(0, 16, restrict2, 0, unroll=4)
    work2[pl.ds(0, 512), :] = dot(work[pl.ds(0, 512), :], mats[SUM])

    def pack(rows, q):
        count = len(rows) // 2
        red = [jnp.where(q, rows[2 * p], rows[2 * p + 1]) for p in range(count)]
        black = [jnp.where(q, rows[2 * p + 1], rows[2 * p]) for p in range(count)]
        return red, black

    def half_small(colour, src, source, k, q, own=None):
        count = len(src)
        out = []
        for p in range(count):
            coef = lambda n: k[n, p]
            total = gathered_sum(colour, src[p], src[p - 1], src[(p + 1) % count], source[p], coef, q)
            if own is None:
                out.append(total * k[ID_R if colour == RED else ID_B, p])
            else:
                out.append(total - k[D_R if colour == RED else D_B, p] * own[p])
        return out

    def paired(count, rows):
        return [
            0.125 * (work2[pl.ds(2 * rows * m, rows, stride=2), :] + work2[pl.ds(2 * rows * m + 1, rows, stride=2), :])
            for m in range(count)
        ]

    def unpacked(red, black, q):
        out = []
        for r, b in zip(red, black):
            out += [jnp.where(q, r, b), jnp.where(q, b, r)]
        return out

    fr3, fb3 = pack(paired(16, 16), q16)
    r3 = [fr3[p] * k3[ID_R, p] for p in range(8)]
    b3 = half_small(BLACK, r3, fb3, k3, q16)
    r3 = half_small(RED, b3, fr3, k3, q16)
    b3 = half_small(BLACK, r3, fb3, k3, q16)
    left_r = half_small(RED, b3, fr3, k3, q16, r3)
    left_b = half_small(BLACK, r3, fb3, k3, q16, b3)
    for p in range(8):
        work[pl.ds(16 * p, 16), :] = left_r[p] + left_b[p]
    work2[pl.ds(0, 128), :] = dot(work[pl.ds(0, 128), :], mats[SUM])

    fr4, fb4 = pack(paired(8, 8), q8)
    r4 = [fr4[p] * k4[ID_R, p] for p in range(4)]
    b4 = half_small(BLACK, r4, fb4, k4, q8)

    def bottom(step, carry):
        black = list(carry[4:])
        red = half_small(RED, black, fr4, k4, q8)
        black = half_small(BLACK, red, fb4, k4, q8)
        return tuple(red + black)

    done = lax.fori_loop(0, 11, bottom, tuple(r4 + b4))
    e4 = unpacked(done[:4], done[4:], q8)

    def doubled(rows, size):
        total = 2 * size * len(rows)
        for m, value in enumerate(rows):
            work[pl.ds(2 * size * m, size, stride=2), :] = value
            work[pl.ds(2 * size * m + 1, size, stride=2), :] = value
        work2[pl.ds(0, total), :] = dot(work[pl.ds(0, total), :], mats[DOUBLE])
        return [work2[pl.ds(2 * size * m, 2 * size), :] for m in range(len(rows))]

    up3 = doubled(e4, 8)
    b3 = [b3[p] + up3[p] for p in range(8)]
    r3 = half_small(RED, b3, fr3, k3, q16)
    b3 = half_small(BLACK, r3, fb3, k3, q16)
    r3 = half_small(RED, b3, fr3, k3, q16)
    b3 = half_small(BLACK, r3, fb3, k3, q16)
    up2 = doubled(unpacked(r3, b3, q16), 16)
    for p in range(16):
        b2[p + 1] = b2[p + 1] + up2[p]

    half2(RED, b2, r2)
    half2(BLACK, r2, b2)
    half2(RED, b2, r2)
    half2(BLACK, r2, b2)

    for c in black1:
        c.wait()

    turn = (4 - 8 * gy) & 31
    for p in range(12):
        x = (p - 4 + 4 * gx) & 31
        red, black = r2[x // 2 + 1], b2[x // 2 + 1]
        lower = jnp.where((x & 1) == 0, 1, 0) == jnp.where(q_in, 1, 0)
        value = pltpu.roll(jnp.where(lower, red, black), turn, 0)[:16]
        work[pl.ds(32 * p, 16, stride=2), :] = value
        work[pl.ds(32 * p + 1, 16, stride=2), :] = value
    work2[pl.ds(0, 384), :] = dot(work[pl.ds(0, 384), :], mats[TO1])

    def lift1(p, carry):
        value = joined(v1[p], v1s_lo[p // 4], v1s_hi[p // 4], lax.rem(p, 4))
        b1[p + 1] = value + work2[pl.ds(pl.multiple_of(32 * p, 32), 32), :]
        return carry

    lax.fori_loop(0, 12, lift1, 0, unroll=4)
    half1(RED, b1, r1)
    half1(BLACK, r1, b1)
    half1(RED, b1, r1)
    half1(BLACK, r1, b1)

    for c in fine:
        c.wait()
    used = (lane32 < 72) | (lane32 >= 120)

    for p in range(14):
        x = p + 5
        red, black = r1[x // 2 + 1], b1[x // 2 + 1]
        value = jnp.where(q_in, red, black) if x % 2 == 0 else jnp.where(q_in, black, red)
        value = jnp.where(used, value, 0.0)[4:28]
        work[pl.ds(48 * p, 24, stride=2), :] = value
        work[pl.ds(48 * p + 1, 24, stride=2), :] = value
    work3[...] = dot(work[pl.ds(0, 672), :], qz0[...])

    def lift_halo(p, carry):
        at = p + 5
        group, m = at // 8, lax.rem(at, 8)
        merged = jnp.where(first48, us_lo[group], us_hi[group])
        beyond = pltpu.roll(merged, lax.rem(120 - 16 * m + 128, 128), 1)
        u1[p] = jnp.concatenate([u1[p, :, pl.ds(0, 128)], beyond], axis=1) + work3[pl.ds(pl.multiple_of(48 * p, 16), 48), :]
        return carry

    def own_black(p, carry):
        u1[p, pl.ds(8, 32), pl.ds(0, 128)] = b0[p, pl.ds(8, 32), pl.ds(0, 128)]
        return carry

    lax.fori_loop(3, 11, own_black, 0)
    lax.fori_loop(0, 14, lift_halo, 0, unroll=2)
    half0(RED, u1, r0, 0, 12)
    half0(BLACK, r0, b0, 0, 12)
    half0(RED, b0, r0, 1, 11)
    half0(BLACK, r0, b0, 1, 11)

    def finish(p, carry):
        red, black = resid0(p + 2)
        red, black = red[8:40, :128], black[8:40, :128]
        res[2 * p] = jnp.where(q_in, red, black)
        res[2 * p + 1] = jnp.where(q_in, black, red)
        red, black = r0[p + 3, pl.ds(8, 32), pl.ds(0, 128)], b0[p + 3, pl.ds(8, 32), pl.ds(0, 128)]
        sol[2 * p] = jnp.where(q_in, red, black)
        sol[2 * p + 1] = jnp.where(q_in, black, red)
        return carry

    lax.fori_loop(0, 8, finish, 0, unroll=2)


def on_device(right_side, initial, alpha, beta_x, beta_y, beta_z):
    block = jax.ShapeDtypeStruct(right_side.shape, F32)
    V = lambda *shape: pltpu.VMEM(shape, F32)
    D = lambda n: pltpu.SemaphoreType.DMA((n,))
    scratch = [
        V(5, 26, 32, 128), V(3, 16, 8, 128), V(3, 16, 8, 128), V(3, 25, 8, 128), V(3, 25, 8, 128),
        V(16, 32, 128), V(14, 48, 256),
        V(3, 2, 32, 128), V(3, 2, 32, 128), V(3, 4, 48, 128), V(3, 4, 48, 128),
        V(15, 12, 48, 256), V(2, 12, 48, 256), V(14, 48, 256), V(14, 48, 256), V(14, 48, 256),
        V(32, 128), V(3, 48, 128), V(3, 48, 128),
        V(2, 24, 32, 128), V(2, 16, 128), V(2, 16, 128), V(2, 3, 32, 128), V(2, 3, 32, 128), V(15, 12, 32, 128),
        V(12, 32, 128), V(16, 128), V(3, 32, 128), V(3, 32, 128),
        V(2, 12, 32, 128), V(14, 32, 128), V(14, 32, 128),
        V(12, 32, 128), V(16, 128), V(3, 32, 128), V(3, 32, 128),
        V(2, 4, 4, 4, 4, 8, 128), V(2, 64, 8, 128), V(4, 32, 32, 128), V(15, 16, 32, 128), V(2, 16, 32, 128),
        V(18, 32, 128), V(18, 32, 128), V(15, 8, 16, 128), V(15, 4, 8, 128),
        V(2048, 128), V(2048, 128), V(672, 256), pltpu.VMEM((5, 128, 128), jnp.bfloat16), pltpu.VMEM((128, 256), jnp.bfloat16),
        D(6), D(34), D(34), D(26), D(26), D(26), D(26), D(26), D(26), D(26), D(26),
        D(18), D(18), D(2), D(2), D(1), D(1),
    ]
    return pl.pallas_call(
        kernel,
        out_shape=(block, block),
        in_specs=[pl.BlockSpec(memory_space=pl.ANY)] * 6,
        out_specs=[pl.BlockSpec(memory_space=pltpu.VMEM)] * 2,
        scratch_shapes=scratch,
        compiler_params=pltpu.CompilerParams(collective_id=0, has_side_effects=True, vmem_limit_bytes=60 << 20),
    )(right_side, initial, alpha, beta_x, beta_y, beta_z)


def solution(mesh):
    spec = P("gx", "gy", "gz")
    return jax.shard_map(on_device, mesh=mesh, in_specs=(spec,) * 6, out_specs=(spec, spec), check_vma=False)
```

```python
import itertools

import jax
import jax.numpy as jnp
from jax import lax
from jax.experimental import pallas as pl
from jax.experimental.pallas import tpu as pltpu
from jax.sharding import PartitionSpec as P

MESH = pl.DeviceIdType.MESH
F32 = jnp.float32
GRID = (8, 4, 4)
OFFS = [o for o in itertools.product((-1, 0, 1), repeat=3) if o != (0, 0, 0)]
FLAT = sorted([o for o in OFFS if o[2] == 0], key=lambda o: (o[0] != 0, o[1] == 0))
TALL = [o for o in OFFS if o[2] != 0]
RED, BLACK = 0, 1
SAME, OTHER_R, YL_R, YH_R, ZL_R, ZH_R, ID_R, D_R, OTHER_B, YL_B, YH_B, ZL_B, ZH_B, ID_B, D_B = range(15)


def dot(a, pick):
    total = None
    for _ in range(3):
        term = a.astype(jnp.bfloat16)
        part = jnp.dot(term, pick, preferred_element_type=F32)
        total = part if total is None else total + part
        a = a - term.astype(F32)
    return total


def iota(shape, dim):
    return lax.broadcasted_iota(jnp.int32, shape, dim)


def checker(shape):
    return ((iota(shape, 0) + iota(shape, 1)) & 1) == 0


def roll(x, shift, axis):
    size = x.shape[axis]
    shift = shift % size
    return pltpu.roll(x, shift, axis) if shift else x


def couplings(even, odd, next_x, keep_x, keep_next, keep_y, keep_z, scale, q0):
    parts = []
    for alpha, low_x, low_y, low_z in (even, odd):
        low_y, low_z = scale * low_y, scale * low_z
        own_y, own_z = low_y * keep_y, low_z * keep_z
        high_y, high_z = roll(own_y, -1, 0), roll(own_z, -1, 1)
        parts.append((own_y, high_y, own_z, high_z, alpha + (low_y + high_y) + (low_z + high_z)))
    x_e, x_o = scale * even[1], scale * odd[1]
    x_n = scale * next_x * keep_next
    d_e = parts[0][4] + (x_e + x_o)
    d_o = parts[1][4] + (x_o + x_n)
    x_e = x_e * keep_x
    i_e, i_o = 1.0 / d_e, 1.0 / d_o
    red = [jnp.where(q0, x_e, x_n)] + [jnp.where(q0, parts[0][n], parts[1][n]) for n in range(4)]
    red += [jnp.where(q0, i_e, i_o), jnp.where(q0, d_e, d_o)]
    black = [jnp.where(q0, x_n, x_e)] + [jnp.where(q0, parts[1][n], parts[0][n]) for n in range(4)]
    black += [jnp.where(q0, i_o, i_e), jnp.where(q0, d_o, d_e)]
    return [x_o] + red + black


def gathered_sum(colour, here, below, above, source, coef, q0):
    if colour == RED:
        other, base = jnp.where(q0, below, above), OTHER_R
    else:
        other, base = jnp.where(q0, above, below), OTHER_B
    total = source + coef(SAME) * here + coef(base) * other
    total = total + (coef(base + 1) * roll(here, 1, 0) + coef(base + 2) * roll(here, -1, 0))
    return total + (coef(base + 3) * roll(here, 1, 1) + coef(base + 4) * roll(here, -1, 1))


def kernel(
    f_hbm, u_hbm, a_hbm, bx_hbm, by_hbm, bz_hbm, sol, res,
    e5, y_top, y_bot, y_lo, y_hi, u_in, u0, s_hi, s_lo, l_lo, l_hi, k0, g0, r0, b0, u1, us, us_lo, us_hi,
    e1, e1s_up, e1s_dn, e1s_lo, e1s_hi, k1, f1, f1s, f1s_lo, f1s_hi, g1, r1, b1, v1, v1s, v1s_lo, v1s_hi,
    ga, gb, w2, k2, g2, r2, b2, k3, k4, work, work2, work3, mats, qz0,
    in_sem, a_send, a_recv, b_send, b_recv, c_send, c_recv, d_send, d_recv, e_send, e_recv,
    h_send, h_recv, p_send, p_recv, i_send, i_recv,
):
    gx, gy, gz = lax.axis_index("gx"), lax.axis_index("gy"), lax.axis_index("gz")
    me = (gx, gy, gz)
    core = lax.rem(gx, 2)
    chip = ((gx // 2) * 4 + gy) * 4 + gz

    near = [[lax.rem(me[d] + (k + GRID[d]), GRID[d]) if k else me[d] for k in (-1, 0, 1)] for d in range(3)]

    def nb(o):
        return tuple(near[d][o[d] + 1] for d in range(3))

    partner = (gx + 1 - 2 * core, gy, gz)

    loads = [pltpu.make_async_copy(u_hbm, u_in, in_sem.at[5])]
    for n, ref in enumerate((f_hbm, a_hbm, bx_hbm, by_hbm, bz_hbm)):
        loads.append(pltpu.make_async_copy(ref, e5.at[n, pl.ds(4, 16)], in_sem.at[n]))
    for c in loads:
        c.start()

    def zero(ref, at):
        ref[at] = jnp.zeros(ref.shape[1:], F32)

    for ref in (u0, u1):
        zero(ref, 0)
        zero(ref, 13)
    barrier = pltpu.get_barrier_semaphore()

    turns = [[lax.rem(at + k, 4) for k in range(4)] for at in (gx // 2, gy, gz)]
    peers = sorted(itertools.product(range(4), repeat=3), key=lambda k: -sum(min(n, 4 - n) for n in k))[:-1]
    peers = [(turns[0][k[0]] * 2 + core, turns[1][k[1]], turns[2][k[2]]) for k in peers]
    for to in peers:
        pl.semaphore_signal(barrier, inc=1, device_id=to, device_id_type=MESH)
    for o in OFFS:
        if o[0]:
            pl.semaphore_signal(barrier, inc=1, device_id=nb(o), device_id_type=MESH)

    row, col = iota((128, 128), 0), iota((128, 128), 1)
    one = lambda cond: jnp.where(cond, 1.0, 0.0).astype(F32)
    SUM, EVEN, SUM32, DOUBLE, TO1 = range(5)
    mats[SUM] = one((row >> 1) == (col & 63)).astype(jnp.bfloat16)
    mats[EVEN] = one(row == 2 * (col & 63)).astype(jnp.bfloat16)
    mats[SUM32] = one((row >> 1) == (col & 31)).astype(jnp.bfloat16)
    mats[DOUBLE] = one(row == (col >> 1)).astype(jnp.bfloat16)
    z1 = jnp.where(col < 96, col, col - 128)
    mats[TO1] = one(row == (((z1 + 64 * gz) >> 1) & 127)).astype(jnp.bfloat16)
    wide_col, wide_row = iota((128, 256), 1), iota((128, 256), 0)
    z0 = jnp.where(wide_col < 192, wide_col, wide_col - 256)
    qz0[...] = one(wide_row == ((z0 >> 1) & 127)).astype(jnp.bfloat16)

    q_l0 = checker((48, 256))
    q_in = checker((32, 128))
    q16 = checker((16, 128))
    q8 = checker((8, 128))
    lane8 = iota((8, 128), 1)
    lane16 = iota((16, 128), 1)
    lane32 = iota((32, 128), 1)
    lane48 = iota((48, 128), 1)
    first16 = (lane32 & 15) < 8
    first48 = (lane48 & 15) < 8

    for ref, at in ((r0, 0), (r0, 13), (b0, 0), (b0, 13), (r1, 0), (r1, 13), (b1, 0), (b1, 13)):
        zero(ref, at)
    for ref in (r2, b2):
        zero(ref, 0)
        zero(ref, 17)

    for c in loads:
        c.wait()

    def take_black(p, carry):
        u0[4 + p - 1, pl.ds(8, 32), pl.ds(0, 128)] = jnp.where(q_in, u_in[2 * p + 1], u_in[2 * p])
        return carry

    lax.fori_loop(0, 8, take_black, 0, unroll=2)

    sub8 = iota((8, 128), 0) < 4
    y_lo[:, 24] = jnp.zeros((3, 8, 128), F32)
    y_hi[:, 24] = jnp.zeros((3, 8, 128), F32)

    def take_ends(x, carry):
        for t, (n, k) in enumerate(((0, 1), (2, 4))):
            y_top[t, x] = jnp.where(sub8, roll(e5[n, 4 + x, pl.ds(24, 8), :], 4, 0), e5[k, 4 + x, pl.ds(24, 8), :])
            y_bot[t, x] = jnp.where(sub8, e5[n, 4 + x, pl.ds(0, 8), :], roll(e5[k, 4 + x, pl.ds(0, 8), :], 4, 0))
        y_top[2, x] = e5[3, 4 + x, pl.ds(24, 8), :]
        y_bot[2, x] = e5[3, 4 + x, pl.ds(0, 8), :]
        return carry

    lax.fori_loop(0, 16, take_ends, 0, unroll=4)

    pl.semaphore_wait(barrier, 81)

    def remote(src, dst, send, recv, to):
        return pltpu.make_async_remote_copy(
            src_ref=src, dst_ref=dst, send_sem=send, recv_sem=recv, device_id=to, device_id_type=MESH
        )

    Y0 = {-1: (8, 40, 8), 0: (8, 8, 32), 1: (32, 0, 8)}
    X5 = {-1: (0, 20, 5), 1: (12, 0, 4)}
    XY = {-1: (0, 20, 4), 0: (0, 4, 16), 1: (12, 0, 4)}
    XE = {-1: (3, 11, 2), 1: (9, 1, 2)}
    XU = {-1: (3, 11, 3), 0: (3, 3, 8), 1: (8, 0, 3)}
    XS = {-1: (0, 3, 1), 0: (0, 1, 2), 1: (1, 0, 1)}
    YS = {-1: (0, 40, 8), 0: (0, 8, 32), 1: (24, 0, 8)}
    first = []
    for n, o in enumerate(FLAT):
        if o[1]:
            (xs, xd, xn), (src, dst) = XY[o[0]], (y_top, y_lo) if o[1] == 1 else (y_bot, y_hi)
        else:
            (xs, xd, xn), (src, dst) = X5[o[0]], (e5, e5)
            xs += 4
        first.append(remote(
            src.at[:, pl.ds(xs, xn)], dst.at[:, pl.ds(xd, xn)], a_send.at[18 + n], a_recv.at[18 + n], nb(o)
        ))
        (xs, xd, xn), (ys, yd, yn) = (XE if o[0] and o[1] else XU)[o[0]], Y0[o[1]]
        first.append(remote(
            u0.at[pl.ds(xs, xn), pl.ds(ys, yn), pl.ds(0, 128)], u0.at[pl.ds(xd, xn), pl.ds(yd, yn), pl.ds(0, 128)],
            a_send.at[26 + n], a_recv.at[26 + n], nb(o),
        ))
    for c in first:
        c.start()

    for half in range(2):
        for t, (one_n, two_n) in enumerate(((0, 1), (2, 3), (4, 5))):
            acc_a = jnp.zeros((32, 128), F32)
            acc_b = jnp.zeros((32, 128), F32)
            for m in range(8):
                at = 8 * half + m
                rolled = roll(e5[one_n, 4 + at], 16 * m + 8, 1)
                acc_a = jnp.where((lane32 >> 4) == m, rolled, acc_a)
                if two_n < 5:
                    rolled = roll(e5[two_n, 4 + at], 16 * m + 16, 1)
                elif m < 4:
                    rolled = roll(u0[3 + 4 * half + m, pl.ds(8, 32), pl.ds(0, 128)], 16 * m + 16, 1)
                else:
                    continue
                acc_b = jnp.where((((lane32 + 120) & 127) >> 4) == m, rolled, acc_b)
            s_hi[t, half] = jnp.where(first16, acc_a, acc_b)
            s_lo[t, half] = jnp.where(first16, acc_b, acc_a)

    beyond = []
    for n, o in enumerate(TALL):
        (xs, xd, xn), (ys, yd, yn) = XS[o[0]], YS[o[1]]
        src, dst = (s_hi, l_lo) if o[2] == 1 else (s_lo, l_hi)
        beyond.append(remote(
            src.at[:, pl.ds(xs, xn), pl.ds(ys, yn)], dst.at[:, pl.ds(xd, xn), pl.ds(yd, yn)],
            a_send.at[n], a_recv.at[n], nb(o),
        ))
    for c in beyond:
        c.start()
    first += beyond

    def coarsen(count, rows, read):
        size = count * rows
        for p in range(count):
            for n in range(4):
                even = read(n, 2 * p)
                work[pl.ds(n * size + p * rows, rows), :] = even if n == 1 else even + read(n, 2 * p + 1)
        work2[pl.ds(0, 3 * size), :] = dot(work[pl.ds(0, 3 * size), :], mats[SUM])
        work2[pl.ds(3 * size, size), :] = dot(work[pl.ds(3 * size, size), :], mats[EVEN])

        def result(n, p):
            at = n * size + p * rows
            low = work2[pl.ds(at, rows // 2, stride=2), :]
            if n == 2:
                return 0.25 * low
            return (0.125 if n == 0 else 0.25) * (low + work2[pl.ds(at + 1, rows // 2, stride=2), :])

        return result

    got = coarsen(8, 32, lambda n, x: e5[n + 1, 4 + x])
    first16b = (lane16 & 15) < 8
    for n in range(0, 4, 2):
        acc_a = jnp.zeros((16, 128), F32)
        acc_b = jnp.zeros((16, 128), F32)
        for m in range(8):
            one_v, two_v = got(n, m), got(n + 1, m)
            e1[n // 2, 8 + m, pl.ds(8, 16), :] = jnp.where(lane16 < 64, one_v, two_v)
            acc_a = jnp.where((lane16 >> 4) == m, roll(one_v, 16 * m + 8, 1), acc_a)
            acc_b = jnp.where((((lane16 + 120) & 127) >> 4) == m, roll(two_v, 16 * m + 16, 1), acc_b)
        e1s_up[n // 2] = jnp.where(first16b, acc_a, acc_b)
        e1s_dn[n // 2] = jnp.where(first16b, acc_b, acc_a)

    Y1 = {-1: (8, 24, 8), 0: (8, 8, 16), 1: (16, 0, 8)}
    YT = {-1: (0, 24, 8), 0: (0, 8, 16), 1: (8, 0, 8)}
    XT = {-1: 2, 0: 1, 1: 0}

    def spread1(main, to_high, to_low, low, high, send, recv, lead):
        out = []
        for n, o in enumerate(TALL):
            ys, yd, yn = YT[o[1]]
            dst, strip = (low, to_high) if o[2] == 1 else (high, to_low)
            src = strip.at[:, pl.ds(ys, yn)] if lead else strip.at[pl.ds(ys, yn)]
            dst = dst.at[:, XT[o[0]], pl.ds(yd, yn)] if lead else dst.at[XT[o[0]], pl.ds(yd, yn)]
            out.append(remote(src, dst, send.at[n], recv.at[n], nb(o)))
        for n, o in enumerate(FLAT):
            size = main.shape[1 if lead else 0] // 3
            (xs, xd, xn), (ys, yd, yn) = (size, size * (1 - o[0]), size), Y1[o[1]]
            src = (pl.ds(xs, xn), pl.ds(ys, yn))
            dst = (pl.ds(xd, xn), pl.ds(yd, yn))
            if lead:
                src, dst = (slice(None),) + src, (slice(None),) + dst
            out.append(remote(main.at[src], main.at[dst], send.at[18 + n], recv.at[18 + n], nb(o)))
        return out

    coefs1 = spread1(e1, e1s_up, e1s_dn, e1s_lo, e1s_hi, b_send, b_recv, True)
    for c in coefs1:
        c.start()

    def twice(n, value):
        other = roll(value, 64, 1)
        return jnp.where(lane16 < 64, other, value) if n % 2 else jnp.where(lane16 < 64, value, other)

    got = coarsen(4, 16, lambda n, x: twice(n, e1[n // 2, 8 + x, pl.ds(8, 16), :]))
    for n in range(4):
        acc = got(n, 0)
        for m in range(1, 4):
            acc = jnp.where((lane8 >> 5) == m, got(n, m), acc)
        ga[core, gx // 2, gy, gz, n] = acc

    def along(axis, k):
        if axis == "z":
            return lax.rem(gx + 2 * k, 8), gy, gz
        return (gx, lax.rem(gy + k, 4), gz) if axis == "y" else (gx, gy, lax.rem(gz + k, 4))

    def part(order, axis, back):
        z, y, x = gx // 2, gy, gz
        if axis == "z":
            z = lax.rem(z + 4 - back, 4)
        elif axis == "y":
            y = lax.rem(y + 4 - back, 4)
        else:
            x = lax.rem(x + 4 - back, 4)
        if order == "xyz":
            y, x = slice(None) if axis == "z" else y, x if axis == "x" else slice(None)
            return ga.at[core, z, y, x, pl.ds(0, 2)]
        z, y = slice(None) if axis == "x" else z, y if axis == "y" else slice(None)
        return ga.at[core, z, y, x, pl.ds(2, 2)]

    def legs(stage):
        for n, order in enumerate(("xyz", "yzx")):
            for k in range(1, 4):
                yield order, order[stage], k, 6 * stage + 3 * n + k - 1

    def pass_on(stage):
        for order, axis, k, at in legs(stage):
            own = part(order, axis, 0)
            remote(own, own, h_send.at[at], h_recv.at[at], along(axis, k)).start()

    def passed_on(stage):
        for order, axis, k, at in legs(stage):
            own, theirs = part(order, axis, 0), part(order, axis, k)
            remote(own, own, h_send.at[at], h_recv.at[at], along(axis, k)).wait_send()
            remote(theirs, theirs, h_send.at[at], h_recv.at[at], along(axis, k)).wait_recv()

    pass_on(0)
    passed_on(0)
    pass_on(1)

    for c in first:
        c.wait_recv()
    keep_y0 = one(((iota((48, 256), 0) - 8 + 32 * gy) & 127) != 0)
    lane256 = iota((48, 256), 1)
    keep_z0 = one(((jnp.where(lane256 < 192, lane256, lane256 - 256) + 128 * gz) & 511) != 0)

    def side(n, group, m):
        t, low, high = n // 2, l_lo, l_hi
        if n % 2:
            return pltpu.roll(jnp.where(first48, high[t, group], low[t, group]), lax.rem(112 - 16 * m + 128, 128), 1)
        return pltpu.roll(jnp.where(first48, low[t, group], high[t, group]), lax.rem(120 - 16 * m + 128, 128), 1)

    def fine_row(n, x):
        at = x + 4
        t, swap = ((0, 0), (0, 4), (1, 0), (2, 0), (1, 4))[n]
        low = y_lo[t, x] if swap or n == 3 else roll(y_lo[t, x], 4, 0)
        high = roll(y_hi[t, x], 4, 0) if swap else y_hi[t, x]
        main = jnp.concatenate([low, e5[n, x], high], axis=0)
        return jnp.concatenate([main, side(n, at // 8, lax.rem(at, 8))], axis=1)

    def build0(p, carry):
        e, o = 2 * p, 2 * p + 1
        even = tuple(fine_row(n, e) for n in range(1, 5))
        odd = tuple(fine_row(n, o) for n in range(1, 5))
        keep_e = jnp.where(((e - 4 + 16 * gx) & 127) == 0, 0.0, 1.0).astype(F32)
        keep_n = jnp.where(((e - 2 + 16 * gx) & 127) == 0, 0.0, 1.0).astype(F32)
        for n, value in enumerate(couplings(even, odd, fine_row(2, e + 2), keep_e, keep_n, keep_y0, keep_z0, 1.0, q_l0)):
            k0[n, p] = value
        f_e, f_o = fine_row(0, e), fine_row(0, o)
        g0[RED, p] = jnp.where(q_l0, f_e, f_o)
        g0[BLACK, p] = jnp.where(q_l0, f_o, f_e)
        return carry

    lax.fori_loop(0, 12, build0, 0, unroll=2)

    passed_on(1)
    pass_on(2)

    def side_u(p, carry):
        at = p + 1
        u0[p, :, pl.ds(128, 128)] = side(5, at // 4, lax.rem(at, 4))
        return carry

    lax.fori_loop(0, 14, side_u, 0, unroll=7)

    def half0(colour, src, dst, start, stop):
        def one_pair(p, carry):
            coef = lambda n: k0[n, p]
            total = gathered_sum(colour, src[p + 1], src[p], src[p + 2], g0[colour, p], coef, q_l0)
            dst[p + 1] = total * k0[ID_R if colour == RED else ID_B, p]
            return carry

        lax.fori_loop(start, stop, one_pair, 0, unroll=4)

    half0(RED, u0, r0, 0, 12)
    half0(BLACK, r0, b0, 0, 12)
    half0(RED, b0, r0, 1, 11)
    half0(BLACK, r0, b0, 1, 11)

    def resid0(p):
        coef = lambda n: k0[n, p]
        out = []
        for colour, own, far in ((RED, r0, b0), (BLACK, b0, r0)):
            total = gathered_sum(colour, far[p + 1], far[p], far[p + 2], g0[colour, p], coef, q_l0)
            out.append(total - k0[D_R if colour == RED else D_B, p] * own[p + 1])
        return out

    def restrict0(p, carry):
        red, black = resid0(p + 2)
        work[pl.ds(32 * p, 32), :] = (red + black)[8:40, :128]
        return carry

    lax.fori_loop(0, 8, restrict0, 0, unroll=4)
    work2[pl.ds(0, 256), :] = dot(work[pl.ds(0, 256), :], mats[SUM])
    acc = jnp.zeros((16, 128), F32)
    values = []
    for m in range(8):
        value = 0.125 * (work2[pl.ds(32 * m, 16, stride=2), :] + work2[pl.ds(32 * m + 1, 16, stride=2), :])
        values.append(value)
        if m >= 4:
            f1[m, pl.ds(8, 16), :] = jnp.where(lane16 < 64, values[m - 4], value)
        acc = jnp.where((lane16 >> 4) == m, roll(value, 16 * m + 8, 1), acc)
    f1s[...] = acc

    right1 = spread1(f1, f1s, f1s, f1s_lo, f1s_hi, c_send, c_recv, False)
    for c in right1:
        c.start()

    acc = jnp.zeros((32, 128), F32)
    for m in range(8):
        acc = jnp.where((lane32 >> 4) == m, roll(b0[3 + m, pl.ds(8, 32), pl.ds(0, 128)], 16 * m + 8, 1), acc)
    us[...] = acc
    YU = {-1: (0, 40, 8), 0: (0, 8, 32), 1: (24, 0, 8)}
    fine = []
    for n, o in enumerate(TALL):
        ys, yd, yn = YU[o[1]]
        dst = us_lo if o[2] == 1 else us_hi
        fine.append(remote(us.at[pl.ds(ys, yn)], dst.at[XT[o[0]], pl.ds(yd, yn)], d_send.at[n], d_recv.at[n], nb(o)))
    for n, o in enumerate(FLAT):
        (xs, xd, xn), (ys, yd, yn) = (XE if o[0] and o[1] else XU)[o[0]], Y0[o[1]]
        fine.append(remote(
            b0.at[pl.ds(xs, xn), pl.ds(ys, yn), pl.ds(0, 128)], u1.at[pl.ds(xd, xn), pl.ds(yd, yn), pl.ds(0, 128)],
            d_send.at[18 + n], d_recv.at[18 + n], nb(o),
        ))
    for c in fine:
        c.start()

    for c in first:
        c.wait_send()
    for c in coefs1:
        c.wait()
    keep_y1 = one(((iota((32, 128), 0) - 8 + 16 * gy) & 63) != 0)
    keep_z1 = one(((jnp.where(lane32 < 96, lane32, lane32 - 128) + 64 * gz) & 255) != 0)

    def joined(main, low, high, m, back=0):
        above = pltpu.roll(high, lax.rem(56 - back - 16 * m + 256, 128), 1)
        below = pltpu.roll(low, lax.rem(120 - back - 16 * m + 256, 128), 1)
        return jnp.where(lane32 < 64, main, jnp.where(lane32 < 96, above, below))

    def coarse_row(n, x):
        main = e1[n // 2, x]
        if n % 2:
            main = roll(main, 64, 1)
        return joined(main, e1s_lo[n // 2, x // 8], e1s_hi[n // 2, x // 8], lax.rem(x, 8), 8 * (n % 2))

    def build1(p, carry):
        e, o = 2 * p, 2 * p + 1
        even = tuple(coarse_row(n, e) for n in range(4))
        odd = tuple(coarse_row(n, o) for n in range(4))
        after = coarse_row(1, lax.rem(e + 2, 24))
        keep_e = jnp.where(((e - 8 + 8 * gx) & 63) == 0, 0.0, 1.0).astype(F32)
        keep_n = jnp.where(((e - 6 + 8 * gx) & 63) == 0, 0.0, 1.0).astype(F32)
        for n, value in enumerate(couplings(even, odd, after, keep_e, keep_n, keep_y1, keep_z1, 0.25, q_in)):
            k1[n, p] = value
        return carry

    lax.fori_loop(0, 12, build1, 0, unroll=2)

    passed_on(2)
    pair_a = remote(ga.at[core], ga.at[core], p_send.at[0], p_recv.at[0], partner)
    pair_a.start()

    for c in right1:
        c.wait_recv()

    def source1(p, carry):
        e, o = 2 * p, 2 * p + 1
        f_e, f_o = (
            joined(pltpu.roll(f1[(x // 8) * 4 + lax.rem(x, 4)], 64 * (lax.rem(x, 8) // 4), 1),
                   f1s_lo[x // 8], f1s_hi[x // 8], lax.rem(x, 8))
            for x in (e, o)
        )
        red = jnp.where(q_in, f_e, f_o)
        g1[RED, p] = red
        g1[BLACK, p] = jnp.where(q_in, f_o, f_e)
        r1[p + 1] = red * k1[ID_R, p]
        return carry

    lax.fori_loop(0, 12, source1, 0, unroll=4)

    def half1(colour, src, dst):
        def one_pair(p, carry):
            coef = lambda n: k1[n, p]
            total = gathered_sum(colour, src[p + 1], src[p], src[p + 2], g1[colour, p], coef, q_in)
            dst[p + 1] = total * k1[ID_R if colour == RED else ID_B, p]
            return carry

        lax.fori_loop(0, 12, one_pair, 0, unroll=12)

    half1(BLACK, r1, b1)
    half1(RED, b1, r1)
    half1(BLACK, r1, b1)
    for p in range(4):
        coef = lambda n: k1[n, p + 4]
        total = gathered_sum(RED, b1[p + 5], b1[p + 4], b1[p + 6], g1[RED, p + 4], coef, q_in) - k1[D_R, p + 4] * r1[p + 5]
        other = gathered_sum(BLACK, r1[p + 5], r1[p + 4], r1[p + 6], g1[BLACK, p + 4], coef, q_in)
        total = total + (other - k1[D_B, p + 4] * b1[p + 5])
        work[pl.ds(16 * p, 16), :] = jnp.where(lane16 < 64, total[8:24], 0.0)
    work2[pl.ds(0, 64), :] = dot(work[pl.ds(0, 64), :], mats[SUM32])
    acc = jnp.zeros((8, 128), F32)
    for m in range(4):
        value = 0.125 * (work2[pl.ds(16 * m, 8, stride=2), :] + work2[pl.ds(16 * m + 1, 8, stride=2), :])
        acc = jnp.where((lane8 >> 5) == m, value, acc)
    gb[core, chip] = acc

    for to in peers:
        remote(gb.at[core, chip], gb.at[core, chip], i_send.at[0], i_recv.at[0], to).start()

    acc = jnp.zeros((16, 128), F32)
    for m in range(4):
        value = b1[5 + m, pl.ds(8, 16), :]
        value = jnp.where(lane16 < 64, value, roll(value, 64, 1))
        acc = jnp.where((lane16 >> 4) == m, roll(value, 16 * m + 8, 1), acc)
        v1[4 + m, pl.ds(8, 16), :] = value
    v1s[...] = acc
    black1 = []
    for n, o in enumerate(TALL):
        ys, yd, yn = YT[o[1]]
        dst = v1s_lo if o[2] == 1 else v1s_hi
        black1.append(remote(v1s.at[pl.ds(ys, yn)], dst.at[XT[o[0]], pl.ds(yd, yn)], e_send.at[n], e_recv.at[n], nb(o)))
    for n, o in enumerate(FLAT):
        (xs, xd, xn), (ys, yd, yn) = {-1: (4, 8, 4), 0: (4, 4, 4), 1: (4, 0, 4)}[o[0]], Y1[o[1]]
        black1.append(remote(
            v1.at[pl.ds(xs, xn), pl.ds(ys, yn)], v1.at[pl.ds(xd, xn), pl.ds(yd, yn)],
            e_send.at[18 + n], e_recv.at[18 + n], nb(o),
        ))
    for c in black1:
        c.start()

    for c in right1:
        c.wait_send()

    pair_a.wait()

    def untile(tiles):
        out = []
        for m in range(4):
            total = tiles[0] if m == 0 else roll(tiles[0], -32 * m, 1)
            for k in range(1, 4):
                total = jnp.where((lane8 >> 5) == k, roll(tiles[k], 32 * (k - m), 1), total)
            out.append(total)
        return out

    def place(tiles_of, count):
        def one_block(t, carry):
            bx, by = t // 4, lax.rem(t, 4)
            rows = pl.ds(pl.multiple_of(8 * by, 8), 8)
            for n in range(count):
                for m, value in enumerate(untile([tiles_of(lax.rem(bx, 2), bx // 2, by, k, n) for k in range(4)])):
                    w2[n, 4 * bx + m, rows, :] = value
            return carry

        lax.fori_loop(0, 32, one_block, 0, unroll=4)

    place(lambda side_core, bz, by, k, n: ga[side_core, bz, by, k, n], 4)

    keep_y2 = one(iota((32, 128), 0) != 0)
    keep_z2 = one(lane32 != 0)

    def build2(p, carry):
        e, o = 2 * p, 2 * p + 1
        even = tuple(w2[n, e] for n in range(4))
        odd = tuple(w2[n, o] for n in range(4))
        keep_e = jnp.where(p == 0, 0.0, 1.0).astype(F32)
        keep_n = jnp.where(p == 15, 0.0, 1.0).astype(F32)
        after = w2[1, lax.rem(e + 2, 32)]
        for n, value in enumerate(couplings(even, odd, after, keep_e, keep_n, keep_y2, keep_z2, 0.25**2, q_in)):
            k2[n, p] = value
        return carry

    lax.fori_loop(0, 16, build2, 0, unroll=2)

    def small(level_coefs, count, rows, period, scale, q, dest):
        keep_y = one(iota((rows, 128), 0) != 0)
        keep_z = one((iota((rows, 128), 1) & (period - 1)) != 0)
        for p in range(count):
            even = tuple(level_coefs(n, 2 * p) for n in range(4))
            odd = tuple(level_coefs(n, 2 * p + 1) for n in range(4))
            after = level_coefs(1, (2 * p + 2) % (2 * count))
            for n, value in enumerate(couplings(
                even, odd, after, 0.0 if p == 0 else 1.0, 0.0 if p == count - 1 else 1.0, keep_y, keep_z, scale, q
            )):
                dest[n, p] = value

    got3 = coarsen(16, 32, lambda n, x: w2[n, x])
    rows3 = [[got3(n, x) for x in range(16)] for n in range(4)]
    for n in range(4):
        for x in range(16):
            w2[n, x, pl.ds(0, 16), :] = rows3[n][x]
    small(lambda n, x: w2[n, x, pl.ds(0, 16), :], 8, 16, 64, 0.25**3, q16, k3)
    got4 = coarsen(8, 16, lambda n, x: w2[n, x, pl.ds(0, 16), :])
    small(got4, 4, 8, 32, 0.25**4, q8, k4)

    others = gb.at[core, pl.ds(0, 63)]
    remote(others, others, i_send.at[0], i_recv.at[0], partner).wait()
    pair_b = remote(gb.at[core], gb.at[core], p_send.at[1], p_recv.at[1], partner)
    pair_b.start()
    pair_b.wait()

    place(lambda side_core, bz, by, k, n: gb[side_core, bz * 16 + by * 4 + k], 1)

    def source2(p, carry):
        f_e, f_o = w2[0, 2 * p], w2[0, 2 * p + 1]
        red = jnp.where(q_in, f_e, f_o)
        g2[RED, p] = red
        g2[BLACK, p] = jnp.where(q_in, f_o, f_e)
        r2[p + 1] = red * k2[ID_R, p]
        return carry

    lax.fori_loop(0, 16, source2, 0, unroll=2)

    def half2(colour, src, dst):
        def one_pair(p, carry):
            coef = lambda n: k2[n, p]
            total = gathered_sum(colour, src[p + 1], src[p], src[p + 2], g2[colour, p], coef, q_in)
            dst[p + 1] = total * k2[ID_R if colour == RED else ID_B, p]
            return carry

        lax.fori_loop(0, 16, one_pair, 0, unroll=16)

    half2(BLACK, r2, b2)
    half2(RED, b2, r2)
    half2(BLACK, r2, b2)

    def restrict2(p, carry):
        coef = lambda n: k2[n, p]
        total = gathered_sum(RED, b2[p + 1], b2[p], b2[p + 2], g2[RED, p], coef, q_in) - k2[D_R, p] * r2[p + 1]
        other = gathered_sum(BLACK, r2[p + 1], r2[p], r2[p + 2], g2[BLACK, p], coef, q_in)
        work[pl.ds(pl.multiple_of(32 * p, 32), 32), :] = total + (other - k2[D_B, p] * b2[p + 1])
        return carry

    lax.fori_loop(0, 16, restrict2, 0, unroll=4)
    work2[pl.ds(0, 512), :] = dot(work[pl.ds(0, 512), :], mats[SUM])

    def pack(rows, q):
        count = len(rows) // 2
        red = [jnp.where(q, rows[2 * p], rows[2 * p + 1]) for p in range(count)]
        black = [jnp.where(q, rows[2 * p + 1], rows[2 * p]) for p in range(count)]
        return red, black

    def half_small(colour, src, source, k, q, own=None):
        count = len(src)
        out = []
        for p in range(count):
            coef = lambda n: k[n, p]
            total = gathered_sum(colour, src[p], src[p - 1], src[(p + 1) % count], source[p], coef, q)
            if own is None:
                out.append(total * k[ID_R if colour == RED else ID_B, p])
            else:
                out.append(total - k[D_R if colour == RED else D_B, p] * own[p])
        return out

    def paired(count, rows):
        return [
            0.125 * (work2[pl.ds(2 * rows * m, rows, stride=2), :] + work2[pl.ds(2 * rows * m + 1, rows, stride=2), :])
            for m in range(count)
        ]

    def unpacked(red, black, q):
        out = []
        for r, b in zip(red, black):
            out += [jnp.where(q, r, b), jnp.where(q, b, r)]
        return out

    fr3, fb3 = pack(paired(16, 16), q16)
    r3 = [fr3[p] * k3[ID_R, p] for p in range(8)]
    b3 = half_small(BLACK, r3, fb3, k3, q16)
    r3 = half_small(RED, b3, fr3, k3, q16)
    b3 = half_small(BLACK, r3, fb3, k3, q16)
    left_r = half_small(RED, b3, fr3, k3, q16, r3)
    left_b = half_small(BLACK, r3, fb3, k3, q16, b3)
    for p in range(8):
        work[pl.ds(16 * p, 16), :] = left_r[p] + left_b[p]
    work2[pl.ds(0, 128), :] = dot(work[pl.ds(0, 128), :], mats[SUM])

    fr4, fb4 = pack(paired(8, 8), q8)
    r4 = [fr4[p] * k4[ID_R, p] for p in range(4)]
    b4 = half_small(BLACK, r4, fb4, k4, q8)

    def bottom(step, carry):
        black = list(carry[4:])
        red = half_small(RED, black, fr4, k4, q8)
        black = half_small(BLACK, red, fb4, k4, q8)
        return tuple(red + black)

    done = lax.fori_loop(0, 11, bottom, tuple(r4 + b4), unroll=11)
    e4 = unpacked(done[:4], done[4:], q8)

    def doubled(rows, size):
        total = 2 * size * len(rows)
        for m, value in enumerate(rows):
            work[pl.ds(2 * size * m, size, stride=2), :] = value
            work[pl.ds(2 * size * m + 1, size, stride=2), :] = value
        work2[pl.ds(0, total), :] = dot(work[pl.ds(0, total), :], mats[DOUBLE])
        return [work2[pl.ds(2 * size * m, 2 * size), :] for m in range(len(rows))]

    up3 = doubled(e4, 8)
    b3 = [b3[p] + up3[p] for p in range(8)]
    r3 = half_small(RED, b3, fr3, k3, q16)
    b3 = half_small(BLACK, r3, fb3, k3, q16)
    r3 = half_small(RED, b3, fr3, k3, q16)
    b3 = half_small(BLACK, r3, fb3, k3, q16)
    up2 = doubled(unpacked(r3, b3, q16), 16)
    for p in range(16):
        b2[p + 1] = b2[p + 1] + up2[p]

    half2(RED, b2, r2)
    half2(BLACK, r2, b2)
    half2(RED, b2, r2)
    half2(BLACK, r2, b2)

    for c in black1:
        c.wait()

    turn = (4 - 8 * gy) & 31
    for p in range(12):
        x = (p - 4 + 4 * gx) & 31
        red, black = r2[x // 2 + 1], b2[x // 2 + 1]
        lower = jnp.where((x & 1) == 0, 1, 0) == jnp.where(q_in, 1, 0)
        value = pltpu.roll(jnp.where(lower, red, black), turn, 0)[:16]
        work[pl.ds(32 * p, 16, stride=2), :] = value
        work[pl.ds(32 * p + 1, 16, stride=2), :] = value
    work2[pl.ds(0, 384), :] = dot(work[pl.ds(0, 384), :], mats[TO1])

    def lift1(p, carry):
        value = joined(v1[p], v1s_lo[p // 4], v1s_hi[p // 4], lax.rem(p, 4))
        b1[p + 1] = value + work2[pl.ds(pl.multiple_of(32 * p, 32), 32), :]
        return carry

    lax.fori_loop(0, 12, lift1, 0, unroll=4)
    half1(RED, b1, r1)
    half1(BLACK, r1, b1)
    half1(RED, b1, r1)
    half1(BLACK, r1, b1)

    for c in fine:
        c.wait()
    used = (lane32 < 72) | (lane32 >= 120)

    for p in range(14):
        x = p + 5
        red, black = r1[x // 2 + 1], b1[x // 2 + 1]
        value = jnp.where(q_in, red, black) if x % 2 == 0 else jnp.where(q_in, black, red)
        value = jnp.where(used, value, 0.0)[4:28]
        work[pl.ds(48 * p, 24, stride=2), :] = value
        work[pl.ds(48 * p + 1, 24, stride=2), :] = value
    work3[...] = dot(work[pl.ds(0, 672), :], qz0[...])

    def lift_halo(p, carry):
        at = p + 5
        group, m = at // 8, lax.rem(at, 8)
        merged = jnp.where(first48, us_lo[group], us_hi[group])
        beyond = pltpu.roll(merged, lax.rem(120 - 16 * m + 128, 128), 1)
        u1[p] = jnp.concatenate([u1[p, :, pl.ds(0, 128)], beyond], axis=1) + work3[pl.ds(pl.multiple_of(48 * p, 16), 48), :]
        return carry

    def own_black(p, carry):
        u1[p, pl.ds(8, 32), pl.ds(0, 128)] = b0[p, pl.ds(8, 32), pl.ds(0, 128)]
        return carry

    lax.fori_loop(3, 11, own_black, 0)
    lax.fori_loop(0, 14, lift_halo, 0, unroll=7)
    half0(RED, u1, r0, 0, 12)
    half0(BLACK, r0, b0, 0, 12)
    half0(RED, b0, r0, 1, 11)
    half0(BLACK, r0, b0, 1, 11)

    def finish(p, carry):
        red, black = resid0(p + 2)
        red, black = red[8:40, :128], black[8:40, :128]
        res[2 * p] = jnp.where(q_in, red, black)
        res[2 * p + 1] = jnp.where(q_in, black, red)
        red, black = r0[p + 3, pl.ds(8, 32), pl.ds(0, 128)], b0[p + 3, pl.ds(8, 32), pl.ds(0, 128)]
        sol[2 * p] = jnp.where(q_in, red, black)
        sol[2 * p + 1] = jnp.where(q_in, black, red)
        return carry

    lax.fori_loop(0, 8, finish, 0, unroll=4)


def on_device(right_side, initial, alpha, beta_x, beta_y, beta_z):
    block = jax.ShapeDtypeStruct(right_side.shape, F32)
    V = lambda *shape: pltpu.VMEM(shape, F32)
    D = lambda n: pltpu.SemaphoreType.DMA((n,))
    scratch = [
        V(5, 26, 32, 128), V(3, 16, 8, 128), V(3, 16, 8, 128), V(3, 25, 8, 128), V(3, 25, 8, 128),
        V(16, 32, 128), V(14, 48, 256),
        V(3, 2, 32, 128), V(3, 2, 32, 128), V(3, 4, 48, 128), V(3, 4, 48, 128),
        V(15, 12, 48, 256), V(2, 12, 48, 256), V(14, 48, 256), V(14, 48, 256), V(14, 48, 256),
        V(32, 128), V(3, 48, 128), V(3, 48, 128),
        V(2, 24, 32, 128), V(2, 16, 128), V(2, 16, 128), V(2, 3, 32, 128), V(2, 3, 32, 128), V(15, 12, 32, 128),
        V(12, 32, 128), V(16, 128), V(3, 32, 128), V(3, 32, 128),
        V(2, 12, 32, 128), V(14, 32, 128), V(14, 32, 128),
        V(12, 32, 128), V(16, 128), V(3, 32, 128), V(3, 32, 128),
        V(2, 4, 4, 4, 4, 8, 128), V(2, 64, 8, 128), V(4, 32, 32, 128), V(15, 16, 32, 128), V(2, 16, 32, 128),
        V(18, 32, 128), V(18, 32, 128), V(15, 8, 16, 128), V(15, 4, 8, 128),
        V(2048, 128), V(2048, 128), V(672, 256), pltpu.VMEM((5, 128, 128), jnp.bfloat16), pltpu.VMEM((128, 256), jnp.bfloat16),
        D(6), D(34), D(34), D(26), D(26), D(26), D(26), D(26), D(26), D(26), D(26),
        D(18), D(18), D(2), D(2), D(1), D(1),
    ]
    return pl.pallas_call(
        kernel,
        out_shape=(block, block),
        in_specs=[pl.BlockSpec(memory_space=pl.ANY)] * 6,
        out_specs=[pl.BlockSpec(memory_space=pltpu.VMEM)] * 2,
        scratch_shapes=scratch,
        compiler_params=pltpu.CompilerParams(collective_id=0, has_side_effects=True, vmem_limit_bytes=60 << 20),
    )(right_side, initial, alpha, beta_x, beta_y, beta_z)


def solution(mesh):
    spec = P("gx", "gy", "gz")
    return jax.shard_map(on_device, mesh=mesh, in_specs=(spec,) * 6, out_specs=(spec, spec), check_vma=False)
```

```python
import itertools

import jax
import jax.numpy as jnp
from jax import lax
from jax.experimental import pallas as pl
from jax.experimental.pallas import tpu as pltpu
from jax.sharding import PartitionSpec as P

MESH = pl.DeviceIdType.MESH
F32 = jnp.float32
GRID = (8, 4, 4)
OFFS = [o for o in itertools.product((-1, 0, 1), repeat=3) if o != (0, 0, 0)]
FLAT = sorted([o for o in OFFS if o[2] == 0], key=lambda o: (o[0] != 0, o[1] == 0))
TALL = [o for o in OFFS if o[2] != 0]
RED, BLACK = 0, 1
SAME, OTHER_R, YL_R, YH_R, ZL_R, ZH_R, ID_R, D_R, OTHER_B, YL_B, YH_B, ZL_B, ZH_B, ID_B, D_B = range(15)


def dot(a, pick):
    total = None
    for _ in range(3):
        term = a.astype(jnp.bfloat16)
        part = jnp.dot(term, pick, preferred_element_type=F32)
        total = part if total is None else total + part
        a = a - term.astype(F32)
    return total


def iota(shape, dim):
    return lax.broadcasted_iota(jnp.int32, shape, dim)


def checker(shape):
    return ((iota(shape, 0) + iota(shape, 1)) & 1) == 0


def roll(x, shift, axis):
    size = x.shape[axis]
    shift = shift % size
    return pltpu.roll(x, shift, axis) if shift else x


def couplings(even, odd, next_x, keep_x, keep_next, keep_y, keep_z, scale, q0):
    parts = []
    for alpha, low_x, low_y, low_z in (even, odd):
        low_y, low_z = scale * low_y, scale * low_z
        own_y, own_z = low_y * keep_y, low_z * keep_z
        high_y, high_z = roll(own_y, -1, 0), roll(own_z, -1, 1)
        parts.append((own_y, high_y, own_z, high_z, alpha + (low_y + high_y) + (low_z + high_z)))
    x_e, x_o = scale * even[1], scale * odd[1]
    x_n = scale * next_x * keep_next
    d_e = parts[0][4] + (x_e + x_o)
    d_o = parts[1][4] + (x_o + x_n)
    x_e = x_e * keep_x
    i_e, i_o = 1.0 / d_e, 1.0 / d_o
    red = [jnp.where(q0, x_e, x_n)] + [jnp.where(q0, parts[0][n], parts[1][n]) for n in range(4)]
    red += [jnp.where(q0, i_e, i_o), jnp.where(q0, d_e, d_o)]
    black = [jnp.where(q0, x_n, x_e)] + [jnp.where(q0, parts[1][n], parts[0][n]) for n in range(4)]
    black += [jnp.where(q0, i_o, i_e), jnp.where(q0, d_o, d_e)]
    return [x_o] + red + black


def gathered_sum(colour, here, below, above, source, coef, q0):
    if colour == RED:
        other, base = jnp.where(q0, below, above), OTHER_R
    else:
        other, base = jnp.where(q0, above, below), OTHER_B
    total = source + coef(SAME) * here + coef(base) * other
    total = total + (coef(base + 1) * roll(here, 1, 0) + coef(base + 2) * roll(here, -1, 0))
    return total + (coef(base + 3) * roll(here, 1, 1) + coef(base + 4) * roll(here, -1, 1))


def kernel(
    f_hbm, u_hbm, a_hbm, bx_hbm, by_hbm, bz_hbm, sol, res,
    e5, y_top, y_bot, y_lo, y_hi, u_in, u0, s_hi, s_lo, l_lo, l_hi, k0, g0, r0, b0, u1, us, us_lo, us_hi,
    e1, e1s_up, e1s_dn, e1s_lo, e1s_hi, k1, f1, f1s, f1s_lo, f1s_hi, g1, r1, b1, v1, v1s, v1s_lo, v1s_hi,
    ga, gb, w2, k2, g2, r2, b2, k3, k4, work, work2, work3, mats, qz0,
    in_sem, a_send, a_recv, b_send, b_recv, c_send, c_recv, d_send, d_recv, e_send, e_recv,
    h_send, h_recv, p_send, p_recv, i_send, i_recv,
):
    gx, gy, gz = lax.axis_index("gx"), lax.axis_index("gy"), lax.axis_index("gz")
    me = (gx, gy, gz)
    core = lax.rem(gx, 2)
    chip = ((gx // 2) * 4 + gy) * 4 + gz

    near = [[lax.rem(me[d] + (k + GRID[d]), GRID[d]) if k else me[d] for k in (-1, 0, 1)] for d in range(3)]

    def nb(o):
        return tuple(near[d][o[d] + 1] for d in range(3))

    partner = (gx + 1 - 2 * core, gy, gz)

    loads = [pltpu.make_async_copy(u_hbm, u_in, in_sem.at[5])]
    for n, ref in enumerate((f_hbm, a_hbm, bx_hbm, by_hbm, bz_hbm)):
        loads.append(pltpu.make_async_copy(ref, e5.at[n, pl.ds(4, 16)], in_sem.at[n]))
    for c in loads:
        c.start()

    def zero(ref, at):
        ref[at] = jnp.zeros(ref.shape[1:], F32)

    for ref in (u0, u1):
        zero(ref, 0)
        zero(ref, 13)
    barrier = pltpu.get_barrier_semaphore()

    turns = [[lax.rem(at + k, 4) for k in range(4)] for at in (gx // 2, gy, gz)]
    peers = sorted(itertools.product(range(4), repeat=3), key=lambda k: -sum(min(n, 4 - n) for n in k))[:-1]
    peers = [(turns[0][k[0]] * 2 + core, turns[1][k[1]], turns[2][k[2]]) for k in peers]
    for to in peers:
        pl.semaphore_signal(barrier, inc=1, device_id=to, device_id_type=MESH)
    for o in OFFS:
        if o[0]:
            pl.semaphore_signal(barrier, inc=1, device_id=nb(o), device_id_type=MESH)

    row, col = iota((128, 128), 0), iota((128, 128), 1)
    one = lambda cond: jnp.where(cond, 1.0, 0.0).astype(F32)
    SUM, EVEN, SUM32, DOUBLE, TO1 = range(5)
    mats[SUM] = one((row >> 1) == (col & 63)).astype(jnp.bfloat16)
    mats[EVEN] = one(row == 2 * (col & 63)).astype(jnp.bfloat16)
    mats[SUM32] = one((row >> 1) == (col & 31)).astype(jnp.bfloat16)
    mats[DOUBLE] = one(row == (col >> 1)).astype(jnp.bfloat16)
    z1 = jnp.where(col < 96, col, col - 128)
    mats[TO1] = one(row == (((z1 + 64 * gz) >> 1) & 127)).astype(jnp.bfloat16)
    wide_col, wide_row = iota((128, 256), 1), iota((128, 256), 0)
    z0 = jnp.where(wide_col < 192, wide_col, wide_col - 256)
    qz0[...] = one(wide_row == ((z0 >> 1) & 127)).astype(jnp.bfloat16)

    q_l0 = checker((48, 256))
    q_in = checker((32, 128))
    q16 = checker((16, 128))
    q8 = checker((8, 128))
    lane8 = iota((8, 128), 1)
    lane16 = iota((16, 128), 1)
    lane32 = iota((32, 128), 1)
    lane48 = iota((48, 128), 1)
    first16 = (lane32 & 15) < 8
    first48 = (lane48 & 15) < 8

    for ref, at in ((r0, 0), (r0, 13), (b0, 0), (b0, 13), (r1, 0), (r1, 13), (b1, 0), (b1, 13)):
        zero(ref, at)
    for ref in (r2, b2):
        zero(ref, 0)
        zero(ref, 17)

    for c in loads:
        c.wait()

    def take_black(p, carry):
        u0[4 + p - 1, pl.ds(8, 32), pl.ds(0, 128)] = jnp.where(q_in, u_in[2 * p + 1], u_in[2 * p])
        return carry

    lax.fori_loop(0, 8, take_black, 0, unroll=2)

    sub8 = iota((8, 128), 0) < 4
    y_lo[:, 24] = jnp.zeros((3, 8, 128), F32)
    y_hi[:, 24] = jnp.zeros((3, 8, 128), F32)

    def take_ends(x, carry):
        for t, (n, k) in enumerate(((0, 1), (2, 4))):
            y_top[t, x] = jnp.where(sub8, roll(e5[n, 4 + x, pl.ds(24, 8), :], 4, 0), e5[k, 4 + x, pl.ds(24, 8), :])
            y_bot[t, x] = jnp.where(sub8, e5[n, 4 + x, pl.ds(0, 8), :], roll(e5[k, 4 + x, pl.ds(0, 8), :], 4, 0))
        y_top[2, x] = e5[3, 4 + x, pl.ds(24, 8), :]
        y_bot[2, x] = e5[3, 4 + x, pl.ds(0, 8), :]
        return carry

    lax.fori_loop(0, 16, take_ends, 0, unroll=4)

    pl.semaphore_wait(barrier, 81)

    def remote(src, dst, send, recv, to):
        return pltpu.make_async_remote_copy(
            src_ref=src, dst_ref=dst, send_sem=send, recv_sem=recv, device_id=to, device_id_type=MESH
        )

    Y0 = {-1: (8, 40, 8), 0: (8, 8, 32), 1: (32, 0, 8)}
    X5 = {-1: (0, 20, 5), 1: (12, 0, 4)}
    XY = {-1: (0, 20, 4), 0: (0, 4, 16), 1: (12, 0, 4)}
    XE = {-1: (3, 11, 2), 1: (9, 1, 2)}
    XU = {-1: (3, 11, 3), 0: (3, 3, 8), 1: (8, 0, 3)}
    XS = {-1: (0, 3, 1), 0: (0, 1, 2), 1: (1, 0, 1)}
    YS = {-1: (0, 40, 8), 0: (0, 8, 32), 1: (24, 0, 8)}
    first = []
    for n, o in enumerate(FLAT):
        if o[1]:
            (xs, xd, xn), (src, dst) = XY[o[0]], (y_top, y_lo) if o[1] == 1 else (y_bot, y_hi)
        else:
            (xs, xd, xn), (src, dst) = X5[o[0]], (e5, e5)
            xs += 4
        first.append(remote(
            src.at[:, pl.ds(xs, xn)], dst.at[:, pl.ds(xd, xn)], a_send.at[18 + n], a_recv.at[18 + n], nb(o)
        ))
        (xs, xd, xn), (ys, yd, yn) = (XE if o[0] and o[1] else XU)[o[0]], Y0[o[1]]
        first.append(remote(
            u0.at[pl.ds(xs, xn), pl.ds(ys, yn), pl.ds(0, 128)], u0.at[pl.ds(xd, xn), pl.ds(yd, yn), pl.ds(0, 128)],
            a_send.at[26 + n], a_recv.at[26 + n], nb(o),
        ))
    for c in first:
        c.start()

    for half in range(2):
        for t, (one_n, two_n) in enumerate(((0, 1), (2, 3), (4, 5))):
            acc_a = jnp.zeros((32, 128), F32)
            acc_b = jnp.zeros((32, 128), F32)
            for m in range(8):
                at = 8 * half + m
                rolled = roll(e5[one_n, 4 + at], 16 * m + 8, 1)
                acc_a = jnp.where((lane32 >> 4) == m, rolled, acc_a)
                if two_n < 5:
                    rolled = roll(e5[two_n, 4 + at], 16 * m + 16, 1)
                elif m < 4:
                    rolled = roll(u0[3 + 4 * half + m, pl.ds(8, 32), pl.ds(0, 128)], 16 * m + 16, 1)
                else:
                    continue
                acc_b = jnp.where((((lane32 + 120) & 127) >> 4) == m, rolled, acc_b)
            s_hi[t, half] = jnp.where(first16, acc_a, acc_b)
            s_lo[t, half] = jnp.where(first16, acc_b, acc_a)

    beyond = []
    for n, o in enumerate(TALL):
        (xs, xd, xn), (ys, yd, yn) = XS[o[0]], YS[o[1]]
        src, dst = (s_hi, l_lo) if o[2] == 1 else (s_lo, l_hi)
        beyond.append(remote(
            src.at[:, pl.ds(xs, xn), pl.ds(ys, yn)], dst.at[:, pl.ds(xd, xn), pl.ds(yd, yn)],
            a_send.at[n], a_recv.at[n], nb(o),
        ))
    for c in beyond:
        c.start()
    first += beyond

    def coarsen(count, rows, read):
        size = count * rows
        for p in range(count):
            for n in range(4):
                even = read(n, 2 * p)
                work[pl.ds(n * size + p * rows, rows), :] = even if n == 1 else even + read(n, 2 * p + 1)
        work2[pl.ds(0, 3 * size), :] = dot(work[pl.ds(0, 3 * size), :], mats[SUM])
        work2[pl.ds(3 * size, size), :] = dot(work[pl.ds(3 * size, size), :], mats[EVEN])

        def result(n, p):
            at = n * size + p * rows
            low = work2[pl.ds(at, rows // 2, stride=2), :]
            if n == 2:
                return 0.25 * low
            return (0.125 if n == 0 else 0.25) * (low + work2[pl.ds(at + 1, rows // 2, stride=2), :])

        return result

    got = coarsen(8, 32, lambda n, x: e5[n + 1, 4 + x])
    first16b = (lane16 & 15) < 8
    for n in range(0, 4, 2):
        acc_a = jnp.zeros((16, 128), F32)
        acc_b = jnp.zeros((16, 128), F32)
        for m in range(8):
            one_v, two_v = got(n, m), got(n + 1, m)
            e1[n // 2, 8 + m, pl.ds(8, 16), :] = jnp.where(lane16 < 64, one_v, two_v)
            acc_a = jnp.where((lane16 >> 4) == m, roll(one_v, 16 * m + 8, 1), acc_a)
            acc_b = jnp.where((((lane16 + 120) & 127) >> 4) == m, roll(two_v, 16 * m + 16, 1), acc_b)
        e1s_up[n // 2] = jnp.where(first16b, acc_a, acc_b)
        e1s_dn[n // 2] = jnp.where(first16b, acc_b, acc_a)

    Y1 = {-1: (8, 24, 8), 0: (8, 8, 16), 1: (16, 0, 8)}
    YT = {-1: (0, 24, 8), 0: (0, 8, 16), 1: (8, 0, 8)}
    XT = {-1: 2, 0: 1, 1: 0}

    def spread1(main, to_high, to_low, low, high, send, recv, lead):
        out = []
        for n, o in enumerate(TALL):
            ys, yd, yn = YT[o[1]]
            dst, strip = (low, to_high) if o[2] == 1 else (high, to_low)
            src = strip.at[:, pl.ds(ys, yn)] if lead else strip.at[pl.ds(ys, yn)]
            dst = dst.at[:, XT[o[0]], pl.ds(yd, yn)] if lead else dst.at[XT[o[0]], pl.ds(yd, yn)]
            out.append(remote(src, dst, send.at[n], recv.at[n], nb(o)))
        for n, o in enumerate(FLAT):
            size = main.shape[1 if lead else 0] // 3
            (xs, xd, xn), (ys, yd, yn) = (size, size * (1 - o[0]), size), Y1[o[1]]
            src = (pl.ds(xs, xn), pl.ds(ys, yn))
            dst = (pl.ds(xd, xn), pl.ds(yd, yn))
            if lead:
                src, dst = (slice(None),) + src, (slice(None),) + dst
            out.append(remote(main.at[src], main.at[dst], send.at[18 + n], recv.at[18 + n], nb(o)))
        return out

    coefs1 = spread1(e1, e1s_up, e1s_dn, e1s_lo, e1s_hi, b_send, b_recv, True)
    for c in coefs1:
        c.start()

    def twice(n, value):
        other = roll(value, 64, 1)
        return jnp.where(lane16 < 64, other, value) if n % 2 else jnp.where(lane16 < 64, value, other)

    got = coarsen(4, 16, lambda n, x: twice(n, e1[n // 2, 8 + x, pl.ds(8, 16), :]))
    for n in range(4):
        acc = got(n, 0)
        for m in range(1, 4):
            acc = jnp.where((lane8 >> 5) == m, got(n, m), acc)
        ga[core, gx // 2, gy, gz, n] = acc

    def along(axis, k):
        if axis == "z":
            return lax.rem(gx + 2 * k, 8), gy, gz
        return (gx, lax.rem(gy + k, 4), gz) if axis == "y" else (gx, gy, lax.rem(gz + k, 4))

    def part(order, axis, back):
        z, y, x = gx // 2, gy, gz
        if axis == "z":
            z = lax.rem(z + 4 - back, 4)
        elif axis == "y":
            y = lax.rem(y + 4 - back, 4)
        else:
            x = lax.rem(x + 4 - back, 4)
        if order == "xyz":
            y, x = slice(None) if axis == "z" else y, x if axis == "x" else slice(None)
            return ga.at[core, z, y, x, pl.ds(0, 2)]
        z, y = slice(None) if axis == "x" else z, y if axis == "y" else slice(None)
        return ga.at[core, z, y, x, pl.ds(2, 2)]

    def legs(stage):
        for n, order in enumerate(("xyz", "yzx")):
            for k in range(1, 4):
                yield order, order[stage], k, 6 * stage + 3 * n + k - 1

    def pass_on(stage):
        for order, axis, k, at in legs(stage):
            own = part(order, axis, 0)
            remote(own, own, h_send.at[at], h_recv.at[at], along(axis, k)).start()

    def passed_on(stage):
        for order, axis, k, at in legs(stage):
            own, theirs = part(order, axis, 0), part(order, axis, k)
            remote(own, own, h_send.at[at], h_recv.at[at], along(axis, k)).wait_send()
            remote(theirs, theirs, h_send.at[at], h_recv.at[at], along(axis, k)).wait_recv()

    pass_on(0)
    passed_on(0)
    pass_on(1)

    for c in first:
        c.wait_recv()
    keep_y0 = one(((iota((48, 256), 0) - 8 + 32 * gy) & 127) != 0)
    lane256 = iota((48, 256), 1)
    keep_z0 = one(((jnp.where(lane256 < 192, lane256, lane256 - 256) + 128 * gz) & 511) != 0)

    def side(n, group, m):
        t, low, high = n // 2, l_lo, l_hi
        if n % 2:
            return pltpu.roll(jnp.where(first48, high[t, group], low[t, group]), lax.rem(112 - 16 * m + 128, 128), 1)
        return pltpu.roll(jnp.where(first48, low[t, group], high[t, group]), lax.rem(120 - 16 * m + 128, 128), 1)

    def fine_row(n, x):
        at = x + 4
        t, swap = ((0, 0), (0, 4), (1, 0), (2, 0), (1, 4))[n]
        low = y_lo[t, x] if swap or n == 3 else roll(y_lo[t, x], 4, 0)
        high = roll(y_hi[t, x], 4, 0) if swap else y_hi[t, x]
        main = jnp.concatenate([low, e5[n, x], high], axis=0)
        return jnp.concatenate([main, side(n, at // 8, lax.rem(at, 8))], axis=1)

    def build0(p, carry):
        e, o = 2 * p, 2 * p + 1
        even = tuple(fine_row(n, e) for n in range(1, 5))
        odd = tuple(fine_row(n, o) for n in range(1, 5))
        keep_e = jnp.where(((e - 4 + 16 * gx) & 127) == 0, 0.0, 1.0).astype(F32)
        keep_n = jnp.where(((e - 2 + 16 * gx) & 127) == 0, 0.0, 1.0).astype(F32)
        for n, value in enumerate(couplings(even, odd, fine_row(2, e + 2), keep_e, keep_n, keep_y0, keep_z0, 1.0, q_l0)):
            k0[n, p] = value
        f_e, f_o = fine_row(0, e), fine_row(0, o)
        g0[RED, p] = jnp.where(q_l0, f_e, f_o)
        g0[BLACK, p] = jnp.where(q_l0, f_o, f_e)
        return carry

    lax.fori_loop(0, 12, build0, 0, unroll=2)

    passed_on(1)
    pass_on(2)

    def side_u(p, carry):
        at = p + 1
        u0[p, :, pl.ds(128, 128)] = side(5, at // 4, lax.rem(at, 4))
        return carry

    lax.fori_loop(0, 14, side_u, 0, unroll=7)

    def half0(colour, src, dst, start, stop):
        def one_pair(p, carry):
            coef = lambda n: k0[n, p]
            total = gathered_sum(colour, src[p + 1], src[p], src[p + 2], g0[colour, p], coef, q_l0)
            dst[p + 1] = total * k0[ID_R if colour == RED else ID_B, p]
            return carry

        lax.fori_loop(start, stop, one_pair, 0, unroll=4)

    half0(RED, u0, r0, 0, 12)
    half0(BLACK, r0, b0, 0, 12)
    half0(RED, b0, r0, 1, 11)
    half0(BLACK, r0, b0, 1, 11)

    def resid0(p):
        coef = lambda n: k0[n, p]
        out = []
        for colour, own, far in ((RED, r0, b0), (BLACK, b0, r0)):
            total = gathered_sum(colour, far[p + 1], far[p], far[p + 2], g0[colour, p], coef, q_l0)
            out.append(total - k0[D_R if colour == RED else D_B, p] * own[p + 1])
        return out

    def restrict0(p, carry):
        red, black = resid0(p + 2)
        work[pl.ds(32 * p, 32), :] = (red + black)[8:40, :128]
        return carry

    lax.fori_loop(0, 8, restrict0, 0, unroll=4)
    work2[pl.ds(0, 256), :] = dot(work[pl.ds(0, 256), :], mats[SUM])
    acc = jnp.zeros((16, 128), F32)
    values = []
    for m in range(8):
        value = 0.125 * (work2[pl.ds(32 * m, 16, stride=2), :] + work2[pl.ds(32 * m + 1, 16, stride=2), :])
        values.append(value)
        if m >= 4:
            f1[m, pl.ds(8, 16), :] = jnp.where(lane16 < 64, values[m - 4], value)
        acc = jnp.where((lane16 >> 4) == m, roll(value, 16 * m + 8, 1), acc)
    f1s[...] = acc

    right1 = spread1(f1, f1s, f1s, f1s_lo, f1s_hi, c_send, c_recv, False)
    for c in right1:
        c.start()

    acc = jnp.zeros((32, 128), F32)
    for m in range(8):
        acc = jnp.where((lane32 >> 4) == m, roll(b0[3 + m, pl.ds(8, 32), pl.ds(0, 128)], 16 * m + 8, 1), acc)
    us[...] = acc
    YU = {-1: (0, 40, 8), 0: (0, 8, 32), 1: (24, 0, 8)}
    fine = []
    for n, o in enumerate(TALL):
        ys, yd, yn = YU[o[1]]
        dst = us_lo if o[2] == 1 else us_hi
        fine.append(remote(us.at[pl.ds(ys, yn)], dst.at[XT[o[0]], pl.ds(yd, yn)], d_send.at[n], d_recv.at[n], nb(o)))
    for n, o in enumerate(FLAT):
        (xs, xd, xn), (ys, yd, yn) = (XE if o[0] and o[1] else XU)[o[0]], Y0[o[1]]
        fine.append(remote(
            b0.at[pl.ds(xs, xn), pl.ds(ys, yn), pl.ds(0, 128)], u1.at[pl.ds(xd, xn), pl.ds(yd, yn), pl.ds(0, 128)],
            d_send.at[18 + n], d_recv.at[18 + n], nb(o),
        ))
    for c in fine:
        c.start()

    for c in first:
        c.wait_send()
    for c in coefs1:
        c.wait()
    keep_y1 = one(((iota((32, 128), 0) - 8 + 16 * gy) & 63) != 0)
    keep_z1 = one(((jnp.where(lane32 < 96, lane32, lane32 - 128) + 64 * gz) & 255) != 0)

    def joined(main, low, high, m, back=0):
        above = pltpu.roll(high, lax.rem(56 - back - 16 * m + 256, 128), 1)
        below = pltpu.roll(low, lax.rem(120 - back - 16 * m + 256, 128), 1)
        return jnp.where(lane32 < 64, main, jnp.where(lane32 < 96, above, below))

    def coarse_row(n, x):
        main = e1[n // 2, x]
        if n % 2:
            main = roll(main, 64, 1)
        return joined(main, e1s_lo[n // 2, x // 8], e1s_hi[n // 2, x // 8], lax.rem(x, 8), 8 * (n % 2))

    def build1(p, carry):
        e, o = 2 * p, 2 * p + 1
        even = tuple(coarse_row(n, e) for n in range(4))
        odd = tuple(coarse_row(n, o) for n in range(4))
        after = coarse_row(1, lax.rem(e + 2, 24))
        keep_e = jnp.where(((e - 8 + 8 * gx) & 63) == 0, 0.0, 1.0).astype(F32)
        keep_n = jnp.where(((e - 6 + 8 * gx) & 63) == 0, 0.0, 1.0).astype(F32)
        for n, value in enumerate(couplings(even, odd, after, keep_e, keep_n, keep_y1, keep_z1, 0.25, q_in)):
            k1[n, p] = value
        return carry

    lax.fori_loop(0, 12, build1, 0, unroll=2)

    passed_on(2)
    pair_a = remote(ga.at[core], ga.at[core], p_send.at[0], p_recv.at[0], partner)
    pair_a.start()

    for c in right1:
        c.wait_recv()

    def source1(p, carry):
        e, o = 2 * p, 2 * p + 1
        f_e, f_o = (
            joined(pltpu.roll(f1[(x // 8) * 4 + lax.rem(x, 4)], 64 * (lax.rem(x, 8) // 4), 1),
                   f1s_lo[x // 8], f1s_hi[x // 8], lax.rem(x, 8))
            for x in (e, o)
        )
        red = jnp.where(q_in, f_e, f_o)
        g1[RED, p] = red
        g1[BLACK, p] = jnp.where(q_in, f_o, f_e)
        r1[p + 1] = red * k1[ID_R, p]
        return carry

    lax.fori_loop(0, 12, source1, 0, unroll=12)

    def half1(colour, src, dst):
        def one_pair(p, carry):
            coef = lambda n: k1[n, p]
            total = gathered_sum(colour, src[p + 1], src[p], src[p + 2], g1[colour, p], coef, q_in)
            dst[p + 1] = total * k1[ID_R if colour == RED else ID_B, p]
            return carry

        lax.fori_loop(0, 12, one_pair, 0, unroll=12)

    half1(BLACK, r1, b1)
    half1(RED, b1, r1)
    half1(BLACK, r1, b1)
    for p in range(4):
        coef = lambda n: k1[n, p + 4]
        total = gathered_sum(RED, b1[p + 5], b1[p + 4], b1[p + 6], g1[RED, p + 4], coef, q_in) - k1[D_R, p + 4] * r1[p + 5]
        other = gathered_sum(BLACK, r1[p + 5], r1[p + 4], r1[p + 6], g1[BLACK, p + 4], coef, q_in)
        total = total + (other - k1[D_B, p + 4] * b1[p + 5])
        work[pl.ds(16 * p, 16), :] = jnp.where(lane16 < 64, total[8:24], 0.0)
    work2[pl.ds(0, 64), :] = dot(work[pl.ds(0, 64), :], mats[SUM32])
    acc = jnp.zeros((8, 128), F32)
    for m in range(4):
        value = 0.125 * (work2[pl.ds(16 * m, 8, stride=2), :] + work2[pl.ds(16 * m + 1, 8, stride=2), :])
        acc = jnp.where((lane8 >> 5) == m, value, acc)
    gb[core, chip] = acc

    for to in peers:
        remote(gb.at[core, chip], gb.at[core, chip], i_send.at[0], i_recv.at[0], to).start()

    acc = jnp.zeros((16, 128), F32)
    for m in range(4):
        value = b1[5 + m, pl.ds(8, 16), :]
        value = jnp.where(lane16 < 64, value, roll(value, 64, 1))
        acc = jnp.where((lane16 >> 4) == m, roll(value, 16 * m + 8, 1), acc)
        v1[4 + m, pl.ds(8, 16), :] = value
    v1s[...] = acc
    black1 = []
    for n, o in enumerate(TALL):
        ys, yd, yn = YT[o[1]]
        dst = v1s_lo if o[2] == 1 else v1s_hi
        black1.append(remote(v1s.at[pl.ds(ys, yn)], dst.at[XT[o[0]], pl.ds(yd, yn)], e_send.at[n], e_recv.at[n], nb(o)))
    for n, o in enumerate(FLAT):
        (xs, xd, xn), (ys, yd, yn) = {-1: (4, 8, 4), 0: (4, 4, 4), 1: (4, 0, 4)}[o[0]], Y1[o[1]]
        black1.append(remote(
            v1.at[pl.ds(xs, xn), pl.ds(ys, yn)], v1.at[pl.ds(xd, xn), pl.ds(yd, yn)],
            e_send.at[18 + n], e_recv.at[18 + n], nb(o),
        ))
    for c in black1:
        c.start()

    for c in right1:
        c.wait_send()

    pair_a.wait()

    def untile(tiles):
        out = []
        for m in range(4):
            total = tiles[0] if m == 0 else roll(tiles[0], -32 * m, 1)
            for k in range(1, 4):
                total = jnp.where((lane8 >> 5) == k, roll(tiles[k], 32 * (k - m), 1), total)
            out.append(total)
        return out

    def place(tiles_of, count):
        def one_block(t, carry):
            bx, by = t // 4, lax.rem(t, 4)
            rows = pl.ds(pl.multiple_of(8 * by, 8), 8)
            for n in range(count):
                for m, value in enumerate(untile([tiles_of(lax.rem(bx, 2), bx // 2, by, k, n) for k in range(4)])):
                    w2[n, 4 * bx + m, rows, :] = value
            return carry

        lax.fori_loop(0, 32, one_block, 0, unroll=4)

    place(lambda side_core, bz, by, k, n: ga[side_core, bz, by, k, n], 4)

    keep_y2 = one(iota((32, 128), 0) != 0)
    keep_z2 = one(lane32 != 0)

    def build2(p, carry):
        e, o = 2 * p, 2 * p + 1
        even = tuple(w2[n, e] for n in range(4))
        odd = tuple(w2[n, o] for n in range(4))
        keep_e = jnp.where(p == 0, 0.0, 1.0).astype(F32)
        keep_n = jnp.where(p == 15, 0.0, 1.0).astype(F32)
        after = w2[1, lax.rem(e + 2, 32)]
        for n, value in enumerate(couplings(even, odd, after, keep_e, keep_n, keep_y2, keep_z2, 0.25**2, q_in)):
            k2[n, p] = value
        return carry

    lax.fori_loop(0, 16, build2, 0, unroll=2)

    def small(level_coefs, count, rows, period, scale, q, dest):
        keep_y = one(iota((rows, 128), 0) != 0)
        keep_z = one((iota((rows, 128), 1) & (period - 1)) != 0)
        for p in range(count):
            even = tuple(level_coefs(n, 2 * p) for n in range(4))
            odd = tuple(level_coefs(n, 2 * p + 1) for n in range(4))
            after = level_coefs(1, (2 * p + 2) % (2 * count))
            for n, value in enumerate(couplings(
                even, odd, after, 0.0 if p == 0 else 1.0, 0.0 if p == count - 1 else 1.0, keep_y, keep_z, scale, q
            )):
                dest[n, p] = value

    got3 = coarsen(16, 32, lambda n, x: w2[n, x])
    rows3 = [[got3(n, x) for x in range(16)] for n in range(4)]
    for n in range(4):
        for x in range(16):
            w2[n, x, pl.ds(0, 16), :] = rows3[n][x]
    small(lambda n, x: w2[n, x, pl.ds(0, 16), :], 8, 16, 64, 0.25**3, q16, k3)
    got4 = coarsen(8, 16, lambda n, x: w2[n, x, pl.ds(0, 16), :])
    small(got4, 4, 8, 32, 0.25**4, q8, k4)

    others = gb.at[core, pl.ds(0, 63)]
    remote(others, others, i_send.at[0], i_recv.at[0], partner).wait()
    pair_b = remote(gb.at[core], gb.at[core], p_send.at[1], p_recv.at[1], partner)
    pair_b.start()
    pair_b.wait()

    place(lambda side_core, bz, by, k, n: gb[side_core, bz * 16 + by * 4 + k], 1)

    def source2(p, carry):
        f_e, f_o = w2[0, 2 * p], w2[0, 2 * p + 1]
        red = jnp.where(q_in, f_e, f_o)
        g2[RED, p] = red
        g2[BLACK, p] = jnp.where(q_in, f_o, f_e)
        r2[p + 1] = red * k2[ID_R, p]
        return carry

    lax.fori_loop(0, 16, source2, 0, unroll=16)

    def half2(colour, src, dst):
        def one_pair(p, carry):
            coef = lambda n: k2[n, p]
            total = gathered_sum(colour, src[p + 1], src[p], src[p + 2], g2[colour, p], coef, q_in)
            dst[p + 1] = total * k2[ID_R if colour == RED else ID_B, p]
            return carry

        lax.fori_loop(0, 16, one_pair, 0, unroll=16)

    half2(BLACK, r2, b2)
    half2(RED, b2, r2)
    half2(BLACK, r2, b2)

    def restrict2(p, carry):
        coef = lambda n: k2[n, p]
        total = gathered_sum(RED, b2[p + 1], b2[p], b2[p + 2], g2[RED, p], coef, q_in) - k2[D_R, p] * r2[p + 1]
        other = gathered_sum(BLACK, r2[p + 1], r2[p], r2[p + 2], g2[BLACK, p], coef, q_in)
        work[pl.ds(pl.multiple_of(32 * p, 32), 32), :] = total + (other - k2[D_B, p] * b2[p + 1])
        return carry

    lax.fori_loop(0, 16, restrict2, 0, unroll=16)
    work2[pl.ds(0, 512), :] = dot(work[pl.ds(0, 512), :], mats[SUM])

    def pack(rows, q):
        count = len(rows) // 2
        red = [jnp.where(q, rows[2 * p], rows[2 * p + 1]) for p in range(count)]
        black = [jnp.where(q, rows[2 * p + 1], rows[2 * p]) for p in range(count)]
        return red, black

    def half_small(colour, src, source, k, q, own=None):
        count = len(src)
        out = []
        for p in range(count):
            coef = lambda n: k[n, p]
            total = gathered_sum(colour, src[p], src[p - 1], src[(p + 1) % count], source[p], coef, q)
            if own is None:
                out.append(total * k[ID_R if colour == RED else ID_B, p])
            else:
                out.append(total - k[D_R if colour == RED else D_B, p] * own[p])
        return out

    def paired(count, rows):
        return [
            0.125 * (work2[pl.ds(2 * rows * m, rows, stride=2), :] + work2[pl.ds(2 * rows * m + 1, rows, stride=2), :])
            for m in range(count)
        ]

    def unpacked(red, black, q):
        out = []
        for r, b in zip(red, black):
            out += [jnp.where(q, r, b), jnp.where(q, b, r)]
        return out

    fr3, fb3 = pack(paired(16, 16), q16)
    r3 = [fr3[p] * k3[ID_R, p] for p in range(8)]
    b3 = half_small(BLACK, r3, fb3, k3, q16)
    r3 = half_small(RED, b3, fr3, k3, q16)
    b3 = half_small(BLACK, r3, fb3, k3, q16)
    left_r = half_small(RED, b3, fr3, k3, q16, r3)
    left_b = half_small(BLACK, r3, fb3, k3, q16, b3)
    for p in range(8):
        work[pl.ds(16 * p, 16), :] = left_r[p] + left_b[p]
    work2[pl.ds(0, 128), :] = dot(work[pl.ds(0, 128), :], mats[SUM])

    fr4, fb4 = pack(paired(8, 8), q8)
    r4 = [fr4[p] * k4[ID_R, p] for p in range(4)]
    b4 = half_small(BLACK, r4, fb4, k4, q8)

    def bottom(step, carry):
        black = list(carry[4:])
        red = half_small(RED, black, fr4, k4, q8)
        black = half_small(BLACK, red, fb4, k4, q8)
        return tuple(red + black)

    done = lax.fori_loop(0, 11, bottom, tuple(r4 + b4), unroll=11)
    e4 = unpacked(done[:4], done[4:], q8)

    def doubled(rows, size):
        total = 2 * size * len(rows)
        for m, value in enumerate(rows):
            work[pl.ds(2 * size * m, size, stride=2), :] = value
            work[pl.ds(2 * size * m + 1, size, stride=2), :] = value
        work2[pl.ds(0, total), :] = dot(work[pl.ds(0, total), :], mats[DOUBLE])
        return [work2[pl.ds(2 * size * m, 2 * size), :] for m in range(len(rows))]

    up3 = doubled(e4, 8)
    b3 = [b3[p] + up3[p] for p in range(8)]
    r3 = half_small(RED, b3, fr3, k3, q16)
    b3 = half_small(BLACK, r3, fb3, k3, q16)
    r3 = half_small(RED, b3, fr3, k3, q16)
    b3 = half_small(BLACK, r3, fb3, k3, q16)
    up2 = doubled(unpacked(r3, b3, q16), 16)
    for p in range(16):
        b2[p + 1] = b2[p + 1] + up2[p]

    half2(RED, b2, r2)
    half2(BLACK, r2, b2)
    half2(RED, b2, r2)
    half2(BLACK, r2, b2)

    for c in black1:
        c.wait()

    turn = (4 - 8 * gy) & 31
    for p in range(12):
        x = (p - 4 + 4 * gx) & 31
        red, black = r2[x // 2 + 1], b2[x // 2 + 1]
        lower = jnp.where((x & 1) == 0, 1, 0) == jnp.where(q_in, 1, 0)
        value = pltpu.roll(jnp.where(lower, red, black), turn, 0)[:16]
        work[pl.ds(32 * p, 16, stride=2), :] = value
        work[pl.ds(32 * p + 1, 16, stride=2), :] = value
    work2[pl.ds(0, 384), :] = dot(work[pl.ds(0, 384), :], mats[TO1])

    def lift1(p, carry):
        value = joined(v1[p], v1s_lo[p // 4], v1s_hi[p // 4], lax.rem(p, 4))
        b1[p + 1] = value + work2[pl.ds(pl.multiple_of(32 * p, 32), 32), :]
        return carry

    lax.fori_loop(0, 12, lift1, 0, unroll=12)
    half1(RED, b1, r1)
    half1(BLACK, r1, b1)
    half1(RED, b1, r1)
    half1(BLACK, r1, b1)

    for c in fine:
        c.wait()
    used = (lane32 < 72) | (lane32 >= 120)

    for p in range(14):
        x = p + 5
        red, black = r1[x // 2 + 1], b1[x // 2 + 1]
        value = jnp.where(q_in, red, black) if x % 2 == 0 else jnp.where(q_in, black, red)
        value = jnp.where(used, value, 0.0)[4:28]
        work[pl.ds(48 * p, 24, stride=2), :] = value
        work[pl.ds(48 * p + 1, 24, stride=2), :] = value
    work3[...] = dot(work[pl.ds(0, 672), :], qz0[...])

    def lift_halo(p, carry):
        at = p + 5
        group, m = at // 8, lax.rem(at, 8)
        merged = jnp.where(first48, us_lo[group], us_hi[group])
        beyond = pltpu.roll(merged, lax.rem(120 - 16 * m + 128, 128), 1)
        u1[p] = jnp.concatenate([u1[p, :, pl.ds(0, 128)], beyond], axis=1) + work3[pl.ds(pl.multiple_of(48 * p, 16), 48), :]
        return carry

    def own_black(p, carry):
        u1[p, pl.ds(8, 32), pl.ds(0, 128)] = b0[p, pl.ds(8, 32), pl.ds(0, 128)]
        return carry

    lax.fori_loop(3, 11, own_black, 0)
    lax.fori_loop(0, 14, lift_halo, 0, unroll=7)
    half0(RED, u1, r0, 0, 12)
    half0(BLACK, r0, b0, 0, 12)
    half0(RED, b0, r0, 1, 11)
    half0(BLACK, r0, b0, 1, 11)

    def finish(p, carry):
        red, black = resid0(p + 2)
        red, black = red[8:40, :128], black[8:40, :128]
        res[2 * p] = jnp.where(q_in, red, black)
        res[2 * p + 1] = jnp.where(q_in, black, red)
        red, black = r0[p + 3, pl.ds(8, 32), pl.ds(0, 128)], b0[p + 3, pl.ds(8, 32), pl.ds(0, 128)]
        sol[2 * p] = jnp.where(q_in, red, black)
        sol[2 * p + 1] = jnp.where(q_in, black, red)
        return carry

    lax.fori_loop(0, 8, finish, 0, unroll=4)


def on_device(right_side, initial, alpha, beta_x, beta_y, beta_z):
    block = jax.ShapeDtypeStruct(right_side.shape, F32)
    V = lambda *shape: pltpu.VMEM(shape, F32)
    D = lambda n: pltpu.SemaphoreType.DMA((n,))
    scratch = [
        V(5, 26, 32, 128), V(3, 16, 8, 128), V(3, 16, 8, 128), V(3, 25, 8, 128), V(3, 25, 8, 128),
        V(16, 32, 128), V(14, 48, 256),
        V(3, 2, 32, 128), V(3, 2, 32, 128), V(3, 4, 48, 128), V(3, 4, 48, 128),
        V(15, 12, 48, 256), V(2, 12, 48, 256), V(14, 48, 256), V(14, 48, 256), V(14, 48, 256),
        V(32, 128), V(3, 48, 128), V(3, 48, 128),
        V(2, 24, 32, 128), V(2, 16, 128), V(2, 16, 128), V(2, 3, 32, 128), V(2, 3, 32, 128), V(15, 12, 32, 128),
        V(12, 32, 128), V(16, 128), V(3, 32, 128), V(3, 32, 128),
        V(2, 12, 32, 128), V(14, 32, 128), V(14, 32, 128),
        V(12, 32, 128), V(16, 128), V(3, 32, 128), V(3, 32, 128),
        V(2, 4, 4, 4, 4, 8, 128), V(2, 64, 8, 128), V(4, 32, 32, 128), V(15, 16, 32, 128), V(2, 16, 32, 128),
        V(18, 32, 128), V(18, 32, 128), V(15, 8, 16, 128), V(15, 4, 8, 128),
        V(2048, 128), V(2048, 128), V(672, 256), pltpu.VMEM((5, 128, 128), jnp.bfloat16), pltpu.VMEM((128, 256), jnp.bfloat16),
        D(6), D(34), D(34), D(26), D(26), D(26), D(26), D(26), D(26), D(26), D(26),
        D(18), D(18), D(2), D(2), D(1), D(1),
    ]
    return pl.pallas_call(
        kernel,
        out_shape=(block, block),
        in_specs=[pl.BlockSpec(memory_space=pl.ANY)] * 6,
        out_specs=[pl.BlockSpec(memory_space=pltpu.VMEM)] * 2,
        scratch_shapes=scratch,
        compiler_params=pltpu.CompilerParams(collective_id=0, has_side_effects=True, vmem_limit_bytes=60 << 20),
    )(right_side, initial, alpha, beta_x, beta_y, beta_z)


def solution(mesh):
    spec = P("gx", "gy", "gz")
    return jax.shard_map(on_device, mesh=mesh, in_specs=(spec,) * 6, out_specs=(spec, spec), check_vma=False)
```

```python
import itertools

import jax
import jax.numpy as jnp
from jax import lax
from jax.experimental import pallas as pl
from jax.experimental.pallas import tpu as pltpu
from jax.sharding import PartitionSpec as P

MESH = pl.DeviceIdType.MESH
F32 = jnp.float32
GRID = (8, 4, 4)
OFFS = [o for o in itertools.product((-1, 0, 1), repeat=3) if o != (0, 0, 0)]
FLAT = sorted([o for o in OFFS if o[2] == 0], key=lambda o: (o[0] != 0, o[1] == 0))
TALL = [o for o in OFFS if o[2] != 0]
RED, BLACK = 0, 1
SAME, OTHER_R, YL_R, YH_R, ZL_R, ZH_R, ID_R, D_R, OTHER_B, YL_B, YH_B, ZL_B, ZH_B, ID_B, D_B = range(15)


def dot(a, pick):
    total = None
    for _ in range(3):
        term = a.astype(jnp.bfloat16)
        part = jnp.dot(term, pick, preferred_element_type=F32)
        total = part if total is None else total + part
        a = a - term.astype(F32)
    return total


def iota(shape, dim):
    return lax.broadcasted_iota(jnp.int32, shape, dim)


def checker(shape):
    return ((iota(shape, 0) + iota(shape, 1)) & 1) == 0


def roll(x, shift, axis):
    size = x.shape[axis]
    shift = shift % size
    return pltpu.roll(x, shift, axis) if shift else x


def couplings(even, odd, next_x, keep_x, keep_next, keep_y, keep_z, scale, q0):
    parts = []
    for alpha, low_x, low_y, low_z in (even, odd):
        low_y, low_z = scale * low_y, scale * low_z
        own_y, own_z = low_y * keep_y, low_z * keep_z
        high_y, high_z = roll(own_y, -1, 0), roll(own_z, -1, 1)
        parts.append((own_y, high_y, own_z, high_z, alpha + (low_y + high_y) + (low_z + high_z)))
    x_e, x_o = scale * even[1], scale * odd[1]
    x_n = scale * next_x * keep_next
    d_e = parts[0][4] + (x_e + x_o)
    d_o = parts[1][4] + (x_o + x_n)
    x_e = x_e * keep_x
    i_e, i_o = 1.0 / d_e, 1.0 / d_o
    red = [jnp.where(q0, x_e, x_n)] + [jnp.where(q0, parts[0][n], parts[1][n]) for n in range(4)]
    red += [jnp.where(q0, i_e, i_o), jnp.where(q0, d_e, d_o)]
    black = [jnp.where(q0, x_n, x_e)] + [jnp.where(q0, parts[1][n], parts[0][n]) for n in range(4)]
    black += [jnp.where(q0, i_o, i_e), jnp.where(q0, d_o, d_e)]
    return [x_o] + red + black


def gathered_sum(colour, here, below, above, source, coef, q0):
    if colour == RED:
        other, base = jnp.where(q0, below, above), OTHER_R
    else:
        other, base = jnp.where(q0, above, below), OTHER_B
    total = source + coef(SAME) * here + coef(base) * other
    total = total + (coef(base + 1) * roll(here, 1, 0) + coef(base + 2) * roll(here, -1, 0))
    return total + (coef(base + 3) * roll(here, 1, 1) + coef(base + 4) * roll(here, -1, 1))


def kernel(
    f_hbm, u_hbm, a_hbm, bx_hbm, by_hbm, bz_hbm, sol, res,
    e5, y_top, y_bot, y_lo, y_hi, u_in, u0, s_hi, s_lo, l_lo, l_hi, k0, g0, r0, b0, u1, us, us_lo, us_hi,
    e1, e1s_up, e1s_dn, e1s_lo, e1s_hi, k1, f1, f1s, f1s_lo, f1s_hi, g1, r1, b1, v1, v1s, v1s_lo, v1s_hi,
    ga, gb, w2, k2, g2, r2, b2, k3, k4, work, work2, work3, mats, qz0,
    in_sem, a_send, a_recv, b_send, b_recv, c_send, c_recv, d_send, d_recv, e_send, e_recv,
    h_send, h_recv, p_send, p_recv, i_send, i_recv,
):
    gx, gy, gz = lax.axis_index("gx"), lax.axis_index("gy"), lax.axis_index("gz")
    me = (gx, gy, gz)
    core = lax.rem(gx, 2)
    chip = ((gx // 2) * 4 + gy) * 4 + gz

    near = [[lax.rem(me[d] + (k + GRID[d]), GRID[d]) if k else me[d] for k in (-1, 0, 1)] for d in range(3)]

    def nb(o):
        return tuple(near[d][o[d] + 1] for d in range(3))

    partner = (gx + 1 - 2 * core, gy, gz)

    loads = [pltpu.make_async_copy(u_hbm, u_in, in_sem.at[5])]
    for n, ref in enumerate((f_hbm, a_hbm, bx_hbm, by_hbm, bz_hbm)):
        loads.append(pltpu.make_async_copy(ref, e5.at[n, pl.ds(4, 16)], in_sem.at[n]))
    for c in loads:
        c.start()

    def zero(ref, at):
        ref[at] = jnp.zeros(ref.shape[1:], F32)

    for ref in (u0, u1):
        zero(ref, 0)
        zero(ref, 13)
    barrier = pltpu.get_barrier_semaphore()

    turns = [[lax.rem(at + k, 4) for k in range(4)] for at in (gx // 2, gy, gz)]
    peers = sorted(itertools.product(range(4), repeat=3), key=lambda k: -sum(min(n, 4 - n) for n in k))[:-1]
    peers = [(turns[0][k[0]] * 2 + core, turns[1][k[1]], turns[2][k[2]]) for k in peers]
    for to in peers:
        pl.semaphore_signal(barrier, inc=1, device_id=to, device_id_type=MESH)
    for o in OFFS:
        if o[0]:
            pl.semaphore_signal(barrier, inc=1, device_id=nb(o), device_id_type=MESH)

    row, col = iota((128, 128), 0), iota((128, 128), 1)
    one = lambda cond: jnp.where(cond, 1.0, 0.0).astype(F32)
    SUM, EVEN, SUM32, DOUBLE, TO1 = range(5)
    mats[SUM] = one((row >> 1) == (col & 63)).astype(jnp.bfloat16)
    mats[EVEN] = one(row == 2 * (col & 63)).astype(jnp.bfloat16)
    mats[SUM32] = one((row >> 1) == (col & 31)).astype(jnp.bfloat16)
    mats[DOUBLE] = one(row == (col >> 1)).astype(jnp.bfloat16)
    z1 = jnp.where(col < 96, col, col - 128)
    mats[TO1] = one(row == (((z1 + 64 * gz) >> 1) & 127)).astype(jnp.bfloat16)
    wide_col, wide_row = iota((128, 256), 1), iota((128, 256), 0)
    z0 = jnp.where(wide_col < 192, wide_col, wide_col - 256)
    qz0[...] = one(wide_row == ((z0 >> 1) & 127)).astype(jnp.bfloat16)

    q_l0 = checker((48, 256))
    q_in = checker((32, 128))
    q16 = checker((16, 128))
    q8 = checker((8, 128))
    lane8 = iota((8, 128), 1)
    lane16 = iota((16, 128), 1)
    lane32 = iota((32, 128), 1)
    lane48 = iota((48, 128), 1)
    first16 = (lane32 & 15) < 8
    first48 = (lane48 & 15) < 8

    for ref, at in ((r0, 0), (r0, 13), (b0, 0), (b0, 13), (r1, 0), (r1, 13), (b1, 0), (b1, 13)):
        zero(ref, at)
    for ref in (r2, b2):
        zero(ref, 0)
        zero(ref, 17)

    for c in loads:
        c.wait()

    def take_black(p, carry):
        u0[4 + p - 1, pl.ds(8, 32), pl.ds(0, 128)] = jnp.where(q_in, u_in[2 * p + 1], u_in[2 * p])
        return carry

    lax.fori_loop(0, 8, take_black, 0, unroll=2)

    sub8 = iota((8, 128), 0) < 4
    y_lo[:, 24] = jnp.zeros((3, 8, 128), F32)
    y_hi[:, 24] = jnp.zeros((3, 8, 128), F32)

    def take_ends(x, carry):
        for t, (n, k) in enumerate(((0, 1), (2, 4))):
            y_top[t, x] = jnp.where(sub8, roll(e5[n, 4 + x, pl.ds(24, 8), :], 4, 0), e5[k, 4 + x, pl.ds(24, 8), :])
            y_bot[t, x] = jnp.where(sub8, e5[n, 4 + x, pl.ds(0, 8), :], roll(e5[k, 4 + x, pl.ds(0, 8), :], 4, 0))
        y_top[2, x] = e5[3, 4 + x, pl.ds(24, 8), :]
        y_bot[2, x] = e5[3, 4 + x, pl.ds(0, 8), :]
        return carry

    lax.fori_loop(0, 16, take_ends, 0, unroll=4)

    pl.semaphore_wait(barrier, 81)

    def remote(src, dst, send, recv, to):
        return pltpu.make_async_remote_copy(
            src_ref=src, dst_ref=dst, send_sem=send, recv_sem=recv, device_id=to, device_id_type=MESH
        )

    Y0 = {-1: (8, 40, 8), 0: (8, 8, 32), 1: (32, 0, 8)}
    X5 = {-1: (0, 20, 5), 1: (12, 0, 4)}
    XY = {-1: (0, 20, 4), 0: (0, 4, 16), 1: (12, 0, 4)}
    XE = {-1: (3, 11, 2), 1: (9, 1, 2)}
    XU = {-1: (3, 11, 3), 0: (3, 3, 8), 1: (8, 0, 3)}
    XS = {-1: (0, 3, 1), 0: (0, 1, 2), 1: (1, 0, 1)}
    YS = {-1: (0, 40, 8), 0: (0, 8, 32), 1: (24, 0, 8)}
    first = []
    for n, o in enumerate(FLAT):
        if o[1]:
            (xs, xd, xn), (src, dst) = XY[o[0]], (y_top, y_lo) if o[1] == 1 else (y_bot, y_hi)
        else:
            (xs, xd, xn), (src, dst) = X5[o[0]], (e5, e5)
            xs += 4
        first.append(remote(
            src.at[:, pl.ds(xs, xn)], dst.at[:, pl.ds(xd, xn)], a_send.at[18 + n], a_recv.at[18 + n], nb(o)
        ))
        (xs, xd, xn), (ys, yd, yn) = (XE if o[0] and o[1] else XU)[o[0]], Y0[o[1]]
        first.append(remote(
            u0.at[pl.ds(xs, xn), pl.ds(ys, yn), pl.ds(0, 128)], u0.at[pl.ds(xd, xn), pl.ds(yd, yn), pl.ds(0, 128)],
            a_send.at[26 + n], a_recv.at[26 + n], nb(o),
        ))
    for c in first:
        c.start()

    for half in range(2):
        for t, (one_n, two_n) in enumerate(((0, 1), (2, 3), (4, 5))):
            acc_a = jnp.zeros((32, 128), F32)
            acc_b = jnp.zeros((32, 128), F32)
            for m in range(8):
                at = 8 * half + m
                rolled = roll(e5[one_n, 4 + at], 16 * m + 8, 1)
                acc_a = jnp.where((lane32 >> 4) == m, rolled, acc_a)
                if two_n < 5:
                    rolled = roll(e5[two_n, 4 + at], 16 * m + 16, 1)
                elif m < 4:
                    rolled = roll(u0[3 + 4 * half + m, pl.ds(8, 32), pl.ds(0, 128)], 16 * m + 16, 1)
                else:
                    continue
                acc_b = jnp.where((((lane32 + 120) & 127) >> 4) == m, rolled, acc_b)
            s_hi[t, half] = jnp.where(first16, acc_a, acc_b)
            s_lo[t, half] = jnp.where(first16, acc_b, acc_a)

    beyond = []
    for n, o in enumerate(TALL):
        (xs, xd, xn), (ys, yd, yn) = XS[o[0]], YS[o[1]]
        src, dst = (s_hi, l_lo) if o[2] == 1 else (s_lo, l_hi)
        beyond.append(remote(
            src.at[:, pl.ds(xs, xn), pl.ds(ys, yn)], dst.at[:, pl.ds(xd, xn), pl.ds(yd, yn)],
            a_send.at[n], a_recv.at[n], nb(o),
        ))
    for c in beyond:
        c.start()
    first += beyond

    def coarsen(count, rows, read):
        size = count * rows
        for p in range(count):
            for n in range(4):
                even = read(n, 2 * p)
                work[pl.ds(n * size + p * rows, rows), :] = even if n == 1 else even + read(n, 2 * p + 1)
        work2[pl.ds(0, 3 * size), :] = dot(work[pl.ds(0, 3 * size), :], mats[SUM])
        work2[pl.ds(3 * size, size), :] = dot(work[pl.ds(3 * size, size), :], mats[EVEN])

        def result(n, p):
            at = n * size + p * rows
            low = work2[pl.ds(at, rows // 2, stride=2), :]
            if n == 2:
                return 0.25 * low
            return (0.125 if n == 0 else 0.25) * (low + work2[pl.ds(at + 1, rows // 2, stride=2), :])

        return result

    got = coarsen(8, 32, lambda n, x: e5[n + 1, 4 + x])
    first16b = (lane16 & 15) < 8
    for n in range(0, 4, 2):
        acc_a = jnp.zeros((16, 128), F32)
        acc_b = jnp.zeros((16, 128), F32)
        for m in range(8):
            one_v, two_v = got(n, m), got(n + 1, m)
            e1[n // 2, 8 + m, pl.ds(8, 16), :] = jnp.where(lane16 < 64, one_v, two_v)
            acc_a = jnp.where((lane16 >> 4) == m, roll(one_v, 16 * m + 8, 1), acc_a)
            acc_b = jnp.where((((lane16 + 120) & 127) >> 4) == m, roll(two_v, 16 * m + 16, 1), acc_b)
        e1s_up[n // 2] = jnp.where(first16b, acc_a, acc_b)
        e1s_dn[n // 2] = jnp.where(first16b, acc_b, acc_a)

    Y1 = {-1: (8, 24, 8), 0: (8, 8, 16), 1: (16, 0, 8)}
    YT = {-1: (0, 24, 8), 0: (0, 8, 16), 1: (8, 0, 8)}
    XT = {-1: 2, 0: 1, 1: 0}

    def spread1(main, to_high, to_low, low, high, send, recv, lead):
        out = []
        for n, o in enumerate(TALL):
            ys, yd, yn = YT[o[1]]
            dst, strip = (low, to_high) if o[2] == 1 else (high, to_low)
            src = strip.at[:, pl.ds(ys, yn)] if lead else strip.at[pl.ds(ys, yn)]
            dst = dst.at[:, XT[o[0]], pl.ds(yd, yn)] if lead else dst.at[XT[o[0]], pl.ds(yd, yn)]
            out.append(remote(src, dst, send.at[n], recv.at[n], nb(o)))
        for n, o in enumerate(FLAT):
            size = main.shape[1 if lead else 0] // 3
            (xs, xd, xn), (ys, yd, yn) = (size, size * (1 - o[0]), size), Y1[o[1]]
            src = (pl.ds(xs, xn), pl.ds(ys, yn))
            dst = (pl.ds(xd, xn), pl.ds(yd, yn))
            if lead:
                src, dst = (slice(None),) + src, (slice(None),) + dst
            out.append(remote(main.at[src], main.at[dst], send.at[18 + n], recv.at[18 + n], nb(o)))
        return out

    coefs1 = spread1(e1, e1s_up, e1s_dn, e1s_lo, e1s_hi, b_send, b_recv, True)
    for c in coefs1:
        c.start()

    def twice(n, value):
        other = roll(value, 64, 1)
        return jnp.where(lane16 < 64, other, value) if n % 2 else jnp.where(lane16 < 64, value, other)

    got = coarsen(4, 16, lambda n, x: twice(n, e1[n // 2, 8 + x, pl.ds(8, 16), :]))
    for n in range(4):
        acc = got(n, 0)
        for m in range(1, 4):
            acc = jnp.where((lane8 >> 5) == m, got(n, m), acc)
        ga[core, gx // 2, gy, gz, n] = acc

    def along(axis, k):
        if axis == "z":
            return lax.rem(gx + 2 * k, 8), gy, gz
        return (gx, lax.rem(gy + k, 4), gz) if axis == "y" else (gx, gy, lax.rem(gz + k, 4))

    def part(order, axis, back):
        z, y, x = gx // 2, gy, gz
        if axis == "z":
            z = lax.rem(z + 4 - back, 4)
        elif axis == "y":
            y = lax.rem(y + 4 - back, 4)
        else:
            x = lax.rem(x + 4 - back, 4)
        if order == "xyz":
            y, x = slice(None) if axis == "z" else y, x if axis == "x" else slice(None)
            return ga.at[core, z, y, x, pl.ds(0, 2)]
        z, y = slice(None) if axis == "x" else z, y if axis == "y" else slice(None)
        return ga.at[core, z, y, x, pl.ds(2, 2)]

    def legs(stage):
        for n, order in enumerate(("xyz", "yzx")):
            for k in range(1, 4):
                yield order, order[stage], k, 6 * stage + 3 * n + k - 1

    def pass_on(stage):
        for order, axis, k, at in legs(stage):
            own = part(order, axis, 0)
            remote(own, own, h_send.at[at], h_recv.at[at], along(axis, k)).start()

    def passed_on(stage):
        for order, axis, k, at in legs(stage):
            own, theirs = part(order, axis, 0), part(order, axis, k)
            remote(own, own, h_send.at[at], h_recv.at[at], along(axis, k)).wait_send()
            remote(theirs, theirs, h_send.at[at], h_recv.at[at], along(axis, k)).wait_recv()

    pass_on(0)
    passed_on(0)
    pass_on(1)

    for c in first:
        c.wait_recv()
    keep_y0 = one(((iota((48, 256), 0) - 8 + 32 * gy) & 127) != 0)
    lane256 = iota((48, 256), 1)
    keep_z0 = one(((jnp.where(lane256 < 192, lane256, lane256 - 256) + 128 * gz) & 511) != 0)

    def side(n, group, m):
        t, low, high = n // 2, l_lo, l_hi
        if n % 2:
            return pltpu.roll(jnp.where(first48, high[t, group], low[t, group]), lax.rem(112 - 16 * m + 128, 128), 1)
        return pltpu.roll(jnp.where(first48, low[t, group], high[t, group]), lax.rem(120 - 16 * m + 128, 128), 1)

    def fine_row(n, x):
        at = x + 4
        t, swap = ((0, 0), (0, 4), (1, 0), (2, 0), (1, 4))[n]
        low = y_lo[t, x] if swap or n == 3 else roll(y_lo[t, x], 4, 0)
        high = roll(y_hi[t, x], 4, 0) if swap else y_hi[t, x]
        main = jnp.concatenate([low, e5[n, x], high], axis=0)
        return jnp.concatenate([main, side(n, at // 8, lax.rem(at, 8))], axis=1)

    def build0(p, carry):
        e, o = 2 * p, 2 * p + 1
        even = tuple(fine_row(n, e) for n in range(1, 5))
        odd = tuple(fine_row(n, o) for n in range(1, 5))
        keep_e = jnp.where(((e - 4 + 16 * gx) & 127) == 0, 0.0, 1.0).astype(F32)
        keep_n = jnp.where(((e - 2 + 16 * gx) & 127) == 0, 0.0, 1.0).astype(F32)
        for n, value in enumerate(couplings(even, odd, fine_row(2, e + 2), keep_e, keep_n, keep_y0, keep_z0, 1.0, q_l0)):
            k0[n, p] = value
        f_e, f_o = fine_row(0, e), fine_row(0, o)
        g0[RED, p] = jnp.where(q_l0, f_e, f_o)
        g0[BLACK, p] = jnp.where(q_l0, f_o, f_e)
        return carry

    lax.fori_loop(0, 12, build0, 0, unroll=3)

    passed_on(1)
    pass_on(2)

    def side_u(p, carry):
        at = p + 1
        u0[p, :, pl.ds(128, 128)] = side(5, at // 4, lax.rem(at, 4))
        return carry

    lax.fori_loop(0, 14, side_u, 0, unroll=7)

    def half0(colour, src, dst, start, stop):
        def one_pair(p, carry):
            coef = lambda n: k0[n, p]
            total = gathered_sum(colour, src[p + 1], src[p], src[p + 2], g0[colour, p], coef, q_l0)
            dst[p + 1] = total * k0[ID_R if colour == RED else ID_B, p]
            return carry

        lax.fori_loop(start, stop, one_pair, 0, unroll=4)

    half0(RED, u0, r0, 0, 12)
    half0(BLACK, r0, b0, 0, 12)
    half0(RED, b0, r0, 1, 11)
    half0(BLACK, r0, b0, 1, 11)

    def resid0(p):
        coef = lambda n: k0[n, p]
        out = []
        for colour, own, far in ((RED, r0, b0), (BLACK, b0, r0)):
            total = gathered_sum(colour, far[p + 1], far[p], far[p + 2], g0[colour, p], coef, q_l0)
            out.append(total - k0[D_R if colour == RED else D_B, p] * own[p + 1])
        return out

    def restrict0(p, carry):
        red, black = resid0(p + 2)
        work[pl.ds(32 * p, 32), :] = (red + black)[8:40, :128]
        return carry

    lax.fori_loop(0, 8, restrict0, 0, unroll=4)
    work2[pl.ds(0, 256), :] = dot(work[pl.ds(0, 256), :], mats[SUM])
    acc = jnp.zeros((16, 128), F32)
    values = []
    for m in range(8):
        value = 0.125 * (work2[pl.ds(32 * m, 16, stride=2), :] + work2[pl.ds(32 * m + 1, 16, stride=2), :])
        values.append(value)
        if m >= 4:
            f1[m, pl.ds(8, 16), :] = jnp.where(lane16 < 64, values[m - 4], value)
        acc = jnp.where((lane16 >> 4) == m, roll(value, 16 * m + 8, 1), acc)
    f1s[...] = acc

    right1 = spread1(f1, f1s, f1s, f1s_lo, f1s_hi, c_send, c_recv, False)
    for c in right1:
        c.start()

    acc = jnp.zeros((32, 128), F32)
    for m in range(8):
        acc = jnp.where((lane32 >> 4) == m, roll(b0[3 + m, pl.ds(8, 32), pl.ds(0, 128)], 16 * m + 8, 1), acc)
    us[...] = acc
    YU = {-1: (0, 40, 8), 0: (0, 8, 32), 1: (24, 0, 8)}
    fine = []
    for n, o in enumerate(TALL):
        ys, yd, yn = YU[o[1]]
        dst = us_lo if o[2] == 1 else us_hi
        fine.append(remote(us.at[pl.ds(ys, yn)], dst.at[XT[o[0]], pl.ds(yd, yn)], d_send.at[n], d_recv.at[n], nb(o)))
    for n, o in enumerate(FLAT):
        (xs, xd, xn), (ys, yd, yn) = (XE if o[0] and o[1] else XU)[o[0]], Y0[o[1]]
        fine.append(remote(
            b0.at[pl.ds(xs, xn), pl.ds(ys, yn), pl.ds(0, 128)], u1.at[pl.ds(xd, xn), pl.ds(yd, yn), pl.ds(0, 128)],
            d_send.at[18 + n], d_recv.at[18 + n], nb(o),
        ))
    for c in fine:
        c.start()

    for c in first:
        c.wait_send()
    for c in coefs1:
        c.wait()
    keep_y1 = one(((iota((32, 128), 0) - 8 + 16 * gy) & 63) != 0)
    keep_z1 = one(((jnp.where(lane32 < 96, lane32, lane32 - 128) + 64 * gz) & 255) != 0)

    def joined(main, low, high, m, back=0):
        above = pltpu.roll(high, lax.rem(56 - back - 16 * m + 256, 128), 1)
        below = pltpu.roll(low, lax.rem(120 - back - 16 * m + 256, 128), 1)
        return jnp.where(lane32 < 64, main, jnp.where(lane32 < 96, above, below))

    def coarse_row(n, x):
        main = e1[n // 2, x]
        if n % 2:
            main = roll(main, 64, 1)
        return joined(main, e1s_lo[n // 2, x // 8], e1s_hi[n // 2, x // 8], lax.rem(x, 8), 8 * (n % 2))

    def build1(p, carry):
        e, o = 2 * p, 2 * p + 1
        even = tuple(coarse_row(n, e) for n in range(4))
        odd = tuple(coarse_row(n, o) for n in range(4))
        after = coarse_row(1, lax.rem(e + 2, 24))
        keep_e = jnp.where(((e - 8 + 8 * gx) & 63) == 0, 0.0, 1.0).astype(F32)
        keep_n = jnp.where(((e - 6 + 8 * gx) & 63) == 0, 0.0, 1.0).astype(F32)
        for n, value in enumerate(couplings(even, odd, after, keep_e, keep_n, keep_y1, keep_z1, 0.25, q_in)):
            k1[n, p] = value
        return carry

    lax.fori_loop(0, 12, build1, 0, unroll=2)

    passed_on(2)
    pair_a = remote(ga.at[core], ga.at[core], p_send.at[0], p_recv.at[0], partner)
    pair_a.start()

    for c in right1:
        c.wait_recv()

    def source1(p, carry):
        e, o = 2 * p, 2 * p + 1
        f_e, f_o = (
            joined(pltpu.roll(f1[(x // 8) * 4 + lax.rem(x, 4)], 64 * (lax.rem(x, 8) // 4), 1),
                   f1s_lo[x // 8], f1s_hi[x // 8], lax.rem(x, 8))
            for x in (e, o)
        )
        red = jnp.where(q_in, f_e, f_o)
        g1[RED, p] = red
        g1[BLACK, p] = jnp.where(q_in, f_o, f_e)
        r1[p + 1] = red * k1[ID_R, p]
        return carry

    lax.fori_loop(0, 12, source1, 0, unroll=12)

    def half1(colour, src, dst):
        def one_pair(p, carry):
            coef = lambda n: k1[n, p]
            total = gathered_sum(colour, src[p + 1], src[p], src[p + 2], g1[colour, p], coef, q_in)
            dst[p + 1] = total * k1[ID_R if colour == RED else ID_B, p]
            return carry

        lax.fori_loop(0, 12, one_pair, 0, unroll=12)

    half1(BLACK, r1, b1)
    half1(RED, b1, r1)
    half1(BLACK, r1, b1)
    for p in range(4):
        coef = lambda n: k1[n, p + 4]
        total = gathered_sum(RED, b1[p + 5], b1[p + 4], b1[p + 6], g1[RED, p + 4], coef, q_in) - k1[D_R, p + 4] * r1[p + 5]
        other = gathered_sum(BLACK, r1[p + 5], r1[p + 4], r1[p + 6], g1[BLACK, p + 4], coef, q_in)
        total = total + (other - k1[D_B, p + 4] * b1[p + 5])
        work[pl.ds(16 * p, 16), :] = jnp.where(lane16 < 64, total[8:24], 0.0)
    work2[pl.ds(0, 64), :] = dot(work[pl.ds(0, 64), :], mats[SUM32])
    acc = jnp.zeros((8, 128), F32)
    for m in range(4):
        value = 0.125 * (work2[pl.ds(16 * m, 8, stride=2), :] + work2[pl.ds(16 * m + 1, 8, stride=2), :])
        acc = jnp.where((lane8 >> 5) == m, value, acc)
    gb[core, chip] = acc

    for to in peers:
        remote(gb.at[core, chip], gb.at[core, chip], i_send.at[0], i_recv.at[0], to).start()

    acc = jnp.zeros((16, 128), F32)
    for m in range(4):
        value = b1[5 + m, pl.ds(8, 16), :]
        value = jnp.where(lane16 < 64, value, roll(value, 64, 1))
        acc = jnp.where((lane16 >> 4) == m, roll(value, 16 * m + 8, 1), acc)
        v1[4 + m, pl.ds(8, 16), :] = value
    v1s[...] = acc
    black1 = []
    for n, o in enumerate(TALL):
        ys, yd, yn = YT[o[1]]
        dst = v1s_lo if o[2] == 1 else v1s_hi
        black1.append(remote(v1s.at[pl.ds(ys, yn)], dst.at[XT[o[0]], pl.ds(yd, yn)], e_send.at[n], e_recv.at[n], nb(o)))
    for n, o in enumerate(FLAT):
        (xs, xd, xn), (ys, yd, yn) = {-1: (4, 8, 4), 0: (4, 4, 4), 1: (4, 0, 4)}[o[0]], Y1[o[1]]
        black1.append(remote(
            v1.at[pl.ds(xs, xn), pl.ds(ys, yn)], v1.at[pl.ds(xd, xn), pl.ds(yd, yn)],
            e_send.at[18 + n], e_recv.at[18 + n], nb(o),
        ))
    for c in black1:
        c.start()

    for c in right1:
        c.wait_send()

    pair_a.wait()

    def untile(tiles):
        out = []
        for m in range(4):
            total = tiles[0] if m == 0 else roll(tiles[0], -32 * m, 1)
            for k in range(1, 4):
                total = jnp.where((lane8 >> 5) == k, roll(tiles[k], 32 * (k - m), 1), total)
            out.append(total)
        return out

    def place(tiles_of, count, batch):
        def one_block(t, carry):
            bx, by = t // 4, lax.rem(t, 4)
            rows = pl.ds(pl.multiple_of(8 * by, 8), 8)
            for n in range(count):
                for m, value in enumerate(untile([tiles_of(lax.rem(bx, 2), bx // 2, by, k, n) for k in range(4)])):
                    w2[n, 4 * bx + m, rows, :] = value
            return carry

        lax.fori_loop(0, 32, one_block, 0, unroll=batch)

    place(lambda side_core, bz, by, k, n: ga[side_core, bz, by, k, n], 4, 4)

    keep_y2 = one(iota((32, 128), 0) != 0)
    keep_z2 = one(lane32 != 0)

    def build2(p, carry):
        e, o = 2 * p, 2 * p + 1
        even = tuple(w2[n, e] for n in range(4))
        odd = tuple(w2[n, o] for n in range(4))
        keep_e = jnp.where(p == 0, 0.0, 1.0).astype(F32)
        keep_n = jnp.where(p == 15, 0.0, 1.0).astype(F32)
        after = w2[1, lax.rem(e + 2, 32)]
        for n, value in enumerate(couplings(even, odd, after, keep_e, keep_n, keep_y2, keep_z2, 0.25**2, q_in)):
            k2[n, p] = value
        return carry

    lax.fori_loop(0, 16, build2, 0, unroll=2)

    def small(level_coefs, count, rows, period, scale, q, dest):
        keep_y = one(iota((rows, 128), 0) != 0)
        keep_z = one((iota((rows, 128), 1) & (period - 1)) != 0)
        for p in range(count):
            even = tuple(level_coefs(n, 2 * p) for n in range(4))
            odd = tuple(level_coefs(n, 2 * p + 1) for n in range(4))
            after = level_coefs(1, (2 * p + 2) % (2 * count))
            for n, value in enumerate(couplings(
                even, odd, after, 0.0 if p == 0 else 1.0, 0.0 if p == count - 1 else 1.0, keep_y, keep_z, scale, q
            )):
                dest[n, p] = value

    got3 = coarsen(16, 32, lambda n, x: w2[n, x])
    rows3 = [[got3(n, x) for x in range(16)] for n in range(4)]
    for n in range(4):
        for x in range(16):
            w2[n, x, pl.ds(0, 16), :] = rows3[n][x]
    small(lambda n, x: w2[n, x, pl.ds(0, 16), :], 8, 16, 64, 0.25**3, q16, k3)
    got4 = coarsen(8, 16, lambda n, x: w2[n, x, pl.ds(0, 16), :])
    small(got4, 4, 8, 32, 0.25**4, q8, k4)

    others = gb.at[core, pl.ds(0, 63)]
    remote(others, others, i_send.at[0], i_recv.at[0], partner).wait()
    pair_b = remote(gb.at[core], gb.at[core], p_send.at[1], p_recv.at[1], partner)
    pair_b.start()
    pair_b.wait()

    place(lambda side_core, bz, by, k, n: gb[side_core, bz * 16 + by * 4 + k], 1, 16)

    def source2(p, carry):
        f_e, f_o = w2[0, 2 * p], w2[0, 2 * p + 1]
        red = jnp.where(q_in, f_e, f_o)
        g2[RED, p] = red
        g2[BLACK, p] = jnp.where(q_in, f_o, f_e)
        r2[p + 1] = red * k2[ID_R, p]
        return carry

    lax.fori_loop(0, 16, source2, 0, unroll=16)

    def half2(colour, src, dst):
        def one_pair(p, carry):
            coef = lambda n: k2[n, p]
            total = gathered_sum(colour, src[p + 1], src[p], src[p + 2], g2[colour, p], coef, q_in)
            dst[p + 1] = total * k2[ID_R if colour == RED else ID_B, p]
            return carry

        lax.fori_loop(0, 16, one_pair, 0, unroll=16)

    half2(BLACK, r2, b2)
    half2(RED, b2, r2)
    half2(BLACK, r2, b2)

    def restrict2(p, carry):
        coef = lambda n: k2[n, p]
        total = gathered_sum(RED, b2[p + 1], b2[p], b2[p + 2], g2[RED, p], coef, q_in) - k2[D_R, p] * r2[p + 1]
        other = gathered_sum(BLACK, r2[p + 1], r2[p], r2[p + 2], g2[BLACK, p], coef, q_in)
        work[pl.ds(pl.multiple_of(32 * p, 32), 32), :] = total + (other - k2[D_B, p] * b2[p + 1])
        return carry

    lax.fori_loop(0, 16, restrict2, 0, unroll=16)
    work2[pl.ds(0, 512), :] = dot(work[pl.ds(0, 512), :], mats[SUM])

    def pack(rows, q):
        count = len(rows) // 2
        red = [jnp.where(q, rows[2 * p], rows[2 * p + 1]) for p in range(count)]
        black = [jnp.where(q, rows[2 * p + 1], rows[2 * p]) for p in range(count)]
        return red, black

    def half_small(colour, src, source, k, q, own=None):
        count = len(src)
        out = []
        for p in range(count):
            coef = lambda n: k[n, p]
            total = gathered_sum(colour, src[p], src[p - 1], src[(p + 1) % count], source[p], coef, q)
            if own is None:
                out.append(total * k[ID_R if colour == RED else ID_B, p])
            else:
                out.append(total - k[D_R if colour == RED else D_B, p] * own[p])
        return out

    def paired(count, rows):
        return [
            0.125 * (work2[pl.ds(2 * rows * m, rows, stride=2), :] + work2[pl.ds(2 * rows * m + 1, rows, stride=2), :])
            for m in range(count)
        ]

    def unpacked(red, black, q):
        out = []
        for r, b in zip(red, black):
            out += [jnp.where(q, r, b), jnp.where(q, b, r)]
        return out

    fr3, fb3 = pack(paired(16, 16), q16)
    r3 = [fr3[p] * k3[ID_R, p] for p in range(8)]
    b3 = half_small(BLACK, r3, fb3, k3, q16)
    r3 = half_small(RED, b3, fr3, k3, q16)
    b3 = half_small(BLACK, r3, fb3, k3, q16)
    left_r = half_small(RED, b3, fr3, k3, q16, r3)
    left_b = half_small(BLACK, r3, fb3, k3, q16, b3)
    for p in range(8):
        work[pl.ds(16 * p, 16), :] = left_r[p] + left_b[p]
    work2[pl.ds(0, 128), :] = dot(work[pl.ds(0, 128), :], mats[SUM])

    fr4, fb4 = pack(paired(8, 8), q8)
    r4 = [fr4[p] * k4[ID_R, p] for p in range(4)]
    b4 = half_small(BLACK, r4, fb4, k4, q8)

    def bottom(step, carry):
        black = list(carry[4:])
        red = half_small(RED, black, fr4, k4, q8)
        black = half_small(BLACK, red, fb4, k4, q8)
        return tuple(red + black)

    done = lax.fori_loop(0, 11, bottom, tuple(r4 + b4), unroll=11)
    e4 = unpacked(done[:4], done[4:], q8)

    def doubled(rows, size):
        total = 2 * size * len(rows)
        for m, value in enumerate(rows):
            work[pl.ds(2 * size * m, size, stride=2), :] = value
            work[pl.ds(2 * size * m + 1, size, stride=2), :] = value
        work2[pl.ds(0, total), :] = dot(work[pl.ds(0, total), :], mats[DOUBLE])
        return [work2[pl.ds(2 * size * m, 2 * size), :] for m in range(len(rows))]

    up3 = doubled(e4, 8)
    b3 = [b3[p] + up3[p] for p in range(8)]
    r3 = half_small(RED, b3, fr3, k3, q16)
    b3 = half_small(BLACK, r3, fb3, k3, q16)
    r3 = half_small(RED, b3, fr3, k3, q16)
    b3 = half_small(BLACK, r3, fb3, k3, q16)
    up2 = doubled(unpacked(r3, b3, q16), 16)
    for p in range(16):
        b2[p + 1] = b2[p + 1] + up2[p]

    half2(RED, b2, r2)
    half2(BLACK, r2, b2)
    half2(RED, b2, r2)
    half2(BLACK, r2, b2)

    for c in black1:
        c.wait()

    turn = (4 - 8 * gy) & 31
    for p in range(12):
        x = (p - 4 + 4 * gx) & 31
        red, black = r2[x // 2 + 1], b2[x // 2 + 1]
        lower = jnp.where((x & 1) == 0, 1, 0) == jnp.where(q_in, 1, 0)
        value = pltpu.roll(jnp.where(lower, red, black), turn, 0)[:16]
        work[pl.ds(32 * p, 16, stride=2), :] = value
        work[pl.ds(32 * p + 1, 16, stride=2), :] = value
    work2[pl.ds(0, 384), :] = dot(work[pl.ds(0, 384), :], mats[TO1])

    def lift1(p, carry):
        value = joined(v1[p], v1s_lo[p // 4], v1s_hi[p // 4], lax.rem(p, 4))
        b1[p + 1] = value + work2[pl.ds(pl.multiple_of(32 * p, 32), 32), :]
        return carry

    lax.fori_loop(0, 12, lift1, 0, unroll=12)
    half1(RED, b1, r1)
    half1(BLACK, r1, b1)
    half1(RED, b1, r1)
    half1(BLACK, r1, b1)

    for c in fine:
        c.wait()
    used = (lane32 < 72) | (lane32 >= 120)

    for p in range(14):
        x = p + 5
        red, black = r1[x // 2 + 1], b1[x // 2 + 1]
        value = jnp.where(q_in, red, black) if x % 2 == 0 else jnp.where(q_in, black, red)
        value = jnp.where(used, value, 0.0)[4:28]
        work[pl.ds(48 * p, 24, stride=2), :] = value
        work[pl.ds(48 * p + 1, 24, stride=2), :] = value
    work3[...] = dot(work[pl.ds(0, 672), :], qz0[...])

    def lift_halo(p, carry):
        at = p + 5
        group, m = at // 8, lax.rem(at, 8)
        merged = jnp.where(first48, us_lo[group], us_hi[group])
        beyond = pltpu.roll(merged, lax.rem(120 - 16 * m + 128, 128), 1)
        u1[p] = jnp.concatenate([u1[p, :, pl.ds(0, 128)], beyond], axis=1) + work3[pl.ds(pl.multiple_of(48 * p, 16), 48), :]
        return carry

    def own_black(p, carry):
        u1[p, pl.ds(8, 32), pl.ds(0, 128)] = b0[p, pl.ds(8, 32), pl.ds(0, 128)]
        return carry

    lax.fori_loop(3, 11, own_black, 0)
    lax.fori_loop(0, 14, lift_halo, 0, unroll=7)
    half0(RED, u1, r0, 0, 12)
    half0(BLACK, r0, b0, 0, 12)
    half0(RED, b0, r0, 1, 11)
    half0(BLACK, r0, b0, 1, 11)

    def finish(p, carry):
        red, black = resid0(p + 2)
        red, black = red[8:40, :128], black[8:40, :128]
        res[2 * p] = jnp.where(q_in, red, black)
        res[2 * p + 1] = jnp.where(q_in, black, red)
        red, black = r0[p + 3, pl.ds(8, 32), pl.ds(0, 128)], b0[p + 3, pl.ds(8, 32), pl.ds(0, 128)]
        sol[2 * p] = jnp.where(q_in, red, black)
        sol[2 * p + 1] = jnp.where(q_in, black, red)
        return carry

    lax.fori_loop(0, 8, finish, 0, unroll=4)


def on_device(right_side, initial, alpha, beta_x, beta_y, beta_z):
    block = jax.ShapeDtypeStruct(right_side.shape, F32)
    V = lambda *shape: pltpu.VMEM(shape, F32)
    D = lambda n: pltpu.SemaphoreType.DMA((n,))
    scratch = [
        V(5, 26, 32, 128), V(3, 16, 8, 128), V(3, 16, 8, 128), V(3, 25, 8, 128), V(3, 25, 8, 128),
        V(16, 32, 128), V(14, 48, 256),
        V(3, 2, 32, 128), V(3, 2, 32, 128), V(3, 4, 48, 128), V(3, 4, 48, 128),
        V(15, 12, 48, 256), V(2, 12, 48, 256), V(14, 48, 256), V(14, 48, 256), V(14, 48, 256),
        V(32, 128), V(3, 48, 128), V(3, 48, 128),
        V(2, 24, 32, 128), V(2, 16, 128), V(2, 16, 128), V(2, 3, 32, 128), V(2, 3, 32, 128), V(15, 12, 32, 128),
        V(12, 32, 128), V(16, 128), V(3, 32, 128), V(3, 32, 128),
        V(2, 12, 32, 128), V(14, 32, 128), V(14, 32, 128),
        V(12, 32, 128), V(16, 128), V(3, 32, 128), V(3, 32, 128),
        V(2, 4, 4, 4, 4, 8, 128), V(2, 64, 8, 128), V(4, 32, 32, 128), V(15, 16, 32, 128), V(2, 16, 32, 128),
        V(18, 32, 128), V(18, 32, 128), V(15, 8, 16, 128), V(15, 4, 8, 128),
        V(2048, 128), V(2048, 128), V(672, 256), pltpu.VMEM((5, 128, 128), jnp.bfloat16), pltpu.VMEM((128, 256), jnp.bfloat16),
        D(6), D(34), D(34), D(26), D(26), D(26), D(26), D(26), D(26), D(26), D(26),
        D(18), D(18), D(2), D(2), D(1), D(1),
    ]
    return pl.pallas_call(
        kernel,
        out_shape=(block, block),
        in_specs=[pl.BlockSpec(memory_space=pl.ANY)] * 6,
        out_specs=[pl.BlockSpec(memory_space=pltpu.VMEM)] * 2,
        scratch_shapes=scratch,
        compiler_params=pltpu.CompilerParams(collective_id=0, has_side_effects=True, vmem_limit_bytes=60 << 20),
    )(right_side, initial, alpha, beta_x, beta_y, beta_z)


def solution(mesh):
    spec = P("gx", "gy", "gz")
    return jax.shard_map(on_device, mesh=mesh, in_specs=(spec,) * 6, out_specs=(spec, spec), check_vma=False)
```
